32 devices in a mesh: gx: 16 (over z, y, x), gy: 2 (over core).
Axes of the slice: x: 2, y: 2, z: 4, core: 2. Of those that a mesh axis runs over, the one named last changes fastest.
Arguments:
- u_old: bfloat16 [32, 4, 64, 128], P('gx', 'gy'), may hold values from -6 to 6
- rhs: bfloat16 [32, 4, 64, 128], P('gx', 'gy'), may hold values from -6 to 6
- classes: int32 [32, 4, 16], P('gx', 'gy'), may hold values from 0 to 7
- flags: int32 [2, 32, 4, 16], P(None, 'gx', 'gy'), may hold values from 0 to 1
- inverse: float32 [8, 64, 64], replicated, may hold values from -2 to 2
- x_face: float32 [8, 16, 16], replicated, may hold values from -2 to 2
- lateral_faces: float32 [4, 8, 16, 16], replicated, may hold values from -1.5 to 1.5
- inflow: float32 [4, 16, 128], P('gy'), may hold values from -6 to 6
Outputs:
- u_new: float32 [32, 4, 64, 128], P('gx', 'gy')
The draws below stay inside these ranges and needn't reach their ends.
All inputs are finite; a program needn't handle non-finite values.
Results may differ from the reference program's by a relative error of at most 0.0003.
Values may be sent and summed in bfloat16 or wider, within the bound.
No kernel may reach another device: no remote copies, remote signals or barrier semaphores. Data moves between devices by JAX's collectives and lax.ppermute only.
A program may use at most 64 MiB of HBM per device.

```python
import math
import jax
import jax.numpy as jnp
from jax import lax

NODES = 64
FACE = 16
TRACERS = 8
NCLASS = 8
NZ = 16
NX = 32
NY = 4
COLS = 128


def basis_and_rates(key, slow_count):
    base = jax.random.fold_in(key, 9001)
    vector = jax.random.normal(jax.random.fold_in(base, 1), (FACE,), jnp.float32)
    basis = jnp.eye(FACE, dtype=jnp.float32) - 2.0 * jnp.outer(vector, vector) / jnp.sum(vector * vector)
    ranking = jax.random.permutation(jax.random.fold_in(base, 2), FACE)
    strength = jnp.exp(jax.random.uniform(jax.random.fold_in(base, 3), (FACE,), jnp.float32, math.log(0.8), math.log(2.2)))
    memory = jnp.exp(jax.random.uniform(jax.random.fold_in(base, 4), (FACE,), jnp.float32, math.log(30.0), math.log(50.0)))
    rates = jnp.where(ranking < slow_count, jnp.exp(-strength / NX), jnp.exp(-1.0 / memory))
    gains = jax.random.uniform(jax.random.fold_in(base, 5), (NCLASS, FACE), jnp.float32, 0.7, 1.3)
    losses = jnp.exp(-jax.random.uniform(jax.random.fold_in(base, 6), (NCLASS, 1), jnp.float32, 0.0, 0.5) / NX)
    return (basis, rates, gains, losses, ranking)


def group_masks(ranking):
    first = (ranking < FACE // 2).astype(jnp.float32)
    second = ((ranking >= FACE // 2) & (ranking < FACE - 2)).astype(jnp.float32)
    third = (ranking >= FACE - 2).astype(jnp.float32)
    return jnp.stack([first, second, third], axis=0)


def group_reflections(key, masks):
    vectors = jax.random.normal(key, (NCLASS, 3, FACE), jnp.float32) * masks[None]
    lengths = jnp.sum(vectors * vectors, axis=2, keepdims=True)
    outers = 2.0 * vectors[:, :, :, None] * vectors[:, :, None, :] / lengths[:, :, :, None]
    return jnp.eye(FACE, dtype=jnp.float32)[None] - jnp.sum(outers, axis=1)


def cross_rotations(key, masks):
    inside = jax.random.normal(jax.random.fold_in(key, 1), (NCLASS, FACE), jnp.float32) * masks[0][None]
    outside = jax.random.normal(jax.random.fold_in(key, 2), (NCLASS, FACE), jnp.float32) * (1.0 - masks[0])[None]
    inside = inside / jnp.sqrt(jnp.sum(inside * inside, axis=1, keepdims=True))
    outside = outside / jnp.sqrt(jnp.sum(outside * outside, axis=1, keepdims=True))
    angle = 0.07
    pair = inside[:, :, None] * inside[:, None, :] + outside[:, :, None] * outside[:, None, :]
    turn = outside[:, :, None] * inside[:, None, :] - inside[:, :, None] * outside[:, None, :]
    return jnp.eye(FACE, dtype=jnp.float32)[None] + (math.cos(angle) - 1.0) * pair + math.sin(angle) * turn


def class_bases(key):
    basis, rates, gains, losses, ranking = basis_and_rates(key, FACE // 2)
    base = jax.random.fold_in(key, 7777)
    masks = group_masks(ranking)
    right_factor = group_reflections(jax.random.fold_in(base, 1), masks)
    left_factor = jnp.einsum('kij,kjl->kil', group_reflections(jax.random.fold_in(base, 2), masks), cross_rotations(jax.random.fold_in(base, 3), masks), precision=lax.Precision.HIGHEST)
    right_basis = jnp.einsum('ij,kjm->kim', basis, right_factor, precision=lax.Precision.HIGHEST)
    left_basis = jnp.einsum('ij,kjm->kim', basis, left_factor, precision=lax.Precision.HIGHEST)
    return (left_basis, right_basis)


def draw_x_face(key, part):
    basis, rates, gains, losses, ranking = basis_and_rates(key, FACE // 2)
    left_basis, right_basis = class_bases(key)
    return -jnp.einsum('kim,km,klm->kil', right_basis, gains, right_basis, precision=lax.Precision.HIGHEST)


def draw_inverse(key, part):
    own = jax.random.fold_in(key, 4242)
    slow_count = FACE // 2
    spread = jnp.clip(0.0375 * jax.random.normal(jax.random.fold_in(own, 1), (NCLASS, NODES, NODES), jnp.float32), -0.15, 0.15)
    basis, rates, gains, losses, ranking = basis_and_rates(key, slow_count)
    left_basis, right_basis = class_bases(key)
    leading = jnp.exp(jax.random.uniform(jax.random.fold_in(own, 2), (NCLASS, NODES), jnp.float32, math.log(0.5), math.log(1.5)))
    identity = jnp.eye(NODES, dtype=jnp.float32)
    matrix = spread * (1.0 - identity) + leading[:, :, None] * identity
    row_scale = jnp.where(jnp.arange(NODES) >= NODES - FACE, 0.3, 1.0).astype(jnp.float32)
    matrix = matrix * row_scale[None, :, None]
    factors = rates[None, :] * losses / gains
    block = jnp.einsum('kim,km,klm->kil', left_basis, factors, right_basis, precision=lax.Precision.HIGHEST)
    return matrix.at[:, NODES - FACE:, :FACE].set(block)


def plant(array, rng, smallest, top_value):
    spot = [jax.random.randint(jax.random.fold_in(rng, axis), (), 0, length) for axis, length in enumerate(array.shape)]
    longest = array.shape.index(max(array.shape))
    next_to = spot[:longest] + [(spot[longest] + 1) % array.shape[longest]] + spot[longest + 1:]
    return array.at[tuple(spot)].set(smallest).at[tuple(next_to)].set(top_value)


def steps_of(key, shape, pieces, least, top_value):
    gain, own = 1.0, jax.random.fold_in(key, 6)
    for axis_at, parts in pieces:
        heights = jnp.exp(jax.random.uniform(jax.random.fold_in(own, axis_at), (parts,), jnp.float32, least / len(pieces), top_value / len(pieces)))
        gain = gain * jnp.repeat(heights, shape[axis_at] // parts).reshape([-1 if axis == axis_at else 1 for axis in range(len(shape))])
    return gain


def noise(key, shape, width, reach, shards=(), kind=jnp.bfloat16):
    values = jax.random.normal(key, shape, jnp.float32) * width
    if len(shards) > 0:
        values = steps_of(key, shape, shards, -0.22, 0.18) * values
    return jnp.clip(values, min=-reach, max=reach).astype(kind)


def setup_inputs(seed: int = 0) -> dict:
    splits = jax.random.split(jax.random.key(seed), 9)
    u_old = noise(splits[0], (NX, NY, NODES, COLS), 1.0, 6.0, ((0, 16), (1, 2)))
    rhs = noise(splits[1], (NX, NY, NODES, COLS), 1.0, 6.0, ((0, 16), (1, 2)))
    classes = plant(jax.random.randint(splits[2], (NX, NY, NZ), 0, NCLASS), jax.random.fold_in(splits[2], 1), 0, NCLASS - 1).astype(jnp.int32)
    flags = plant(jax.random.randint(splits[3], (2, NX, NY, NZ), 0, 2), jax.random.fold_in(splits[3], 1), 0, 1).astype(jnp.int32)
    inverse = draw_inverse(jax.random.fold_in(splits[8], 71), 0)
    x_face = draw_x_face(jax.random.fold_in(splits[8], 71), 0)
    lateral_faces = noise(splits[6], (4, NCLASS, FACE, FACE), FACE ** -0.5, 1.5, (), jnp.float32)
    inflow = noise(splits[7], (NY, FACE, COLS), 1.0, 6.0, ((0, 2),), jnp.float32)
    return {"u_old": u_old, "rhs": rhs, "classes": classes, "flags": flags, "inverse": inverse, "x_face": x_face, "lateral_faces": lateral_faces, "inflow": inflow}


HIGH = lax.Precision.HIGHEST


def face_traces(field):
    planes, rows_y, columns = field.shape[0], field.shape[1], field.shape[3]
    cube = field.reshape(planes, rows_y, 4, 4, 4, columns)
    y_low = cube[:, :, :, 0].reshape(planes, rows_y, 16, columns)
    y_high = cube[:, :, :, 3].reshape(planes, rows_y, 16, columns)
    z_low = cube[:, :, :, :, 0].reshape(planes, rows_y, 16, columns)
    z_high = cube[:, :, :, :, 3].reshape(planes, rows_y, 16, columns)
    return y_low, y_high, z_low, z_high


def along_z(trace, upward):
    planes, rows_y, columns = trace.shape[0], trace.shape[1], trace.shape[3]
    split = trace.reshape(planes, rows_y, 16, TRACERS, NZ)
    border = jnp.zeros((planes, rows_y, 16, TRACERS, 1), trace.dtype)
    if upward:
        moved = jnp.concatenate([border, split[..., :-1]], axis=4)
    else:
        moved = jnp.concatenate([split[..., 1:], border], axis=4)
    return moved.reshape(planes, rows_y, 16, columns)


def class_onehot(classes):
    labels = jnp.arange(NCLASS, dtype=jnp.int32)[:, None, None, None]
    return (classes[None] == labels).astype(jnp.float32)


def class_columns(onehot):
    count, planes, rows_y = onehot.shape[0], onehot.shape[1], onehot.shape[2]
    spread = jnp.broadcast_to(onehot[:, :, :, None, None, :], (count, planes, rows_y, 1, TRACERS, NZ))
    return spread.reshape(count, planes, rows_y, 1, TRACERS * NZ)


def flag_columns(flag):
    planes, rows_y = flag.shape[0], flag.shape[1]
    spread = jnp.broadcast_to(flag.astype(jnp.float32)[:, :, None, None, :], (planes, rows_y, 1, TRACERS, NZ))
    return spread.reshape(planes, rows_y, 1, TRACERS * NZ)


def lateral_rhs(rhs, u_old, below_row, above_row, class_cols, flags, lateral_faces):
    y_low, y_high, z_low, z_high = face_traces(u_old)
    from_below = jnp.concatenate([below_row, y_high[:, :-1]], axis=1).astype(jnp.float32)
    from_above = jnp.concatenate([y_low[:, 1:], above_row], axis=1).astype(jnp.float32)
    from_front = along_z(z_high, True).astype(jnp.float32)
    from_back = along_z(z_low, False).astype(jnp.float32)
    y_flag = flag_columns(flags[0])
    z_flag = flag_columns(flags[1])

    def couple(face_index, source, weight):
        every = jnp.einsum("kij,xyjc->kxyic", lateral_faces[face_index], source, precision=HIGH)
        return jnp.sum(every * class_cols, axis=0) * weight

    planes, rows_y, columns = rhs.shape[0], rhs.shape[1], rhs.shape[3]
    shape = (planes, rows_y, 4, 4, columns)
    cube = rhs.astype(jnp.float32).reshape(planes, rows_y, 4, 4, 4, columns)
    cube = cube.at[:, :, :, 0].add(-couple(0, from_below, 1.0 - y_flag).reshape(shape))
    cube = cube.at[:, :, :, 3].add(-couple(1, from_above, y_flag).reshape(shape))
    cube = cube.at[:, :, :, :, 0].add(-couple(2, from_front, 1.0 - z_flag).reshape(shape))
    cube = cube.at[:, :, :, :, 3].add(-couple(3, from_back, z_flag).reshape(shape))
    return cube.reshape(planes, rows_y, 64, columns)


def apply_inverse(matrices, source, class_cols):
    total = jnp.zeros(source.shape[:2] + (matrices.shape[1], source.shape[3]), jnp.float32)
    for class_id in range(NCLASS):
        total = total + class_cols[class_id] * jnp.einsum("ij,xyjc->xyic", matrices[class_id], source, precision=HIGH)
    return total


def pick(table, hot_plane):
    return jnp.einsum("kab,kyz->yzab", table, hot_plane, precision=HIGH)


def applied(selected, trace):
    return jnp.einsum("...yzab,...ybtz->...yatz", selected, trace, precision=HIGH)


def reference(u_old, rhs, classes, flags, inverse, x_face, lateral_faces, inflow):
    coupling = -jnp.einsum("kij,kjl->kil", inverse[:, :, :16], x_face, precision=HIGH)
    onehot = class_onehot(classes)
    cols_all = class_columns(onehot)
    edge_row = jnp.zeros((1, 1, 16, COLS), jnp.bfloat16)

    def plane(trace, items):
        u_plane, r_plane, hot_plane, cols_plane, flag_plane = items
        q_plane = lateral_rhs(r_plane[None], u_plane[None], edge_row, edge_row, cols_plane[:, None], flag_plane[:, None], lateral_faces)
        w_plane = apply_inverse(inverse, q_plane, cols_plane[:, None])[0]
        result = w_plane.reshape(NY, 64, TRACERS, NZ) + applied(pick(coupling, hot_plane), trace)
        return result[:, 48:], result.reshape(NY, 64, COLS)

    start = inflow.reshape(NY, 16, TRACERS, NZ)
    items = (u_old, rhs, jnp.moveaxis(onehot, 1, 0), jnp.moveaxis(cols_all, 1, 0), jnp.moveaxis(flags, 1, 0))
    _, solved = lax.scan(plane, start, items)
    return solved
```

```python
import functools

import jax
import jax.numpy as jnp
from jax import lax
from jax.experimental import pallas as pl
from jax.experimental.pallas import tpu as pltpu
from jax.sharding import PartitionSpec as P

FACE = 16
HIGH = lax.Precision.HIGHEST
F32 = jnp.float32
BF16 = jnp.bfloat16


def iota(shape, dim):
    return lax.broadcasted_iota(jnp.int32, shape, dim)


def exact(left, right):
    return jnp.dot(left, right, precision=HIGH, preferred_element_type=F32)


def split(value):
    high = value.astype(BF16)
    return high, (value - high.astype(F32)).astype(BF16)


def params_kernel(inv_ref, x_ref, lat_ref, full_ref, coup_ref, step_ref):
    count, nodes, _ = inv_ref.shape
    column = iota((nodes, 256), 1)
    at = column - 128
    face, item = (at - 64) // FACE, at % FACE
    high, low = item // 4, item % 4
    lateral = jnp.where(face < 2, 16 * high + low + 12 * (face == 1), 16 * high + 4 * low + 3 * (face == 3))
    inner = jnp.where(at < FACE, at, -1)
    source = jnp.where(column < 128, column, jnp.where(at >= 64, lateral, inner))
    chosen = (iota((nodes, 256), 0) == source).astype(F32)
    gathered = exact(inv_ref[...].reshape(count * nodes, nodes), chosen)
    tile = (iota((FACE, 128), 1) % FACE == iota((FACE, 128), 0)).astype(F32)
    lat = exact(lat_ref[...].reshape(4 * count * FACE, FACE), tile)
    x_low = exact(x_ref[...].reshape(count * FACE, FACE), tile)
    row, lane = iota((128, 128), 0) // FACE, iota((128, 128), 1) // FACE
    keep = (row == lane) | ((row == 0) & (lane < 3))
    lane_at = iota((nodes, 128), 1)
    outs = []
    for k in range(count):
        rows = [x_low[k * FACE:(k + 1) * FACE], jnp.zeros((48, 128), F32)]
        for f in range(4):
            begin = (f * count + k) * FACE
            rows.append(lat[begin:begin + FACE])
        blocks = jnp.where(keep, jnp.concatenate(rows, axis=0), 0.0)
        here = pl.ds(k * nodes, nodes)
        joined = -exact(gathered[k * nodes:(k + 1) * nodes, 128:], blocks)
        both = jnp.where(lane_at < 64, gathered[k * nodes:(k + 1) * nodes, :128], joined)
        first, second = split(both)
        full_ref[here, 0:128] = first
        full_ref[here, 128:256] = second
        first, second = split(joined)
        coup_ref[here, :] = jnp.where(lane_at < 32, first.astype(F32), second.astype(F32)).astype(BF16)
        outs.append(joined[nodes - FACE:])
    step_ref[...] = jnp.concatenate(outs, axis=0).T[:FACE]


def encode(value):
    width = value.shape[1]
    tile = (iota((FACE, 256), 1) % FACE == iota((FACE, 256), 0)).astype(F32)
    spread = exact(value.T, tile)
    spread = jnp.where(iota((width, 256), 0) % FACE == iota((width, 256), 1) // FACE, spread, 0.0)
    gather = (iota((8, width), 1) // FACE == iota((8, width), 0)).astype(F32)
    return exact(gather, spread)


def decode(value):
    spread = (iota((128, 8), 0) // FACE == iota((128, 8), 1)).astype(F32)
    rows = exact(spread, value)
    rows = jnp.where(iota((128, 256), 0) % FACE == iota((128, 256), 1) // FACE, rows, 0.0)
    fold = (iota((256, 128), 0) % FACE == iota((256, 128), 1)).astype(F32)
    return exact(rows, fold).T[:FACE]


def block_diagonal(step):
    rows = jnp.concatenate([step] * 16, axis=0)
    return jnp.where(iota((256, 256), 0) // FACE == iota((256, 256), 1) // FACE, rows, 0.0)


def join(earlier, later):
    moved = exact(earlier, block_diagonal(later[:FACE]))
    return moved + jnp.concatenate([jnp.zeros((FACE, 256), F32), later[FACE:]], axis=0)


def advance(trace, later):
    return exact(trace, block_diagonal(later[:FACE])) + later[FACE:]


def sources_kernel(gy_size, u_ref, rhs_ref, below_ref, above_ref, cls_ref, flag_ref, full_ref, step_ref, x_ref, row_ref, map_ref):
    planes, rows_y, nodes, columns = u_ref.shape
    place = lax.axis_index("gy")
    node, item = iota((nodes, nodes), 1), iota((nodes, nodes), 0)
    face, high, low = item // FACE, item % FACE // 4, item % 4
    wanted = jnp.where(face < 2, 16 * high + low + 12 * (face == 1), 16 * high + 4 * low + 3 * (face == 3))
    chosen = (node == wanted).astype(BF16)

    def faces(value):
        return jnp.dot(chosen, value, preferred_element_type=F32)

    labels = []
    for x in range(planes):
        labels.append(cls_ref[x])
    for d in range(2):
        for x in range(planes):
            labels.append(flag_ref[d, x])
    labels = jnp.concatenate(labels, axis=0).astype(F32)
    tile = (iota((FACE, columns), 1) % FACE == iota((FACE, columns), 0)).astype(F32)
    on_columns = jnp.dot(labels, tile, preferred_element_type=F32)
    wide = (iota((FACE, 256), 1) // FACE == iota((FACE, 256), 0)).astype(F32)
    on_wide = jnp.dot(labels, wide, preferred_element_type=F32)
    row_ref[...] = on_columns
    z_at = iota((FACE, columns), 1) % FACE
    out_rows = [full_ref[pl.ds(k * nodes + nodes - FACE, FACE), :] for k in range(8)]
    out_rows = jnp.concatenate(out_rows, axis=0)
    row_class = iota((128, columns), 0) // FACE
    pick_row, pick_lane = iota((128, 256), 0), iota((128, 256), 1)
    maps = [None] * rows_y
    for x in range(planes):
        own = [faces(u_ref[x, y]) for y in range(rows_y)]
        under = jnp.where(place > 0, faces(below_ref[x, below_ref.shape[1] - 1])[16:32], 0.0)
        over = jnp.where(place < gy_size - 1, faces(above_ref[x, 0])[0:16], 0.0)
        for y in range(rows_y):
            at = x * rows_y + y
            y_flag = on_columns[planes * rows_y + at][None, :]
            z_flag = on_columns[2 * planes * rows_y + at][None, :]
            from_below = own[y - 1][16:32] if y > 0 else under
            from_above = own[y + 1][0:16] if y < rows_y - 1 else over
            from_front = jnp.where(z_at == 0, 0.0, pltpu.roll(own[y][48:64], 1, 1))
            from_back = jnp.where(z_at == FACE - 1, 0.0, pltpu.roll(own[y][32:48], columns - 1, 1))
            lateral = jnp.concatenate(
                [
                    from_below * (1.0 - y_flag),
                    from_above * y_flag,
                    from_front * (1.0 - z_flag),
                    from_back * z_flag,
                ],
                axis=0,
            ).astype(BF16)
            data = jnp.concatenate([rhs_ref[x, y], lateral], axis=0)
            x_ref[x, y] = data
            every = jnp.dot(out_rows, jnp.concatenate([data, data], axis=0), preferred_element_type=F32)
            every = jnp.where(row_class == on_columns[at][None, :].astype(jnp.int32), every, 0.0)
            outflow = sum(every[k * FACE:(k + 1) * FACE] for k in range(8))
            wide_class = on_wide[at][None, :].astype(jnp.int32)
            pick = (pick_row // FACE == wide_class) & (pick_row % FACE == pick_lane % FACE)
            linear = exact(step_ref[...], pick.astype(F32))
            here = jnp.concatenate([linear, encode(outflow)], axis=0)
            maps[y] = here if maps[y] is None else join(maps[y], here)
    for y in range(rows_y):
        map_ref[y] = maps[y]


def solve_kernel(x_ref, row_ref, full_ref, inflow_ref, w_ref, start_ref):
    planes, rows_y, _, columns = x_ref.shape
    nodes = w_ref.shape[2]
    for x in range(planes):
        for y in range(rows_y):
            data = x_ref[x, y]
            every = jnp.dot(full_ref[...], jnp.concatenate([data, data], axis=0), preferred_element_type=F32)
            label = row_ref[pl.ds(x * rows_y + y, 1), :]
            total = jnp.zeros((nodes, columns), F32)
            for k in range(8):
                total = total + jnp.where(label == k, every[k * nodes:(k + 1) * nodes], 0.0)
            w_ref[x, y] = total
    for y in range(rows_y):
        start_ref[y] = encode(inflow_ref[y])


def group_kernel(size, power, *refs):
    blocks, (total_ref, before_ref, held) = refs[:size], refs[size:]
    for s in range(size):
        held[s] = blocks[s][...]
    mine = lax.axis_index("gx") % size
    for y in range(total_ref.shape[0]):
        so_far, before = None, None
        for j in range(size):
            slot = (mine ^ j) if power else (mine - j + size) % size
            if j > 0:
                before = so_far if before is None else jnp.where(mine >= j, so_far, before)
            block = held[slot, y]
            so_far = block if so_far is None else join(so_far, block)
        total_ref[y] = so_far
        if before is None:
            before = so_far
        same = (iota((24, 256), 1) % FACE == iota((24, 256), 0)).astype(F32)
        before_ref[y] = jnp.where(mine > 0, before, same)


def finish_kernel(size, inner, power, *refs):
    blocks = refs[:size]
    before_ref, start_ref, w_ref, row_ref, coup_ref, out_ref, held = refs[size:]
    planes, rows_y, nodes, columns = w_ref.shape
    for s in range(size):
        held[s] = blocks[s][...]
    mine = lax.axis_index("gx") // inner
    for y in range(rows_y):
        trace = start_ref[y]
        for j in range(size - 1):
            slot = (mine ^ j) if power else (mine - j + size) % size
            trace = jnp.where(mine > j, advance(trace, held[slot, y]), trace)
        trace = advance(trace, before_ref[y])
        trace = decode(trace)
        for x in range(planes):
            first, second = split(trace)
            both = jnp.concatenate([first, second, first, jnp.zeros((128 - 48, columns), BF16)], axis=0)
            every = jnp.dot(coup_ref[...], both, preferred_element_type=F32)
            label = row_ref[pl.ds(x * rows_y + y, 1), :]
            total = w_ref[x, y]
            for k in range(8):
                total = total + jnp.where(label == k, every[k * nodes:(k + 1) * nodes], 0.0)
            out_ref[x, y] = total
            trace = total[nodes - FACE:]


def moved(value, pairs):
    return lax.ppermute(value, ("gx", "gy"), pairs)


def shape(dims, kind=F32):
    return jax.ShapeDtypeStruct(dims, kind)


def call(kernel, outs, name, args, scratch=(), flops=1000000, limit=48):
    return pl.pallas_call(
        kernel,
        out_shape=outs,
        in_specs=[pl.BlockSpec(memory_space=pltpu.VMEM)] * len(args),
        out_specs=jax.tree.map(lambda _: pl.BlockSpec(memory_space=pltpu.VMEM), outs),
        scratch_shapes=list(scratch),
        name=name,
        cost_estimate=pl.CostEstimate(flops=flops, bytes_accessed=500000, transcendentals=0),
        compiler_params=pltpu.CompilerParams(vmem_limit_bytes=limit * 1024 * 1024),
    )(*args)


def on_device(gx_size, gy_size, u_old, rhs, classes, flags, inverse, x_face, lateral_faces, inflow):
    planes, rows_y, nodes, columns = u_old.shape
    count = inverse.shape[0]
    everyone = [(x, y) for x in range(gx_size) for y in range(gy_size)]

    def at(x, y):
        return x * gy_size + y

    if gy_size == 2:
        below = above = moved(u_old, [(at(x, y), at(x, 1 - y)) for x, y in everyone])
    else:
        below = moved(u_old[:, rows_y - 1:], [(at(x, y), at(x, y + 1)) for x, y in everyone if y + 1 < gy_size])
        above = moved(u_old[:, :1], [(at(x, y), at(x, y - 1)) for x, y in everyone if y > 0])
    full, coup, step = call(
        params_kernel,
        (shape((count * nodes, 256), BF16), shape((count * nodes, 128), BF16), shape((FACE, 128))),
        "class_matrices",
        (inverse, x_face, lateral_faces),
    )
    data, labels, here = call(
        functools.partial(sources_kernel, gy_size),
        (
            shape((planes, rows_y, 128, columns), BF16),
            shape((3 * planes * rows_y, columns)),
            shape((rows_y, 24, 256)),
        ),
        "sources",
        (u_old, rhs, below, above, classes, flags, full, step),
    )
    inner = 4 if gx_size % 4 == 0 else 1
    outer = gx_size // inner
    power = outer & (outer - 1) == 0
    blocks = [here]
    for s in range(1, inner):
        blocks.append(moved(here, [(at(x, y), at(x ^ s, y)) for x, y in everyone]))
    solved, start = call(
        solve_kernel,
        (shape((planes, rows_y, nodes, columns)), shape((rows_y, 8, 256))),
        "local_solve",
        (data, labels, full, inflow),
    )
    total, before = call(
        functools.partial(group_kernel, inner, True),
        (shape((rows_y, 24, 256)), shape((rows_y, 24, 256))),
        "group_maps",
        tuple(blocks),
        [pltpu.VMEM((inner, rows_y, 24, 256), F32)],
    )
    blocks = [total]
    for s in range(1, outer):
        if power:
            pairs = [(at(x, y), at(x ^ (s * inner), y)) for x, y in everyone]
        else:
            pairs = [(at(x, y), at((x + s * inner) % gx_size, y)) for x, y in everyone]
        blocks.append(moved(total, pairs))
    return call(
        functools.partial(finish_kernel, outer, inner, power),
        shape((planes, rows_y, nodes, columns)),
        "finish",
        tuple(blocks) + (before, start, solved, labels, coup),
        [pltpu.VMEM((outer, rows_y, 24, 256), F32)],
    )


def solution(mesh):
    in_specs = (
        P("gx", "gy", None, None),
        P("gx", "gy", None, None),
        P("gx", "gy", None),
        P(None, "gx", "gy", None),
        P(),
        P(),
        P(),
        P("gy", None, None),
    )
    out_specs = P("gx", "gy", None, None)
    body = functools.partial(on_device, mesh.shape["gx"], mesh.shape["gy"])
    return jax.shard_map(body, mesh=mesh, in_specs=in_specs, out_specs=out_specs, check_vma=False)
```

```python
import functools

import jax
import jax.numpy as jnp
from jax import lax
from jax.experimental import pallas as pl
from jax.experimental.pallas import tpu as pltpu
from jax.sharding import PartitionSpec as P

FACE = 16
HIGH = lax.Precision.HIGHEST
F32 = jnp.float32
BF16 = jnp.bfloat16


def iota(shape, dim):
    return lax.broadcasted_iota(jnp.int32, shape, dim)


def exact(left, right):
    return jnp.dot(left, right, precision=HIGH, preferred_element_type=F32)


def split(value):
    high = value.astype(BF16)
    return high, (value - high.astype(F32)).astype(BF16)


def wanted_node(face, item):
    high, low = item // 4, item % 4
    return jnp.where(face < 2, 16 * high + low + 12 * (face == 1), 16 * high + 4 * low + 3 * (face == 3))


def dot(left, right):
    return jnp.dot(left, right, preferred_element_type=F32)


def dot_rows(left, right):
    return lax.dot_general(left, right, (((1,), (1,)), ((), ())), preferred_element_type=F32)


def applied(rows, linear):
    lane = iota((rows.shape[0], 128), 1)
    halves = []
    for begin in (0, 128):
        part, total = rows[:, begin:begin + 128], None
        for b in range(FACE):
            near = jnp.take_along_axis(part, lane // FACE * FACE + b, axis=1, mode="promise_in_bounds")
            term = near * linear[b:b + 1, begin:begin + 128]
            total = term if total is None else total + term
        halves.append(total)
    return jnp.concatenate(halves, axis=1)


def join(earlier, later):
    moved_rows = applied(earlier, later[:FACE])
    return jnp.concatenate([moved_rows[:FACE], moved_rows[FACE:] + later[FACE:]], axis=0)


def advance(trace, later):
    return applied(trace, later[:FACE]) + later[FACE:]


def encode(value):
    high, low = split(value)
    both = jnp.concatenate([high, low], axis=1)
    tile = (iota((256, FACE), 0) % FACE == iota((256, FACE), 1)).astype(BF16)
    spread = dot(tile, both)
    keep = iota((256, 256), 0) // FACE == iota((256, 256), 1) % FACE
    spread = jnp.where(keep, spread, 0.0).astype(BF16)
    gather = (iota((8, 256), 1) % 128 // FACE == iota((8, 256), 0)).astype(BF16)
    return dot_rows(gather, spread)


def class_products(inv_rows, weights):
    count = inv_rows.shape[0]
    high, low = split(inv_rows)
    parts = dot(jnp.concatenate([high, low], axis=0), weights)
    return -(parts[:count, :128] + parts[:count, 128:] + parts[count:, :128])


def with_inverse(inv_rows, products):
    count = inv_rows.shape[0]
    wide = jnp.concatenate([inv_rows, jnp.zeros((count, 128 - inv_rows.shape[1]), F32)], axis=1)
    return jnp.where(iota((count, 128), 1) < 64, wide, products)


def in_parts(value):
    high, low = split(value)
    return jnp.concatenate([high, low], axis=1)


def coupling_parts(products):
    high, low = split(products)
    lane = iota(products.shape, 1)
    return jnp.where(lane < 32, high.astype(F32), jnp.where(lane < 48, low.astype(F32), 0.0)).astype(BF16)


def params_kernel(inv_hbm, x_hbm, lat_hbm, cls_hbm, flag_hbm, weight_ref, out_ref, step_ref, lin_ref, label_ref,
                  inv_ref, x_ref, lat_ref, cls_ref, flag_ref, sems):
    pairs = ((lat_hbm, lat_ref), (x_hbm, x_ref), (inv_hbm, inv_ref), (cls_hbm, cls_ref), (flag_hbm, flag_ref))
    copies = [pltpu.make_async_copy(a, b, sems.at[i]) for i, (a, b) in enumerate(pairs)]
    for copy in copies:
        copy.start()
    count, nodes, _ = inv_ref.shape
    planes, rows_y, _ = cls_ref.shape
    item, lane = iota((FACE, 128), 0), iota((FACE, 128), 1)
    places = [(lane == 64 + FACE * f + item).astype(BF16) for f in range(4)]
    places.append(((lane < 48) & (lane % FACE == item)).astype(BF16))
    at = iota((nodes, 5 * FACE), 1)
    wanted = jnp.where(at < 64, wanted_node(at // FACE, at % FACE), at - 64)
    chosen = (iota((nodes, 5 * FACE), 0) == wanted).astype(BF16)
    for copy in copies:
        copy.wait()
    placed = []
    for f in range(5):
        rows = (lat_ref[f] if f < 4 else x_ref[...]).reshape(count * FACE, FACE)
        placed.append(dot(jnp.concatenate(split(rows), axis=0), places[f]).astype(BF16))
    columns = []
    for k in range(count):
        for part in range(2):
            begin = part * count * FACE + k * FACE
            columns.append(jnp.concatenate([p[begin:begin + FACE] for p in placed], axis=0))
    weights = dot(chosen, jnp.concatenate(columns, axis=1)).astype(BF16)
    weight_ref[...] = weights
    outs, steps = [], []
    for k in range(count):
        inv_rows = inv_ref[k, nodes - FACE:, :]
        products = class_products(inv_rows, weights[:, 256 * k:256 * k + 256])
        outs.append(with_inverse(inv_rows, products))
        steps.append(products)
    out_ref[...] = in_parts(jnp.concatenate(outs, axis=0))
    step = coupling_parts(jnp.concatenate(steps, axis=0))
    step_ref[...] = step
    flip_row, flip_lane = iota((2 * FACE, 128), 0), iota((2 * FACE, 128), 1)
    flip = (flip_lane == flip_row + FACE * (flip_row >= FACE)).astype(BF16)
    turned = dot_rows(flip, step).astype(BF16)
    labels = [cls_ref[x] for x in range(planes)]
    labels += [flag_ref[d, x] for d in range(2) for x in range(planes)]
    labels = jnp.concatenate(labels, axis=0).astype(F32).astype(BF16)
    tile = (iota((FACE, 128), 1) % FACE == iota((FACE, 128), 0)).astype(BF16)
    label_ref[...] = dot(labels, tile)
    wide = (iota((FACE, 256), 1) // FACE == iota((FACE, 256), 0)).astype(BF16)
    on_wide = dot(labels, wide).astype(jnp.int32)
    pick_row, pick_lane = iota((128, 256), 0), iota((128, 256), 1)
    same = pick_row % FACE == pick_lane % FACE
    for y in range(rows_y):
        whole = None
        for x in range(planes):
            here = on_wide[x * rows_y + y:x * rows_y + y + 1]
            pick = jnp.where(same & (pick_row // FACE == here), 1.0, 0.0).astype(BF16)
            both = dot(turned, pick)
            linear = both[:FACE] + both[FACE:]
            lin_ref[x, y] = linear
            whole = linear if whole is None else applied(whole, linear)
        lin_ref[planes, y] = whole


def class_sum(every, label, rows):
    total = None
    for k in range(8):
        term = jnp.where(label == k, every[k * rows:(k + 1) * rows], 0.0)
        total = term if total is None else total + term
    return total


def stacked(value):
    first, second = split(value)
    rest = jnp.zeros((128 - 3 * FACE, value.shape[1]), BF16)
    return jnp.concatenate([first, second, first, rest], axis=0)


def sources_kernel(gy_size, u_ref, rhs_ref, below_ref, above_ref, label_ref, out_ref, step_ref, lin_ref, x_ref, flow_ref, map_ref):
    planes, rows_y, nodes, columns = u_ref.shape
    place = lax.axis_index("gy")
    node, item = iota((nodes, nodes), 1), iota((nodes, nodes), 0)
    chosen = (node == wanted_node(item // FACE, item % FACE)).astype(BF16)
    own = [u_ref[x, y] for x in range(planes) for y in range(rows_y)]
    other = [below_ref[x, below_ref.shape[1] - 1] for x in range(planes)] + [above_ref[x, 0] for x in range(planes)]
    faces = dot(chosen, jnp.concatenate(own + other, axis=1))
    faces = [faces[:, i * columns:(i + 1) * columns] for i in range(len(own) + len(other))]
    z_at = iota((FACE, columns), 1) % FACE
    has_below = jnp.where(place > 0, 1.0, 0.0)
    has_above = jnp.where(place < gy_size - 1, 1.0, 0.0)
    data = []
    for x in range(planes):
        under = faces[len(own) + x][16:32] * has_below
        over = faces[len(own) + planes + x][0:16] * has_above
        for y in range(rows_y):
            at = x * rows_y + y
            y_flag = label_ref[pl.ds(planes * rows_y + at, 1), :]
            z_flag = label_ref[pl.ds(2 * planes * rows_y + at, 1), :]
            from_below = faces[at - 1][16:32] if y > 0 else under
            from_above = faces[at + 1][0:16] if y < rows_y - 1 else over
            from_front = jnp.where(z_at == 0, 0.0, pltpu.roll(faces[at][48:64], 1, 1))
            from_back = jnp.where(z_at == FACE - 1, 0.0, pltpu.roll(faces[at][32:48], columns - 1, 1))
            lateral = jnp.concatenate(
                [
                    from_below * (1.0 - y_flag),
                    from_above * y_flag,
                    from_front * (1.0 - z_flag),
                    from_back * z_flag,
                ],
                axis=0,
            ).astype(BF16)
            here = jnp.concatenate([rhs_ref[x, y], lateral], axis=0)
            x_ref[x, y] = here
            data.append(here)
    data = jnp.concatenate(data, axis=1)
    every = dot(out_ref[...], jnp.concatenate([data, data], axis=0))
    total = None
    for x in range(planes):
        begin = x * rows_y * columns
        label = jnp.concatenate([label_ref[pl.ds(x * rows_y + y, 1), :] for y in range(rows_y)], axis=1)
        flow = class_sum(every[:, begin:begin + rows_y * columns], label, FACE)
        flow_ref[x] = flow
        if total is not None:
            flow = flow + class_sum(dot(step_ref[...], stacked(total)), label, FACE)
        total = flow
    for y in range(rows_y):
        map_ref[y, 0:FACE] = lin_ref[planes, y]
        map_ref[y, FACE:] = encode(total[:, y * columns:(y + 1) * columns])


def block_diagonal(linear):
    keep = (iota((256, 256), 0) // FACE == iota((256, 256), 1) // FACE).astype(BF16)
    return [jnp.concatenate([part] * 16, axis=0) * keep for part in split(linear)]


def join_blocks(earlier, later):
    high, low = split(jnp.concatenate([earlier, jnp.zeros((8, 256), F32)], axis=0))
    first, second = block_diagonal(later[:FACE])
    parts = dot(jnp.concatenate([high, low], axis=0), first)
    total = (parts[:32] + parts[32:] + dot(high, second))[:24]
    return jnp.concatenate([total[:FACE], total[FACE:] + later[FACE:]], axis=0)


def group_kernel(size, power, *refs):
    blocks, total_ref, held = refs[:size], refs[size], refs[size + 1]
    for s in range(size):
        held[s] = blocks[s][...]
    mine = lax.axis_index("gx") % size
    for y in range(total_ref.shape[0]):
        maps = [held[(mine ^ j) if power else (mine - j + size) % size, y] for j in range(size)]
        while len(maps) > 1:
            maps = [join_blocks(maps[i], maps[i + 1]) if i + 1 < len(maps) else maps[i] for i in range(0, len(maps), 2)]
        total_ref[y] = maps[0]


def solve_kernel(size, power, *refs):
    blocks = refs[:size]
    data_ref, label_ref, weight_ref, lin_ref, flow_ref, inv_ref, inflow_ref = refs[size:size + 7]
    w_ref, start_ref, coup_ref, before_ref, mask_ref, held, full_ref = refs[size + 7:]
    planes, rows_y, nodes, columns = w_ref.shape
    for k in range(inv_ref.shape[0]):
        inv_rows = inv_ref[k]
        products = class_products(inv_rows, weight_ref[:, 256 * k:256 * k + 256])
        here = pl.ds(k * nodes, nodes)
        moved_over = pltpu.roll(products, FACE * k, 1) if k else products
        coupling = jnp.where(iota((nodes, 128), 1) // FACE == k, moved_over, 0.0 if k == 0 else coupling)
        full_ref[here, :] = in_parts(with_inverse(inv_rows, products))
    coup_ref[...] = in_parts(coupling)
    for x in range(planes):
        for y in range(rows_y):
            label = label_ref[pl.ds(x * rows_y + y, 1), :]
            mask_ref[x, y] = jnp.where(iota((128, 128), 0) // FACE == label, 1.0, 0.0).T
            data = data_ref[x, y]
            every = dot(full_ref[...], jnp.concatenate([data, data], axis=0))
            w_ref[x, y] = class_sum(every, label, nodes)
    for s in range(size):
        held[s] = blocks[s][...]
    mine = lax.axis_index("gx") % size
    same = (iota((24, 256), 1) % FACE == iota((24, 256), 0)).astype(F32)
    for y in range(rows_y):
        start_ref[y] = encode(inflow_ref[y])
        before = same
        for j in range(size - 1):
            block = held[(mine ^ j) if power else (mine - j + size) % size, y]
            before = jnp.where(mine > j, block if j == 0 else join(before, block), before)
        for x in range(planes):
            before_ref[x, y] = before
            if x < planes - 1:
                offset = encode(flow_ref[x, :, y * columns:(y + 1) * columns])
                before = join(before, jnp.concatenate([lin_ref[x, y], offset], axis=0))


def finish_kernel(size, inner, power, *refs):
    blocks = refs[:size]
    before_ref, start_ref, w_ref, mask_ref, coup_ref, out_ref, held = refs[size:]
    planes, rows_y, nodes, columns = w_ref.shape
    for s in range(size):
        held[s] = blocks[s][...]
    mine = lax.axis_index("gx") // inner
    traces = []
    for y in range(rows_y):
        trace = start_ref[y]
        for j in range(size - 1):
            slot = (mine ^ j) if power else (mine - j + size) % size
            trace = jnp.where(mine > j, advance(trace, held[slot, y]), trace)
        traces.append(trace)
    entering = [advance(traces[y], before_ref[x, y]) for x in range(planes) for y in range(rows_y)]
    entering = jnp.concatenate(entering, axis=1)
    first, second = split(entering)
    row, lane = iota((256, 2 * FACE), 0), iota((256, 2 * FACE), 1)
    spread = (lane == row % 128 // FACE + FACE * (row >= 128)).astype(BF16)
    rest = jnp.zeros((8, entering.shape[1]), BF16)
    rows = dot(spread, jnp.concatenate([first, rest, second, rest], axis=0))
    keep = iota((256, 256), 0) % FACE == iota((256, 256), 1) // FACE
    fold = (iota((256, 128), 0) % FACE == iota((256, 128), 1) % FACE).astype(BF16)
    parts = [jnp.where(keep, rows[:, at:at + 256], 0.0).astype(BF16) for at in range(0, rows.shape[1], 256)]
    values = dot(jnp.concatenate(parts, axis=0), fold)
    coupling = coup_ref[...]
    for x in range(planes):
        for y in range(rows_y):
            begin = (x * rows_y + y) * 256
            first = (values[begin:begin + 128] * mask_ref[x, y]).astype(BF16)
            second = (values[begin + 128:begin + 256] * mask_ref[x, y]).astype(BF16)
            sums = dot_rows(coupling, jnp.concatenate([first, first], axis=1)) + dot_rows(coupling[:, :128], second)
            out_ref[x, y] = w_ref[x, y] + sums


def moved(value, pairs):
    return lax.ppermute(value, ("gx", "gy"), pairs)


def shape(dims, kind=F32):
    return jax.ShapeDtypeStruct(dims, kind)


def call(kernel, outs, name, args, scratch=(), flops=1000000, limit=48, space=pltpu.VMEM):
    return pl.pallas_call(
        kernel,
        out_shape=outs,
        in_specs=[pl.BlockSpec(memory_space=space)] * len(args),
        out_specs=jax.tree.map(lambda _: pl.BlockSpec(memory_space=pltpu.VMEM), outs),
        scratch_shapes=list(scratch),
        name=name,
        cost_estimate=pl.CostEstimate(flops=flops, bytes_accessed=500000, transcendentals=0),
        compiler_params=pltpu.CompilerParams(vmem_limit_bytes=limit * 1024 * 1024),
    )(*args)


def on_device(gx_size, gy_size, u_old, rhs, classes, flags, inverse, x_face, lateral_faces, inflow):
    planes, rows_y, nodes, columns = u_old.shape
    count = inverse.shape[0]
    everyone = [(x, y) for x in range(gx_size) for y in range(gy_size)]

    def at(x, y):
        return x * gy_size + y

    if gy_size == 2:
        below = above = moved(u_old, [(at(x, y), at(x, 1 - y)) for x, y in everyone])
    else:
        below = moved(u_old[:, rows_y - 1:], [(at(x, y), at(x, y + 1)) for x, y in everyone if y + 1 < gy_size])
        above = moved(u_old[:, :1], [(at(x, y), at(x, y - 1)) for x, y in everyone if y > 0])
    weights, out_rows, step, linear, labels = call(
        params_kernel,
        (
            shape((nodes, count * 256), BF16),
            shape((count * FACE, 256), BF16),
            shape((count * FACE, 128), BF16),
            shape((planes + 1, rows_y, FACE, 256)),
            shape((3 * planes * rows_y, columns)),
        ),
        "class_matrices",
        tuple(
            pltpu.with_memory_space_constraint(value, pltpu.HBM)
            for value in (inverse, x_face, lateral_faces, classes, flags)
        ),
        [
            pltpu.VMEM(inverse.shape, F32),
            pltpu.VMEM(x_face.shape, F32),
            pltpu.VMEM(lateral_faces.shape, F32),
            pltpu.VMEM(classes.shape, jnp.int32),
            pltpu.VMEM(flags.shape, jnp.int32),
            pltpu.SemaphoreType.DMA((5,)),
        ],
        space=pltpu.HBM,
    )
    data, flow, here = call(
        functools.partial(sources_kernel, gy_size),
        (
            shape((planes, rows_y, 128, columns), BF16),
            shape((planes, FACE, rows_y * columns)),
            shape((rows_y, 24, 256)),
        ),
        "sources",
        (u_old, rhs, below, above, labels, out_rows, step, linear),
    )
    inner = 4 if gx_size % 4 == 0 else 1
    outer = gx_size // inner
    power = outer & (outer - 1) == 0
    near = [here]
    for s in range(1, inner):
        near.append(moved(here, [(at(x, y), at(x ^ s, y)) for x, y in everyone]))
    total = call(
        functools.partial(group_kernel, inner, True),
        shape((rows_y, 24, 256)),
        "group_maps",
        tuple(near),
        [pltpu.VMEM((inner, rows_y, 24, 256), F32)],
    )
    blocks = [total]
    for s in range(1, outer):
        if power:
            pairs = [(at(x, y), at(x ^ (s * inner), y)) for x, y in everyone]
        else:
            pairs = [(at(x, y), at((x + s * inner) % gx_size, y)) for x, y in everyone]
        blocks.append(moved(total, pairs))
    solved, start, coup, before, masks = call(
        functools.partial(solve_kernel, inner, True),
        (
            shape((planes, rows_y, nodes, columns)),
            shape((rows_y, 8, 256)),
            shape((nodes, 256), BF16),
            shape((planes, rows_y, 24, 256)),
            shape((planes, rows_y, 128, 128)),
        ),
        "local_solve",
        tuple(near) + (data, labels, weights, linear, flow, inverse, inflow),
        [pltpu.VMEM((inner, rows_y, 24, 256), F32), pltpu.VMEM((count * nodes, 256), BF16)],
    )
    return call(
        functools.partial(finish_kernel, outer, inner, power),
        shape((planes, rows_y, nodes, columns)),
        "finish",
        tuple(blocks) + (before, start, solved, masks, coup),
        [pltpu.VMEM((outer, rows_y, 24, 256), F32)],
    )


def solution(mesh):
    in_specs = (
        P("gx", "gy", None, None),
        P("gx", "gy", None, None),
        P("gx", "gy", None),
        P(None, "gx", "gy", None),
        P(),
        P(),
        P(),
        P("gy", None, None),
    )
    out_specs = P("gx", "gy", None, None)
    body = functools.partial(on_device, mesh.shape["gx"], mesh.shape["gy"])
    return jax.shard_map(body, mesh=mesh, in_specs=in_specs, out_specs=out_specs, check_vma=False)
```

```python
import functools

import jax
import jax.numpy as jnp
from jax import lax
from jax.experimental import pallas as pl
from jax.experimental.pallas import tpu as pltpu
from jax.sharding import PartitionSpec as P

FACE = 16
HIGH = lax.Precision.HIGHEST
F32 = jnp.float32
BF16 = jnp.bfloat16


def iota(shape, dim):
    return lax.broadcasted_iota(jnp.int32, shape, dim)


def exact(left, right):
    return jnp.dot(left, right, precision=HIGH, preferred_element_type=F32)


def split(value):
    high = value.astype(BF16)
    return high, (value - high.astype(F32)).astype(BF16)


def wanted_node(face, item):
    high, low = item // 4, item % 4
    return jnp.where(face < 2, 16 * high + low + 12 * (face == 1), 16 * high + 4 * low + 3 * (face == 3))


def dot(left, right):
    return jnp.dot(left, right, preferred_element_type=F32)


def dot_rows(left, right):
    return lax.dot_general(left, right, (((1,), (1,)), ((), ())), preferred_element_type=F32)


def applied(rows, linear):
    lane = iota((rows.shape[0], 128), 1)
    halves = []
    for begin in (0, 128):
        part, total = rows[:, begin:begin + 128], None
        for b in range(FACE):
            near = jnp.take_along_axis(part, lane // FACE * FACE + b, axis=1, mode="promise_in_bounds")
            term = near * linear[b:b + 1, begin:begin + 128]
            total = term if total is None else total + term
        halves.append(total)
    return jnp.concatenate(halves, axis=1)


def join(earlier, later):
    moved_rows = applied(earlier, later[:FACE])
    return jnp.concatenate([moved_rows[:FACE], moved_rows[FACE:] + later[FACE:]], axis=0)


def advance(trace, later):
    return applied(trace, later[:FACE]) + later[FACE:]


def encode(value):
    high, low = split(value)
    both = jnp.concatenate([high, low], axis=1)
    tile = (iota((256, FACE), 0) % FACE == iota((256, FACE), 1)).astype(BF16)
    spread = dot(tile, both)
    keep = iota((256, 256), 0) // FACE == iota((256, 256), 1) % FACE
    spread = jnp.where(keep, spread, 0.0).astype(BF16)
    gather = (iota((8, 256), 1) % 128 // FACE == iota((8, 256), 0)).astype(BF16)
    return dot_rows(gather, spread)


def class_products(inv_rows, weights):
    count = inv_rows.shape[0]
    high, low = split(inv_rows)
    parts = dot(jnp.concatenate([high, low], axis=0), weights)
    return -(parts[:count, :128] + parts[:count, 128:] + parts[count:, :128])


def with_inverse(inv_rows, products):
    count = inv_rows.shape[0]
    wide = jnp.concatenate([inv_rows, jnp.zeros((count, 128 - inv_rows.shape[1]), F32)], axis=1)
    return jnp.where(iota((count, 128), 1) < 64, wide, products)


def in_parts(value):
    high, low = split(value)
    return jnp.concatenate([high, low], axis=1)


def coupling_parts(products):
    high, low = split(products)
    lane = iota(products.shape, 1)
    return jnp.where(lane < 32, high.astype(F32), jnp.where(lane < 48, low.astype(F32), 0.0)).astype(BF16)


def params_kernel(inv_hbm, x_hbm, lat_hbm, cls_hbm, flag_hbm, weight_ref, out_ref, step_ref, lin_ref, label_ref,
                  inv_ref, x_ref, lat_ref, cls_ref, flag_ref, sems):
    pairs = ((lat_hbm, lat_ref), (x_hbm, x_ref), (inv_hbm, inv_ref), (cls_hbm, cls_ref), (flag_hbm, flag_ref))
    copies = [pltpu.make_async_copy(a, b, sems.at[i]) for i, (a, b) in enumerate(pairs)]
    for copy in copies:
        copy.start()
    count, nodes, _ = inv_ref.shape
    planes, rows_y, _ = cls_ref.shape
    item, lane = iota((FACE, 128), 0), iota((FACE, 128), 1)
    places = [(lane == 64 + FACE * f + item).astype(BF16) for f in range(4)]
    places.append(((lane < 48) & (lane % FACE == item)).astype(BF16))
    at = iota((nodes, 5 * FACE), 1)
    wanted = jnp.where(at < 64, wanted_node(at // FACE, at % FACE), at - 64)
    chosen = (iota((nodes, 5 * FACE), 0) == wanted).astype(BF16)
    for copy in copies:
        copy.wait()
    placed = []
    for f in range(5):
        rows = (lat_ref[f] if f < 4 else x_ref[...]).reshape(count * FACE, FACE)
        placed.append(dot(jnp.concatenate(split(rows), axis=0), places[f]).astype(BF16))
    columns = []
    for k in range(count):
        for part in range(2):
            begin = part * count * FACE + k * FACE
            columns.append(jnp.concatenate([p[begin:begin + FACE] for p in placed], axis=0))
    weights = dot(chosen, jnp.concatenate(columns, axis=1)).astype(BF16)
    weight_ref[...] = weights
    outs, steps = [], []
    for k in range(count):
        inv_rows = inv_ref[k, nodes - FACE:, :]
        products = class_products(inv_rows, weights[:, 256 * k:256 * k + 256])
        outs.append(with_inverse(inv_rows, products))
        steps.append(products)
    out_ref[...] = in_parts(jnp.concatenate(outs, axis=0))
    step = coupling_parts(jnp.concatenate(steps, axis=0))
    step_ref[...] = step
    flip_row, flip_lane = iota((2 * FACE, 128), 0), iota((2 * FACE, 128), 1)
    flip = (flip_lane == flip_row + FACE * (flip_row >= FACE)).astype(BF16)
    turned = dot_rows(flip, step).astype(BF16)
    labels = [cls_ref[x] for x in range(planes)]
    labels += [flag_ref[d, x] for d in range(2) for x in range(planes)]
    labels = jnp.concatenate(labels, axis=0).astype(F32).astype(BF16)
    tile = (iota((FACE, 128), 1) % FACE == iota((FACE, 128), 0)).astype(BF16)
    label_ref[...] = dot(labels, tile)
    wide = (iota((FACE, 256), 1) // FACE == iota((FACE, 256), 0)).astype(BF16)
    on_wide = dot(labels, wide).astype(jnp.int32)
    pick_row, pick_lane = iota((128, 256), 0), iota((128, 256), 1)
    same = pick_row % FACE == pick_lane % FACE
    for y in range(rows_y):
        whole = None
        for x in range(planes):
            here = on_wide[x * rows_y + y:x * rows_y + y + 1]
            pick = jnp.where(same & (pick_row // FACE == here), 1.0, 0.0).astype(BF16)
            both = dot(turned, pick)
            linear = both[:FACE] + both[FACE:]
            lin_ref[x, y] = linear
            whole = linear if whole is None else applied(whole, linear)
        lin_ref[planes, y] = whole


def class_sum(every, label, rows):
    total = None
    for k in range(8):
        term = jnp.where(label == k, every[k * rows:(k + 1) * rows], 0.0)
        total = term if total is None else total + term
    return total


def stacked(value):
    first, second = split(value)
    rest = jnp.zeros((128 - 3 * FACE, value.shape[1]), BF16)
    return jnp.concatenate([first, second, first, rest], axis=0)


def sources_kernel(gy_size, u_ref, rhs_ref, below_ref, above_ref, label_ref, out_ref, step_ref, lin_ref, x_ref, flow_ref, map_ref):
    planes, rows_y, nodes, columns = u_ref.shape
    place = lax.axis_index("gy")
    node, item = iota((nodes, nodes), 1), iota((nodes, nodes), 0)
    chosen = (node == wanted_node(item // FACE, item % FACE)).astype(BF16)
    own = [u_ref[x, y] for x in range(planes) for y in range(rows_y)]
    other = [below_ref[x, below_ref.shape[1] - 1] for x in range(planes)] + [above_ref[x, 0] for x in range(planes)]
    faces = dot(chosen, jnp.concatenate(own + other, axis=1))
    faces = [faces[:, i * columns:(i + 1) * columns] for i in range(len(own) + len(other))]
    z_at = iota((FACE, columns), 1) % FACE
    has_below = jnp.where(place > 0, 1.0, 0.0)
    has_above = jnp.where(place < gy_size - 1, 1.0, 0.0)
    data = []
    for x in range(planes):
        under = faces[len(own) + x][16:32] * has_below
        over = faces[len(own) + planes + x][0:16] * has_above
        for y in range(rows_y):
            at = x * rows_y + y
            y_flag = label_ref[pl.ds(planes * rows_y + at, 1), :]
            z_flag = label_ref[pl.ds(2 * planes * rows_y + at, 1), :]
            from_below = faces[at - 1][16:32] if y > 0 else under
            from_above = faces[at + 1][0:16] if y < rows_y - 1 else over
            from_front = jnp.where(z_at == 0, 0.0, pltpu.roll(faces[at][48:64], 1, 1))
            from_back = jnp.where(z_at == FACE - 1, 0.0, pltpu.roll(faces[at][32:48], columns - 1, 1))
            lateral = jnp.concatenate(
                [
                    from_below * (1.0 - y_flag),
                    from_above * y_flag,
                    from_front * (1.0 - z_flag),
                    from_back * z_flag,
                ],
                axis=0,
            ).astype(BF16)
            here = jnp.concatenate([rhs_ref[x, y], lateral], axis=0)
            x_ref[x, y] = here
            data.append(here)
    data = jnp.concatenate(data, axis=1)
    every = dot(out_ref[...], jnp.concatenate([data, data], axis=0))
    total = None
    for x in range(planes):
        begin = x * rows_y * columns
        label = jnp.concatenate([label_ref[pl.ds(x * rows_y + y, 1), :] for y in range(rows_y)], axis=1)
        flow = class_sum(every[:, begin:begin + rows_y * columns], label, FACE)
        flow_ref[x] = flow
        if total is not None:
            flow = flow + class_sum(dot(step_ref[...], stacked(total)), label, FACE)
        total = flow
    for y in range(rows_y):
        map_ref[y, 0:FACE] = lin_ref[planes, y]
        map_ref[y, FACE:] = encode(total[:, y * columns:(y + 1) * columns])


def block_diagonal(linear):
    keep = (iota((256, 256), 0) // FACE == iota((256, 256), 1) // FACE).astype(BF16)
    return [jnp.concatenate([part] * 16, axis=0) * keep for part in split(linear)]


def join_blocks(earlier, later):
    high, low = split(jnp.concatenate([earlier, jnp.zeros((8, 256), F32)], axis=0))
    first, second = block_diagonal(later[:FACE])
    parts = dot(jnp.concatenate([high, low], axis=0), first)
    total = (parts[:32] + parts[32:] + dot(high, second))[:24]
    return jnp.concatenate([total[:FACE], total[FACE:] + later[FACE:]], axis=0)


def group_kernel(size, power, *refs):
    blocks, total_ref, held = refs[:size], refs[size], refs[size + 1]
    for s in range(size):
        held[s] = blocks[s][...]
    mine = lax.axis_index("gx") % size
    for y in range(total_ref.shape[0]):
        maps = [held[(mine ^ j) if power else (mine - j + size) % size, y] for j in range(size)]
        while len(maps) > 1:
            maps = [join_blocks(maps[i], maps[i + 1]) if i + 1 < len(maps) else maps[i] for i in range(0, len(maps), 2)]
        total_ref[y] = maps[0]


def carried(parts, traces, count):
    first, second = split(jnp.concatenate(traces, axis=1))
    row, lane = iota((256, 2 * FACE), 0), iota((256, 2 * FACE), 1)
    spread = (lane == row % 128 // FACE + FACE * (row >= 128)).astype(BF16)
    rest = jnp.zeros((8, first.shape[1]), BF16)
    rows = dot(spread, jnp.concatenate([first, rest, second, rest], axis=0))
    keep = iota((256, 256), 0) % FACE == iota((256, 256), 1) // FACE
    sums = []
    for y, part in enumerate(parts):
        here = jnp.where(keep, rows[:, y * 256:y * 256 + 256], 0.0).astype(BF16)
        high = part[:count]
        by_first = dot_rows(part, here[:128])
        sums.append(by_first[:count] + by_first[count:] + dot_rows(high, here[128:]))
    return sums


def write_nodes(result_ref, out_ref, sems, base_ref, part_ref, traces):
    planes, rows_y, nodes, _ = result_ref.shape
    sums = carried([part_ref[y] for y in range(rows_y)], traces, planes * nodes)
    copies = []
    for y in range(rows_y):
        for x in range(planes):
            result_ref[x, y] = base_ref[x, y] + sums[y][x * nodes:(x + 1) * nodes]
            copies.append(pltpu.make_async_copy(result_ref.at[x, y], out_ref.at[x, y], sems.at[x, y]))
            copies[-1].start()
    for copy in copies:
        copy.wait()


def solve_kernel(size, power, *refs):
    blocks = refs[:size]
    data_ref, label_ref, weight_ref, lin_ref, flow_ref, inv_ref, inflow_ref = refs[size:size + 7]
    base_ref, start_ref, part_ref, out_ref, held, full_ref, result_ref, sems = refs[size + 7:]
    planes, rows_y, nodes, columns = base_ref.shape
    coupling = jnp.zeros((nodes, 128), F32)
    for k in range(inv_ref.shape[0]):
        inv_rows = inv_ref[k]
        products = class_products(inv_rows, weight_ref[:, 256 * k:256 * k + 256])
        here = pl.ds(k * nodes, nodes)
        shifted = pltpu.roll(products, FACE * k, 1) if k else products
        coupling = jnp.where(iota((nodes, 128), 1) // FACE == k, shifted, coupling)
        full_ref[here, :] = in_parts(with_inverse(inv_rows, products))
    coupling = jnp.concatenate(split(coupling), axis=0)
    for s in range(size):
        held[s] = blocks[s][...]
    place = lax.axis_index("gx")
    mine = place % size
    same = (iota((24, 256), 1) % FACE == iota((24, 256), 0)).astype(F32)
    wide = (iota((FACE, 256), 1) // FACE == iota((FACE, 256), 0)).astype(BF16)
    row, lane = iota((128, 256), 0), iota((128, 256), 1)
    starts = []
    for y in range(rows_y):
        start = encode(inflow_ref[y])
        start_ref[y] = start
        starts.append(start)
        before = same
        for j in range(size - 1):
            block = held[(mine ^ j) if power else (mine - j + size) % size, y]
            before = jnp.where(mine > j, block if j == 0 else join_blocks(before, block), before)
        for x in range(planes):
            at = x * rows_y + y
            label = label_ref[pl.ds(at, 1), :]
            data = data_ref[x, y]
            every = dot(full_ref[...], jnp.concatenate([data, data], axis=0))
            local = class_sum(every, label, nodes)
            on_wide = dot(label[:, :FACE].astype(BF16), wide).astype(jnp.int32)
            pick = jnp.where((row % FACE == lane % FACE) & (row // FACE == on_wide), 1.0, 0.0).astype(BF16)
            chosen = dot(coupling, pick).astype(BF16)
            local = local + carried([chosen], [before[FACE:]], nodes)[0]
            base_ref[x, y] = local
            first, second = block_diagonal(before[:FACE])
            products = dot_rows(chosen, first)
            products = products[:nodes] + products[nodes:] + dot_rows(chosen[:nodes], second)
            high, low = split(products)
            part_ref[y, pl.ds(x * nodes, nodes), :] = high
            part_ref[y, pl.ds((planes + x) * nodes, nodes), :] = low
            if x < planes - 1:
                offset = encode(flow_ref[x, :, y * columns:(y + 1) * columns])
                before = join_blocks(before, jnp.concatenate([lin_ref[x, y], offset], axis=0))

    @pl.when(place < size)
    def _():
        write_nodes(result_ref, out_ref, sems, base_ref, part_ref, [start_ref[y] for y in range(rows_y)])


def finish_kernel(size, inner, power, *refs):
    blocks = refs[:size]
    start_ref, base_ref, part_ref, _, out_ref, result_ref, sems = refs[size:size + 7]
    rows_y = base_ref.shape[1]
    mine = lax.axis_index("gx") // inner
    if power and size <= 4:
        for place in range(1, size):
            @pl.when(mine == place)
            def _():
                traces = []
                for y in range(rows_y):
                    trace = start_ref[y]
                    for j in range(place):
                        trace = advance(trace, blocks[place ^ j][y])
                    traces.append(trace)
                write_nodes(result_ref, out_ref, sems, base_ref, part_ref, traces)
    else:
        held = refs[size + 7]
        for s in range(size):
            held[s] = blocks[s][...]

        @pl.when(mine > 0)
        def _():
            traces = []
            for y in range(rows_y):
                trace = start_ref[y]
                for j in range(size - 1):
                    slot = (mine ^ j) if power else (mine - j + size) % size
                    trace = jnp.where(mine > j, advance(trace, held[slot, y]), trace)
                traces.append(trace)
            write_nodes(result_ref, out_ref, sems, base_ref, part_ref, traces)


def moved(value, pairs):
    return lax.ppermute(value, ("gx", "gy"), pairs)


def shape(dims, kind=F32):
    return jax.ShapeDtypeStruct(dims, kind)


def call(kernel, outs, name, args, scratch=(), space=pltpu.VMEM, out_spaces=None, aliases=None, limit=48):
    many = isinstance(outs, tuple)
    spaces = out_spaces or ((pltpu.VMEM,) * len(outs) if many else pltpu.VMEM)
    if isinstance(space, tuple):
        in_specs = [pl.BlockSpec(memory_space=one) for one in space]
    else:
        in_specs = [pl.BlockSpec(memory_space=space)] * len(args)
    if many:
        out_specs = tuple(pl.BlockSpec(memory_space=one) for one in spaces)
    else:
        out_specs = pl.BlockSpec(memory_space=spaces)
    return pl.pallas_call(
        kernel,
        out_shape=outs,
        in_specs=in_specs,
        out_specs=out_specs,
        scratch_shapes=list(scratch),
        input_output_aliases=aliases or {},
        name=name,
        cost_estimate=pl.CostEstimate(flops=1000000, bytes_accessed=500000, transcendentals=0),
        compiler_params=pltpu.CompilerParams(vmem_limit_bytes=limit * 1024 * 1024),
    )(*args)


def on_device(gx_size, gy_size, u_old, rhs, classes, flags, inverse, x_face, lateral_faces, inflow):
    planes, rows_y, nodes, columns = u_old.shape
    count = inverse.shape[0]
    everyone = [(x, y) for x in range(gx_size) for y in range(gy_size)]

    def at(x, y):
        return x * gy_size + y

    if gy_size == 2:
        below = above = moved(u_old, [(at(x, y), at(x, 1 - y)) for x, y in everyone])
    else:
        below = moved(u_old[:, rows_y - 1:], [(at(x, y), at(x, y + 1)) for x, y in everyone if y + 1 < gy_size])
        above = moved(u_old[:, :1], [(at(x, y), at(x, y - 1)) for x, y in everyone if y > 0])
    weights, out_rows, step, linear, labels = call(
        params_kernel,
        (
            shape((nodes, count * 256), BF16),
            shape((count * FACE, 256), BF16),
            shape((count * FACE, 128), BF16),
            shape((planes + 1, rows_y, FACE, 256)),
            shape((3 * planes * rows_y, columns)),
        ),
        "class_matrices",
        tuple(
            pltpu.with_memory_space_constraint(value, pltpu.HBM)
            for value in (inverse, x_face, lateral_faces, classes, flags)
        ),
        [
            pltpu.VMEM(inverse.shape, F32),
            pltpu.VMEM(x_face.shape, F32),
            pltpu.VMEM(lateral_faces.shape, F32),
            pltpu.VMEM(classes.shape, jnp.int32),
            pltpu.VMEM(flags.shape, jnp.int32),
            pltpu.SemaphoreType.DMA((5,)),
        ],
        space=pltpu.HBM,
    )
    data, flow, here = call(
        functools.partial(sources_kernel, gy_size),
        (
            shape((planes, rows_y, 128, columns), BF16),
            shape((planes, FACE, rows_y * columns)),
            shape((rows_y, 24, 256)),
        ),
        "sources",
        (u_old, rhs, below, above, labels, out_rows, step, linear),
    )
    inner = 4 if gx_size % 4 == 0 else 1
    outer = gx_size // inner
    power = outer & (outer - 1) == 0
    near = [here]
    for s in range(1, inner):
        near.append(moved(here, [(at(x, y), at(x ^ s, y)) for x, y in everyone]))
    total = call(
        functools.partial(group_kernel, inner, True),
        shape((rows_y, 24, 256)),
        "group_maps",
        tuple(near),
        [pltpu.VMEM((inner, rows_y, 24, 256), F32)],
    )
    blocks = [total]
    for s in range(1, outer):
        if power:
            pairs = [(at(x, y), at(x ^ (s * inner), y)) for x, y in everyone]
        else:
            pairs = [(at(x, y), at((x + s * inner) % gx_size, y)) for x, y in everyone]
        blocks.append(moved(total, pairs))
    nodes_shape = (planes, rows_y, nodes, columns)
    writing = [pltpu.VMEM(nodes_shape, F32), pltpu.SemaphoreType.DMA((planes, rows_y))]
    base, start, parts, out = call(
        functools.partial(solve_kernel, inner, True),
        (
            shape(nodes_shape),
            shape((rows_y, 8, 256)),
            shape((rows_y, 2 * planes * nodes, 256), BF16),
            pltpu.HBM(nodes_shape, F32),
        ),
        "local_solve",
        tuple(near) + (data, labels, weights, linear, flow, inverse, inflow),
        [pltpu.VMEM((inner, rows_y, 24, 256), F32), pltpu.VMEM((count * nodes, 256), BF16)] + writing,
        out_spaces=(pltpu.VMEM, pltpu.VMEM, pltpu.VMEM, pltpu.HBM),
    )
    held = [] if power and outer <= 4 else [pltpu.VMEM((outer, rows_y, 24, 256), F32)]
    args = tuple(blocks) + (start, base, parts, out)
    return call(
        functools.partial(finish_kernel, outer, inner, power),
        pltpu.HBM(nodes_shape, F32),
        "finish",
        args,
        writing + held,
        space=(pltpu.VMEM,) * (len(args) - 1) + (pltpu.HBM,),
        out_spaces=pltpu.HBM,
        aliases={len(args) - 1: 0},
    )


def solution(mesh):
    in_specs = (
        P("gx", "gy", None, None),
        P("gx", "gy", None, None),
        P("gx", "gy", None),
        P(None, "gx", "gy", None),
        P(),
        P(),
        P(),
        P("gy", None, None),
    )
    out_specs = P("gx", "gy", None, None)
    body = functools.partial(on_device, mesh.shape["gx"], mesh.shape["gy"])
    return jax.shard_map(body, mesh=mesh, in_specs=in_specs, out_specs=out_specs, check_vma=False)
```

```python
import functools

import jax
import jax.numpy as jnp
from jax import lax
from jax.experimental import pallas as pl
from jax.experimental.pallas import tpu as pltpu
from jax.sharding import PartitionSpec as P

FACE = 16
HIGH = lax.Precision.HIGHEST
F32 = jnp.float32
BF16 = jnp.bfloat16


def iota(shape, dim):
    return lax.broadcasted_iota(jnp.int32, shape, dim)


def exact(left, right):
    return jnp.dot(left, right, precision=HIGH, preferred_element_type=F32)


def split(value):
    high = value.astype(BF16)
    return high, (value - high.astype(F32)).astype(BF16)


def wanted_node(face, item):
    high, low = item // 4, item % 4
    return jnp.where(face < 2, 16 * high + low + 12 * (face == 1), 16 * high + 4 * low + 3 * (face == 3))


def dot(left, right):
    return jnp.dot(left, right, preferred_element_type=F32)


def dot_rows(left, right):
    return lax.dot_general(left, right, (((1,), (1,)), ((), ())), preferred_element_type=F32)


def applied(rows, linear):
    lane = iota((rows.shape[0], 128), 1)
    halves = []
    for begin in (0, 128):
        part, total = rows[:, begin:begin + 128], None
        for b in range(FACE):
            near = jnp.take_along_axis(part, lane // FACE * FACE + b, axis=1, mode="promise_in_bounds")
            term = near * linear[b:b + 1, begin:begin + 128]
            total = term if total is None else total + term
        halves.append(total)
    return jnp.concatenate(halves, axis=1)


def join(earlier, later):
    moved_rows = applied(earlier, later[:FACE])
    return jnp.concatenate([moved_rows[:FACE], moved_rows[FACE:] + later[FACE:]], axis=0)


def advance(trace, later):
    return applied(trace, later[:FACE]) + later[FACE:]


def encode(value):
    high, low = split(value)
    both = jnp.concatenate([high, low], axis=1)
    tile = (iota((256, FACE), 0) % FACE == iota((256, FACE), 1)).astype(BF16)
    spread = dot(tile, both)
    keep = iota((256, 256), 0) // FACE == iota((256, 256), 1) % FACE
    spread = jnp.where(keep, spread, 0.0).astype(BF16)
    gather = (iota((8, 256), 1) % 128 // FACE == iota((8, 256), 0)).astype(BF16)
    return dot_rows(gather, spread)


def face_columns(inv_rows, nodes):
    at = iota((nodes, 5 * FACE), 1)
    wanted = jnp.where(at < 64, wanted_node(at // FACE, at % FACE), at - 64)
    chosen = (iota((nodes, 5 * FACE), 0) == wanted).astype(BF16)
    return dot(jnp.concatenate(split(inv_rows), axis=0), chosen).astype(BF16)


def class_products(high, low, weights):
    count = high.shape[0]
    parts = dot(jnp.concatenate([high, low], axis=0), weights)
    return -(parts[:count, :128] + parts[:count, 128:] + parts[count:, :128])


def with_inverse(inv_rows, products):
    count = inv_rows.shape[0]
    wide = jnp.concatenate([inv_rows, jnp.zeros((count, 128 - inv_rows.shape[1]), F32)], axis=1)
    return jnp.where(iota((count, 128), 1) < 64, wide, products)


def in_parts(value):
    high, low = split(value)
    return jnp.concatenate([high, low], axis=1)


def coupling_parts(products):
    high, low = split(products)
    lane = iota(products.shape, 1)
    return jnp.where(lane < 32, high.astype(F32), jnp.where(lane < 48, low.astype(F32), 0.0)).astype(BF16)


def params_kernel(cls_hbm, flag_hbm, x_hbm, lat_hbm, inv_hbm, weight_ref, out_ref, step_ref, label_ref,
                  cls_ref, flag_ref, x_ref, lat_ref, inv_ref, sems):
    pairs = ((cls_hbm, cls_ref), (flag_hbm, flag_ref), (x_hbm, x_ref), (lat_hbm, lat_ref), (inv_hbm, inv_ref))
    copies = [pltpu.make_async_copy(a, b, sems.at[i]) for i, (a, b) in enumerate(pairs)]
    for copy in copies:
        copy.start()
    count, nodes, _ = inv_ref.shape
    planes = cls_ref.shape[0]
    item, lane = iota((FACE, 128), 0), iota((FACE, 128), 1)
    places = [(lane == 64 + FACE * f + item).astype(BF16) for f in range(4)]
    places.append(((lane < 48) & (lane % FACE == item)).astype(BF16))
    for copy in copies[:2]:
        copy.wait()
    labels = [cls_ref[x] for x in range(planes)]
    labels += [flag_ref[d, x] for d in range(2) for x in range(planes)]
    labels = jnp.concatenate(labels, axis=0).astype(F32).astype(BF16)
    tile = (iota((FACE, 128), 1) % FACE == iota((FACE, 128), 0)).astype(BF16)
    label_ref[...] = dot(labels, tile)
    for copy in copies[2:]:
        copy.wait()
    placed = []
    for f in range(5):
        rows = (lat_ref[f] if f < 4 else x_ref[...]).reshape(count * FACE, FACE)
        placed.append(dot(jnp.concatenate(split(rows), axis=0), places[f]).astype(BF16))
    inv_rows = [inv_ref[k, nodes - FACE:, :] for k in range(count)]
    gathered = face_columns(jnp.concatenate(inv_rows, axis=0), nodes)
    outs, steps = [], []
    for k in range(count):
        columns = []
        for part in range(2):
            begin = part * count * FACE + k * FACE
            columns.append(jnp.concatenate([p[begin:begin + FACE] for p in placed], axis=0))
        weights = jnp.concatenate(columns, axis=1)
        weight_ref[:, 256 * k:256 * k + 256] = weights
        low = (count + k) * FACE
        products = class_products(gathered[k * FACE:k * FACE + FACE], gathered[low:low + FACE], weights)
        outs.append(with_inverse(inv_rows[k], products))
        steps.append(products)
    out_ref[...] = in_parts(jnp.concatenate(outs, axis=0))
    step_ref[...] = coupling_parts(jnp.concatenate(steps, axis=0))


def picked(label, count):
    wide = (iota((FACE, 256), 1) // FACE == iota((FACE, 256), 0)).astype(BF16)
    on_wide = dot(label[:, :FACE].astype(BF16), wide).astype(jnp.int32)
    row, lane = iota((count * FACE, 256), 0), iota((count * FACE, 256), 1)
    return jnp.where((row % FACE == lane % FACE) & (row // FACE == on_wide), 1.0, 0.0).astype(BF16)


def class_sum(every, label, rows):
    total = None
    for k in range(8):
        term = jnp.where(label == k, every[k * rows:(k + 1) * rows], 0.0)
        total = term if total is None else total + term
    return total


def stacked(value):
    first, second = split(value)
    rest = jnp.zeros((128 - 3 * FACE, value.shape[1]), BF16)
    return jnp.concatenate([first, second, first, rest], axis=0)


def sources_kernel(gy_size, u_ref, rhs_ref, below_ref, above_ref, label_ref, out_ref, step_ref, x_ref, flow_ref, lin_ref, map_ref):
    planes, rows_y, nodes, columns = u_ref.shape
    place = lax.axis_index("gy")
    node, item = iota((nodes, nodes), 1), iota((nodes, nodes), 0)
    chosen = (node == wanted_node(item // FACE, item % FACE)).astype(BF16)
    own = [u_ref[x, y] for x in range(planes) for y in range(rows_y)]
    other = [below_ref[x, below_ref.shape[1] - 1] for x in range(planes)] + [above_ref[x, 0] for x in range(planes)]
    step = step_ref[...]
    row, lane = iota((2 * FACE, 128), 0), iota((2 * FACE, 128), 1)
    flip = (lane == row + FACE * (row >= FACE)).astype(BF16)
    turned = dot_rows(flip, step).astype(BF16)
    faces = dot(chosen, jnp.concatenate(own + other, axis=1))
    picks = []
    for at in range(planes * rows_y):
        picks.append(picked(label_ref[pl.ds(at, 1), :], step.shape[0] // FACE))
    linear = dot(turned, jnp.concatenate(picks, axis=1))
    faces = [faces[:, i * columns:(i + 1) * columns] for i in range(len(own) + len(other))]
    z_at = iota((FACE, columns), 1) % FACE
    has_below = jnp.where(place > 0, 1.0, 0.0)
    has_above = jnp.where(place < gy_size - 1, 1.0, 0.0)
    data = []
    for x in range(planes):
        under = faces[len(own) + x][16:32] * has_below
        over = faces[len(own) + planes + x][0:16] * has_above
        for y in range(rows_y):
            at = x * rows_y + y
            y_flag = label_ref[pl.ds(planes * rows_y + at, 1), :]
            z_flag = label_ref[pl.ds(2 * planes * rows_y + at, 1), :]
            from_below = faces[at - 1][16:32] if y > 0 else under
            from_above = faces[at + 1][0:16] if y < rows_y - 1 else over
            from_front = jnp.where(z_at == 0, 0.0, pltpu.roll(faces[at][48:64], 1, 1))
            from_back = jnp.where(z_at == FACE - 1, 0.0, pltpu.roll(faces[at][32:48], columns - 1, 1))
            lateral = jnp.concatenate(
                [
                    from_below * (1.0 - y_flag),
                    from_above * y_flag,
                    from_front * (1.0 - z_flag),
                    from_back * z_flag,
                ],
                axis=0,
            ).astype(BF16)
            here = jnp.concatenate([rhs_ref[x, y], lateral], axis=0)
            x_ref[x, y] = here
            data.append(here)
    data = jnp.concatenate(data, axis=1)
    every = dot(out_ref[...], jnp.concatenate([data, data], axis=0))
    keep = (iota((256, 256), 0) // FACE == iota((256, 256), 1) // FACE).astype(BF16)
    wholes = []
    for at in range(planes * rows_y):
        here = linear[:, at * 256:at * 256 + 256]
        lin_ref[at // rows_y, at % rows_y] = here[:FACE] + here[FACE:]
        both = here.astype(BF16)
        if at < rows_y:
            wholes.append((here[:FACE] + here[FACE:], both))
        else:
            pair = wholes[at % rows_y][1]
            first, second = [jnp.concatenate([part] * 16, axis=0) * keep for part in (both[:FACE], both[FACE:])]
            parts = dot(pair, first)
            whole = parts[:FACE] + parts[FACE:] + dot(pair[:FACE], second)
            if at < (planes - 1) * rows_y:
                both = jnp.concatenate(split(whole), axis=0)
            wholes[at % rows_y] = (whole, both)
    total = None
    for x in range(planes):
        begin = x * rows_y * columns
        label = jnp.concatenate([label_ref[pl.ds(x * rows_y + y, 1), :] for y in range(rows_y)], axis=1)
        flow = class_sum(every[:, begin:begin + rows_y * columns], label, FACE)
        flow_ref[x] = flow
        if total is not None:
            flow = flow + class_sum(dot(step_ref[...], stacked(total)), label, FACE)
        total = flow
    for y in range(rows_y):
        map_ref[y, 0:FACE] = wholes[y][0]
        map_ref[y, FACE:] = encode(total[:, y * columns:(y + 1) * columns])


def block_diagonal(linear):
    keep = (iota((256, 256), 0) // FACE == iota((256, 256), 1) // FACE).astype(BF16)
    return [jnp.concatenate([part] * 16, axis=0) * keep for part in split(linear)]


def join_many(pairs):
    ready = []
    for earlier, later in pairs:
        halves = split(jnp.concatenate([earlier, jnp.zeros((8, 256), F32)], axis=0))
        ready.append((halves[0], jnp.concatenate(halves, axis=0), block_diagonal(later[:FACE])))
    firsts = [dot(both, blocks[0]) for _, both, blocks in ready]
    seconds = [dot(high, blocks[1]) for high, _, blocks in ready]
    joined = []
    for parts, more, (_, later) in zip(firsts, seconds, pairs):
        total = (parts[:32] + parts[32:] + more)[:24]
        joined.append(jnp.concatenate([total[:FACE], total[FACE:] + later[FACE:]], axis=0))
    return joined


def block_slot(mine, other, size, power):
    step = (mine ^ other) if power else (mine - other + size) % size
    return (size - step) % size


def group_kernel(size, power, outer, *refs):
    blocks, total_ref, held = refs[:size], refs[size + 1], refs[size + 2]
    place = lax.axis_index("gx")
    mine = place % size
    rows_y = total_ref.shape[0]

    @pl.when(place // size < outer - 1)
    def _():
        for s in range(size):
            held[s] = blocks[s][...]
        slots = [block_slot(mine, j, size, power) for j in range(size)]
        maps = [[held[slot, y] for slot in slots] for y in range(rows_y)]
        while len(maps[0]) > 1:
            length = len(maps[0])
            joined = join_many([(maps[y][i], maps[y][i + 1]) for y in range(rows_y) for i in range(0, length - 1, 2)])
            half = length // 2
            maps = [joined[y * half:y * half + half] + maps[y][2 * half:] for y in range(rows_y)]
        for y in range(rows_y):
            total_ref[y] = maps[y][0]

    @pl.when(place // size == outer - 1)
    def _():
        total_ref[...] = jnp.zeros(total_ref.shape, F32)


def carried(parts, traces, count):
    first, second = split(jnp.concatenate(traces, axis=1))
    row, lane = iota((256, 2 * FACE), 0), iota((256, 2 * FACE), 1)
    spread = (lane == row % 128 // FACE + FACE * (row >= 128)).astype(BF16)
    rest = jnp.zeros((8, first.shape[1]), BF16)
    rows = dot(spread, jnp.concatenate([first, rest, second, rest], axis=0))
    keep = iota((256, 256), 0) % FACE == iota((256, 256), 1) // FACE
    here = [jnp.where(keep, rows[:, y * 256:y * 256 + 256], 0.0).astype(BF16) for y in range(len(parts))]
    by_first = [dot_rows(part, data[:128]) for part, data in zip(parts, here)]
    by_second = [dot_rows(part[:count], data[128:]) for part, data in zip(parts, here)]
    return [first[:count] + first[count:] + second for first, second in zip(by_first, by_second)]


def write_nodes(result_ref, out_ref, sems, base_ref, part_ref, traces):
    planes, rows_y, nodes, _ = result_ref.shape
    sums = carried([part_ref[y] for y in range(rows_y)], traces, planes * nodes)
    copies = []
    for y in range(rows_y):
        for x in range(planes):
            result_ref[x, y] = base_ref[x, y] + sums[y][x * nodes:(x + 1) * nodes]
            copies.append(pltpu.make_async_copy(result_ref.at[x, y], out_ref.at[x, y], sems.at[x, y]))
            copies[-1].start()
    for copy in copies:
        copy.wait()


def local_kernel(data_ref, label_ref, weight_ref, flow_ref, inv_ref, inflow_ref, base_ref, start_ref, chosen_ref, offset_ref, full_ref):
    planes, rows_y, nodes, columns = base_ref.shape
    coupling = jnp.zeros((nodes, 128), F32)
    count = inv_ref.shape[0]
    gathered = face_columns(inv_ref[...].reshape(count * nodes, nodes), nodes)
    for k in range(count):
        inv_rows = inv_ref[k]
        low = (count + k) * nodes
        products = class_products(
            gathered[k * nodes:k * nodes + nodes], gathered[low:low + nodes], weight_ref[:, 256 * k:256 * k + 256]
        )
        here = pl.ds(k * nodes, nodes)
        shifted = pltpu.roll(products, FACE * k, 1) if k else products
        coupling = jnp.where(iota((nodes, 128), 1) // FACE == k, shifted, coupling)
        full_ref[here, :] = in_parts(with_inverse(inv_rows, products))
    coupling = jnp.concatenate(split(coupling), axis=0)
    for y in range(rows_y):
        start_ref[y] = encode(inflow_ref[y])
    for x in range(planes):
        for y in range(rows_y):
            label = label_ref[pl.ds(x * rows_y + y, 1), :]
            data = data_ref[x, y]
            every = dot(full_ref[...], jnp.concatenate([data, data], axis=0))
            base_ref[x, y] = class_sum(every, label, nodes)
            chosen_ref[x, y] = dot(coupling, picked(label, count)).astype(BF16)
            if x < planes - 1:
                offset_ref[x, y] = encode(flow_ref[x, :, y * columns:(y + 1) * columns])


def carry_kernel(size, power, *refs):
    blocks = refs[:size]
    local_ref, start_ref, chosen_ref, offset_ref, lin_ref = refs[size:size + 5]
    base_ref, part_ref, out_ref, held, result_ref, sems = refs[size + 5:]
    planes, rows_y, nodes, _ = base_ref.shape
    for s in range(size):
        held[s] = blocks[s][...]
    place = lax.axis_index("gx")
    mine = place % size
    same = (iota((24, 256), 1) % FACE == iota((24, 256), 0)).astype(F32)
    ahead = [same] * rows_y
    for j in range(size - 1):
        slot = block_slot(mine, j, size, power)
        block = [held[slot, y] for y in range(rows_y)]
        joined = block if j == 0 else join_many([(ahead[y], block[y]) for y in range(rows_y)])
        ahead = [jnp.where(mine > j, joined[y], ahead[y]) for y in range(rows_y)]
    for x in range(planes):
        chosen = [chosen_ref[x, y] for y in range(rows_y)]
        sums = carried(chosen, [ahead[y][FACE:] for y in range(rows_y)], nodes)
        pairs = [block_diagonal(ahead[y][:FACE]) for y in range(rows_y)]
        firsts = [dot_rows(chosen[y], pairs[y][0]) for y in range(rows_y)]
        seconds = [dot_rows(chosen[y][:nodes], pairs[y][1]) for y in range(rows_y)]
        for y in range(rows_y):
            base_ref[x, y] = local_ref[x, y] + sums[y]
            high, low = split(firsts[y][:nodes] + firsts[y][nodes:] + seconds[y])
            part_ref[y, pl.ds(x * nodes, nodes), :] = high
            part_ref[y, pl.ds((planes + x) * nodes, nodes), :] = low
        if x < planes - 1:
            own = [jnp.concatenate([lin_ref[x, y], offset_ref[x, y]], axis=0) for y in range(rows_y)]
            ahead = join_many([(ahead[y], own[y]) for y in range(rows_y)])

    @pl.when(place < size)
    def _():
        write_nodes(result_ref, out_ref, sems, base_ref, part_ref, [start_ref[y] for y in range(rows_y)])


def finish_kernel(size, inner, power, *refs):
    blocks = refs[:size]
    start_ref, base_ref, part_ref, _, out_ref, result_ref, sems = refs[size:size + 7]
    rows_y = base_ref.shape[1]
    mine = lax.axis_index("gx") // inner
    if power and size <= 4:
        for place in range(1, size):
            @pl.when(mine == place)
            def _():
                traces = [start_ref[y] for y in range(rows_y)]
                for j in range(place):
                    traces = [advance(traces[y], blocks[block_slot(place, j, size, power)][y]) for y in range(rows_y)]
                write_nodes(result_ref, out_ref, sems, base_ref, part_ref, traces)
    else:
        held = refs[size + 7]
        for s in range(size):
            held[s] = blocks[s][...]

        @pl.when(mine > 0)
        def _():
            traces = []
            for y in range(rows_y):
                trace = start_ref[y]
                for j in range(size - 1):
                    slot = block_slot(mine, j, size, power)
                    trace = jnp.where(mine > j, advance(trace, held[slot, y]), trace)
                traces.append(trace)
            write_nodes(result_ref, out_ref, sems, base_ref, part_ref, traces)


def moved(value, pairs):
    return lax.ppermute(value, ("gx", "gy"), pairs)


def shape(dims, kind=F32):
    return jax.ShapeDtypeStruct(dims, kind)


def call(kernel, outs, name, args, scratch=(), space=pltpu.VMEM, out_spaces=None, aliases=None, limit=48):
    many = isinstance(outs, tuple)
    spaces = out_spaces or ((pltpu.VMEM,) * len(outs) if many else pltpu.VMEM)
    if isinstance(space, tuple):
        in_specs = [pl.BlockSpec(memory_space=one) for one in space]
    else:
        in_specs = [pl.BlockSpec(memory_space=space)] * len(args)
    if many:
        out_specs = tuple(pl.BlockSpec(memory_space=one) for one in spaces)
    else:
        out_specs = pl.BlockSpec(memory_space=spaces)
    return pl.pallas_call(
        kernel,
        out_shape=outs,
        in_specs=in_specs,
        out_specs=out_specs,
        scratch_shapes=list(scratch),
        input_output_aliases=aliases or {},
        name=name,
        cost_estimate=pl.CostEstimate(flops=1000000, bytes_accessed=500000, transcendentals=0),
        compiler_params=pltpu.CompilerParams(vmem_limit_bytes=limit * 1024 * 1024),
    )(*args)


def on_device(gx_size, gy_size, u_old, rhs, classes, flags, inverse, x_face, lateral_faces, inflow):
    planes, rows_y, nodes, columns = u_old.shape
    count = inverse.shape[0]
    everyone = [(x, y) for x in range(gx_size) for y in range(gy_size)]

    def at(x, y):
        return x * gy_size + y

    if gy_size == 2:
        below = above = moved(u_old, [(at(x, y), at(x, 1 - y)) for x, y in everyone])
    else:
        below = moved(u_old[:, rows_y - 1:], [(at(x, y), at(x, y + 1)) for x, y in everyone if y + 1 < gy_size])
        above = moved(u_old[:, :1], [(at(x, y), at(x, y - 1)) for x, y in everyone if y > 0])
    weights, out_rows, step, labels = call(
        params_kernel,
        (
            shape((5 * FACE, count * 256), BF16),
            shape((count * FACE, 256), BF16),
            shape((count * FACE, 128), BF16),
            shape((3 * planes * rows_y, columns)),
        ),
        "class_matrices",
        tuple(
            pltpu.with_memory_space_constraint(value, pltpu.HBM)
            for value in (classes, flags, x_face, lateral_faces, inverse)
        ),
        [
            pltpu.VMEM(classes.shape, jnp.int32),
            pltpu.VMEM(flags.shape, jnp.int32),
            pltpu.VMEM(x_face.shape, F32),
            pltpu.VMEM(lateral_faces.shape, F32),
            pltpu.VMEM(inverse.shape, F32),
            pltpu.SemaphoreType.DMA((5,)),
        ],
        space=pltpu.HBM,
    )
    data, flow, linear, here = call(
        functools.partial(sources_kernel, gy_size),
        (
            shape((planes, rows_y, 128, columns), BF16),
            shape((planes, FACE, rows_y * columns)),
            shape((planes, rows_y, FACE, 256)),
            shape((rows_y, 24, 256)),
        ),
        "sources",
        (u_old, rhs, below, above, labels, out_rows, step),
    )
    inner = 4 if gx_size % 4 == 0 else 1
    outer = gx_size // inner
    power = outer & (outer - 1) == 0
    near = [here]
    for s in range(inner - 1, 0, -1):
        near.append(moved(here, [(at(x, y), at(x ^ s, y)) for x, y in everyone]))
    nodes_shape = (planes, rows_y, nodes, columns)
    writing = [pltpu.VMEM(nodes_shape, F32), pltpu.SemaphoreType.DMA((planes, rows_y))]
    local, start, chosen, offsets = call(
        local_kernel,
        (
            shape(nodes_shape),
            shape((rows_y, 8, 256)),
            shape((planes, rows_y, 2 * nodes, 256), BF16),
            shape((max(planes - 1, 1), rows_y, 8, 256)),
        ),
        "local_solve",
        (data, labels, weights, flow, inverse, inflow),
        [pltpu.VMEM((count * nodes, 256), BF16)],
    )
    total = call(
        functools.partial(group_kernel, inner, True, outer),
        shape((rows_y, 24, 256)),
        "group_maps",
        tuple(near) + (start,),
        [pltpu.VMEM((inner, rows_y, 24, 256), F32)],
    )
    blocks = [total]
    for s in range(outer - 1, 0, -1):
        if power:
            pairs = [(at(x, y), at(x ^ (s * inner), y)) for x, y in everyone]
        else:
            pairs = [(at(x, y), at((x + s * inner) % gx_size, y)) for x, y in everyone]
        blocks.append(moved(total, pairs))
    base, parts, out = call(
        functools.partial(carry_kernel, inner, True),
        (
            shape(nodes_shape),
            shape((rows_y, 2 * planes * nodes, 256), BF16),
            pltpu.HBM(nodes_shape, F32),
        ),
        "carry_maps",
        tuple(near) + (local, start, chosen, offsets, linear),
        [pltpu.VMEM((inner, rows_y, 24, 256), F32)] + writing,
        out_spaces=(pltpu.VMEM, pltpu.VMEM, pltpu.HBM),
    )
    held = [] if power and outer <= 4 else [pltpu.VMEM((outer, rows_y, 24, 256), F32)]
    args = tuple(blocks) + (start, base, parts, out)
    return call(
        functools.partial(finish_kernel, outer, inner, power),
        pltpu.HBM(nodes_shape, F32),
        "finish",
        args,
        writing + held,
        space=(pltpu.VMEM,) * (len(args) - 1) + (pltpu.HBM,),
        out_spaces=pltpu.HBM,
        aliases={len(args) - 1: 0},
    )


def solution(mesh):
    in_specs = (
        P("gx", "gy", None, None),
        P("gx", "gy", None, None),
        P("gx", "gy", None),
        P(None, "gx", "gy", None),
        P(),
        P(),
        P(),
        P("gy", None, None),
    )
    out_specs = P("gx", "gy", None, None)
    body = functools.partial(on_device, mesh.shape["gx"], mesh.shape["gy"])
    return jax.shard_map(body, mesh=mesh, in_specs=in_specs, out_specs=out_specs, check_vma=False)
```

```python
import functools

import jax
import jax.numpy as jnp
from jax import lax
from jax.experimental import pallas as pl
from jax.experimental.pallas import tpu as pltpu
from jax.sharding import PartitionSpec as P

FACE = 16
HIGH = lax.Precision.HIGHEST
F32 = jnp.float32
BF16 = jnp.bfloat16


def iota(shape, dim):
    return lax.broadcasted_iota(jnp.int32, shape, dim)


def exact(left, right):
    return jnp.dot(left, right, precision=HIGH, preferred_element_type=F32)


def split(value):
    high = value.astype(BF16)
    return high, (value - high.astype(F32)).astype(BF16)


def wanted_node(face, item):
    high, low = item // 4, item % 4
    return jnp.where(face < 2, 16 * high + low + 12 * (face == 1), 16 * high + 4 * low + 3 * (face == 3))


def dot(left, right):
    return jnp.dot(left, right, preferred_element_type=F32)


def dot_rows(left, right):
    return lax.dot_general(left, right, (((1,), (1,)), ((), ())), preferred_element_type=F32)


def applied(rows, linear):
    lane = iota((rows.shape[0], 128), 1)
    halves = []
    for begin in (0, 128):
        part, total = rows[:, begin:begin + 128], None
        for b in range(FACE):
            near = jnp.take_along_axis(part, lane // FACE * FACE + b, axis=1, mode="promise_in_bounds")
            term = near * linear[b:b + 1, begin:begin + 128]
            total = term if total is None else total + term
        halves.append(total)
    return jnp.concatenate(halves, axis=1)


def join(earlier, later):
    moved_rows = applied(earlier, later[:FACE])
    return jnp.concatenate([moved_rows[:FACE], moved_rows[FACE:] + later[FACE:]], axis=0)


def advance(trace, later):
    return applied(trace, later[:FACE]) + later[FACE:]


def encode(value):
    keep = (iota((256, 128), 0) // FACE == iota((256, 128), 1) % FACE).astype(BF16)
    spread = [jnp.concatenate([part] * 16, axis=0) * keep for part in split(value)]
    gather = (iota((8, 256), 1) % 128 // FACE == iota((8, 256), 0)).astype(BF16)
    return dot_rows(gather, jnp.concatenate(spread, axis=1))


def face_columns(inv_rows, nodes):
    at = iota((nodes, 5 * FACE), 1)
    wanted = jnp.where(at < 64, wanted_node(at // FACE, at % FACE), at - 64)
    chosen = (iota((nodes, 5 * FACE), 0) == wanted).astype(BF16)
    return dot(jnp.concatenate(split(inv_rows), axis=0), chosen).astype(BF16)


def class_products(high, low, weights):
    count = high.shape[0]
    parts = dot(jnp.concatenate([high, low], axis=0), weights)
    return -(parts[:count, :128] + parts[:count, 128:] + parts[count:, :128])


def with_inverse(inv_rows, products):
    count = inv_rows.shape[0]
    wide = jnp.concatenate([inv_rows, jnp.zeros((count, 128 - inv_rows.shape[1]), F32)], axis=1)
    return jnp.where(iota((count, 128), 1) < 64, wide, products)


def in_parts(value):
    high, low = split(value)
    return jnp.concatenate([high, low], axis=1)


def coupling_parts(products):
    high, low = split(products)
    lane = iota(products.shape, 1)
    return jnp.where(lane < 32, high.astype(F32), jnp.where(lane < 48, low.astype(F32), 0.0)).astype(BF16)


def params_kernel(cls_hbm, flag_hbm, x_hbm, lat_hbm, inv_hbm, weight_ref, out_ref, step_ref, label_ref,
                  cls_ref, flag_ref, x_ref, lat_ref, inv_ref, sems):
    pairs = ((cls_hbm, cls_ref), (flag_hbm, flag_ref), (x_hbm, x_ref), (lat_hbm, lat_ref))
    pairs += ((inv_hbm.at[:, inv_hbm.shape[1] - FACE:, :], inv_ref),)
    copies = [pltpu.make_async_copy(a, b, sems.at[i]) for i, (a, b) in enumerate(pairs)]
    for copy in copies:
        copy.start()
    count, nodes, _ = inv_hbm.shape
    planes = cls_ref.shape[0]
    item, lane = iota((FACE, 128), 0), iota((FACE, 128), 1)
    places = [(lane == 64 + FACE * f + item).astype(BF16) for f in range(4)]
    places.append(((lane < 48) & (lane % FACE == item)).astype(BF16))
    for copy in copies[:2]:
        copy.wait()
    labels = [cls_ref[x] for x in range(planes)]
    labels += [flag_ref[d, x] for d in range(2) for x in range(planes)]
    labels = jnp.concatenate(labels, axis=0).astype(F32).astype(BF16)
    tile = (iota((FACE, 128), 1) % FACE == iota((FACE, 128), 0)).astype(BF16)
    label_ref[...] = dot(labels, tile)
    for copy in copies[2:]:
        copy.wait()
    placed = []
    for f in range(5):
        rows = (lat_ref[f] if f < 4 else x_ref[...]).reshape(count * FACE, FACE)
        placed.append(dot(jnp.concatenate(split(rows), axis=0), places[f]).astype(BF16))
    inv_rows = [inv_ref[k] for k in range(count)]
    gathered = face_columns(jnp.concatenate(inv_rows, axis=0), nodes)
    outs, steps = [], []
    for k in range(count):
        columns = []
        for part in range(2):
            begin = part * count * FACE + k * FACE
            columns.append(jnp.concatenate([p[begin:begin + FACE] for p in placed], axis=0))
        weights = jnp.concatenate(columns, axis=1)
        weight_ref[:, 256 * k:256 * k + 256] = weights
        low = (count + k) * FACE
        products = class_products(gathered[k * FACE:k * FACE + FACE], gathered[low:low + FACE], weights)
        outs.append(with_inverse(inv_rows[k], products))
        steps.append(products)
    out_ref[...] = in_parts(jnp.concatenate(outs, axis=0))
    step_ref[...] = coupling_parts(jnp.concatenate(steps, axis=0))


def picked(label, count):
    wide = (iota((FACE, 256), 1) // FACE == iota((FACE, 256), 0)).astype(BF16)
    on_wide = dot(label[:, :FACE].astype(BF16), wide).astype(jnp.int32)
    row, lane = iota((count * FACE, 256), 0), iota((count * FACE, 256), 1)
    return jnp.where((row % FACE == lane % FACE) & (row // FACE == on_wide), 1.0, 0.0).astype(BF16)


def class_sum(every, label, rows):
    total = None
    for k in range(8):
        term = jnp.where(label == k, every[k * rows:(k + 1) * rows], 0.0)
        total = term if total is None else total + term
    return total


def stacked(value):
    first, second = split(value)
    rest = jnp.zeros((128 - 3 * FACE, value.shape[1]), BF16)
    return jnp.concatenate([first, second, first, rest], axis=0)


def sources_kernel(gy_size, u_ref, rhs_ref, below_ref, above_ref, label_ref, out_ref, step_ref, x_ref, flow_ref, lin_ref, map_ref):
    planes, rows_y, nodes, columns = u_ref.shape
    place = lax.axis_index("gy")
    node, item = iota((nodes, nodes), 1), iota((nodes, nodes), 0)
    chosen = (node == wanted_node(item // FACE, item % FACE)).astype(BF16)
    own = [u_ref[x, y] for x in range(planes) for y in range(rows_y)]
    other = [below_ref[x, below_ref.shape[1] - 1] for x in range(planes)] + [above_ref[x, 0] for x in range(planes)]
    step = step_ref[...]
    row, lane = iota((2 * FACE, 128), 0), iota((2 * FACE, 128), 1)
    flip = (lane == row + FACE * (row >= FACE)).astype(BF16)
    turned = dot_rows(flip, step).astype(BF16)
    faces = dot(chosen, jnp.concatenate(own + other, axis=1))
    picks = []
    for at in range(planes * rows_y):
        picks.append(picked(label_ref[pl.ds(at, 1), :], step.shape[0] // FACE))
    linear = dot(turned, jnp.concatenate(picks, axis=1))
    faces = [faces[:, i * columns:(i + 1) * columns] for i in range(len(own) + len(other))]
    z_at = iota((FACE, columns), 1) % FACE
    has_below = jnp.where(place > 0, 1.0, 0.0)
    has_above = jnp.where(place < gy_size - 1, 1.0, 0.0)
    data = []
    for x in range(planes):
        under = faces[len(own) + x][16:32] * has_below
        over = faces[len(own) + planes + x][0:16] * has_above
        for y in range(rows_y):
            at = x * rows_y + y
            y_flag = label_ref[pl.ds(planes * rows_y + at, 1), :]
            z_flag = label_ref[pl.ds(2 * planes * rows_y + at, 1), :]
            from_below = faces[at - 1][16:32] if y > 0 else under
            from_above = faces[at + 1][0:16] if y < rows_y - 1 else over
            from_front = jnp.where(z_at == 0, 0.0, pltpu.roll(faces[at][48:64], 1, 1))
            from_back = jnp.where(z_at == FACE - 1, 0.0, pltpu.roll(faces[at][32:48], columns - 1, 1))
            lateral = jnp.concatenate(
                [
                    from_below * (1.0 - y_flag),
                    from_above * y_flag,
                    from_front * (1.0 - z_flag),
                    from_back * z_flag,
                ],
                axis=0,
            ).astype(BF16)
            here = jnp.concatenate([rhs_ref[x, y], lateral], axis=0)
            x_ref[x, y] = here
            data.append(here)
    data = jnp.concatenate(data, axis=1)
    every = dot(out_ref[...], jnp.concatenate([data, data], axis=0))
    keep = (iota((256, 256), 0) // FACE == iota((256, 256), 1) // FACE).astype(BF16)
    wholes, pairs = None, None
    for x in range(planes):
        here = [linear[:, at * 256:at * 256 + 256] for at in range(x * rows_y, (x + 1) * rows_y)]
        both = [(part[:FACE].astype(BF16), part[FACE:].astype(BF16)) for part in here]
        for y in range(rows_y):
            lin_ref[x, y] = here[y][:FACE] + here[y][FACE:]
        if wholes is None:
            wholes, pairs = [part[:FACE] + part[FACE:] for part in here], both
        else:
            blocks = [[jnp.concatenate([part] * 16, axis=0) * keep for part in parts] for parts in both]
            stacks = [jnp.concatenate(pair, axis=0) for pair in pairs]
            firsts = [dot(stack, block[0]) for stack, block in zip(stacks, blocks)]
            seconds = [dot(pair[0], block[1]) for pair, block in zip(pairs, blocks)]
            wholes = [first[:FACE] + first[FACE:] + second for first, second in zip(firsts, seconds)]
            pairs = [split(whole) for whole in wholes]
    total = None
    for x in range(planes):
        begin = x * rows_y * columns
        label = jnp.concatenate([label_ref[pl.ds(x * rows_y + y, 1), :] for y in range(rows_y)], axis=1)
        flow = class_sum(every[:, begin:begin + rows_y * columns], label, FACE)
        flow_ref[x] = flow
        if total is not None:
            flow = flow + class_sum(dot(step_ref[...], stacked(total)), label, FACE)
        total = flow
    for y in range(rows_y):
        map_ref[y, 0:FACE] = wholes[y]
        map_ref[y, FACE:] = encode(total[:, y * columns:(y + 1) * columns])


def block_diagonal(linear):
    keep = (iota((256, 256), 0) // FACE == iota((256, 256), 1) // FACE).astype(BF16)
    return [jnp.concatenate([part] * 16, axis=0) * keep for part in split(linear)]


def half_weights(high, low, begin):
    keep = (iota((128, 128), 0) // FACE == iota((128, 128), 1) // FACE).astype(BF16)
    parts = [jnp.concatenate([part[:, begin:begin + 128]] * 8, axis=0) * keep for part in (high, low)]
    return jnp.concatenate(parts, axis=0)


def half_rows(high, low, begin):
    high, low = high[:, begin:begin + 128], low[:, begin:begin + 128]
    upper = jnp.concatenate([high, high], axis=1)
    return jnp.concatenate([upper, jnp.concatenate([low, jnp.zeros_like(low)], axis=1)], axis=0)


def joined_rows(pairs):
    ready = [
        (half_rows(*rows, begin), half_weights(*linear, begin)) for rows, linear in pairs for begin in (0, 128)
    ]
    sums = [dot(rows, weights) for rows, weights in ready]
    sums = [both[:both.shape[0] // 2] + both[both.shape[0] // 2:] for both in sums]
    return [jnp.concatenate(sums[i:i + 2], axis=1) for i in range(0, len(sums), 2)]


def join_many(pairs):
    rest = jnp.zeros((8, 256), F32)
    split_pairs = [(split(jnp.concatenate([first, rest], axis=0)), split(second[:FACE])) for first, second in pairs]
    joined = []
    for total, (_, later) in zip(joined_rows(split_pairs), pairs):
        joined.append(jnp.concatenate([total[:FACE], total[FACE:24] + later[FACE:]], axis=0))
    return joined


def block_slot(mine, other, size, power):
    step = (mine ^ other) if power else (mine - other + size) % size
    return (size - step) % size


def group_kernel(size, power, outer, *refs):
    blocks, total_ref, held = refs[:size], refs[size + 1], refs[size + 2]
    place = lax.axis_index("gx")
    mine = place % size
    rows_y = total_ref.shape[0]

    @pl.when(place // size < outer - 1)
    def _():
        for s in range(size):
            held[s] = blocks[s][...]
        slots = [block_slot(mine, j, size, power) for j in range(size)]
        maps = [[held[slot, y] for slot in slots] for y in range(rows_y)]
        while len(maps[0]) > 1:
            length = len(maps[0])
            joined = join_many([(maps[y][i], maps[y][i + 1]) for y in range(rows_y) for i in range(0, length - 1, 2)])
            half = length // 2
            maps = [joined[y * half:y * half + half] + maps[y][2 * half:] for y in range(rows_y)]
        for y in range(rows_y):
            total_ref[y] = maps[y][0]

    @pl.when(place // size == outer - 1)
    def _():
        total_ref[...] = jnp.zeros(total_ref.shape, F32)


def carried(parts, traces, count):
    keep = (iota((128, 256), 0) % FACE == iota((128, 256), 1) // FACE).astype(BF16)
    here = []
    for trace in traces:
        rows = jnp.concatenate([jnp.broadcast_to(trace[t:t + 1], (FACE, 256)) for t in range(8)], axis=0)
        here.append([part * keep for part in split(rows)])
    by_first = [dot_rows(part, data[0]) for part, data in zip(parts, here)]
    by_second = [dot_rows(part[:count], data[1]) for part, data in zip(parts, here)]
    return [first[:count] + first[count:] + second for first, second in zip(by_first, by_second)]


def write_nodes(result_ref, out_ref, sems, base_ref, part_ref, traces):
    planes, rows_y, nodes, _ = result_ref.shape
    sums = carried([part_ref[y] for y in range(rows_y)], traces, planes * nodes)
    copies = []
    for y in range(rows_y):
        for x in range(planes):
            result_ref[x, y] = base_ref[x, y] + sums[y][x * nodes:(x + 1) * nodes]
            copies.append(pltpu.make_async_copy(result_ref.at[x, y], out_ref.at[x, y], sems.at[x, y]))
            copies[-1].start()
    for copy in copies:
        copy.wait()


def local_kernel(data_ref, label_ref, weight_ref, flow_ref, inv_ref, inflow_ref, base_ref, start_ref, chosen_ref, offset_ref, full_ref):
    planes, rows_y, nodes, columns = base_ref.shape
    coupling = jnp.zeros((nodes, 128), F32)
    count = inv_ref.shape[0]
    gathered = face_columns(inv_ref[...].reshape(count * nodes, nodes), nodes)
    for k in range(count):
        inv_rows = inv_ref[k]
        low = (count + k) * nodes
        products = class_products(
            gathered[k * nodes:k * nodes + nodes], gathered[low:low + nodes], weight_ref[:, 256 * k:256 * k + 256]
        )
        here = pl.ds(k * nodes, nodes)
        shifted = pltpu.roll(products, FACE * k, 1) if k else products
        coupling = jnp.where(iota((nodes, 128), 1) // FACE == k, shifted, coupling)
        full_ref[here, :] = in_parts(with_inverse(inv_rows, products))
    coupling = jnp.concatenate(split(coupling), axis=0)
    for y in range(rows_y):
        start_ref[y] = encode(inflow_ref[y])
    for x in range(planes):
        for y in range(rows_y):
            label = label_ref[pl.ds(x * rows_y + y, 1), :]
            data = data_ref[x, y]
            every = dot(full_ref[...], jnp.concatenate([data, data], axis=0))
            base_ref[x, y] = class_sum(every, label, nodes)
            chosen_ref[x, y] = dot(coupling, picked(label, count)).astype(BF16)
            if x < planes - 1:
                offset_ref[x, y] = encode(flow_ref[x, :, y * columns:(y + 1) * columns])


def carry_kernel(size, power, *refs):
    blocks = refs[:size]
    local_ref, start_ref, chosen_ref, offset_ref, lin_ref = refs[size:size + 5]
    base_ref, part_ref, out_ref, held, result_ref, sems = refs[size + 5:]
    planes, rows_y, nodes, _ = base_ref.shape
    for s in range(size):
        held[s] = blocks[s][...]
    place = lax.axis_index("gx")
    mine = place % size
    same = (iota((24, 256), 1) % FACE == iota((24, 256), 0)).astype(F32)
    ahead = [same] * rows_y
    for j in range(size - 1):
        slot = block_slot(mine, j, size, power)
        block = [held[slot, y] for y in range(rows_y)]
        joined = block if j == 0 else join_many([(ahead[y], block[y]) for y in range(rows_y)])
        ahead = [jnp.where(mine > j, joined[y], ahead[y]) for y in range(rows_y)]
    for x in range(planes):
        chosen = [chosen_ref[x, y] for y in range(rows_y)]
        sums = carried(chosen, [ahead[y][FACE:] for y in range(rows_y)], nodes)
        pairs = [block_diagonal(ahead[y][:FACE]) for y in range(rows_y)]
        firsts = [dot_rows(chosen[y], pairs[y][0]) for y in range(rows_y)]
        seconds = [dot_rows(chosen[y][:nodes], pairs[y][1]) for y in range(rows_y)]
        for y in range(rows_y):
            base_ref[x, y] = local_ref[x, y] + sums[y]
            high, low = split(firsts[y][:nodes] + firsts[y][nodes:] + seconds[y])
            part_ref[y, pl.ds(x * nodes, nodes), :] = high
            part_ref[y, pl.ds((planes + x) * nodes, nodes), :] = low
        if x < planes - 1:
            own = [jnp.concatenate([lin_ref[x, y], offset_ref[x, y]], axis=0) for y in range(rows_y)]
            ahead = join_many([(ahead[y], own[y]) for y in range(rows_y)])

    @pl.when(place < size)
    def _():
        write_nodes(result_ref, out_ref, sems, base_ref, part_ref, [start_ref[y] for y in range(rows_y)])


def finish_kernel(size, inner, power, *refs):
    blocks = refs[:size]
    start_ref, base_ref, part_ref, _, out_ref, result_ref, sems = refs[size:size + 7]
    rows_y = base_ref.shape[1]
    mine = lax.axis_index("gx") // inner
    if power and size <= 4:
        for place in range(1, size):
            @pl.when(mine == place)
            def _():
                traces = [start_ref[y] for y in range(rows_y)]
                for j in range(place):
                    traces = [advance(traces[y], blocks[block_slot(place, j, size, power)][y]) for y in range(rows_y)]
                write_nodes(result_ref, out_ref, sems, base_ref, part_ref, traces)
    else:
        held = refs[size + 7]
        for s in range(size):
            held[s] = blocks[s][...]

        @pl.when(mine > 0)
        def _():
            traces = []
            for y in range(rows_y):
                trace = start_ref[y]
                for j in range(size - 1):
                    slot = block_slot(mine, j, size, power)
                    trace = jnp.where(mine > j, advance(trace, held[slot, y]), trace)
                traces.append(trace)
            write_nodes(result_ref, out_ref, sems, base_ref, part_ref, traces)


def moved(value, pairs):
    return lax.ppermute(value, ("gx", "gy"), pairs)


def shape(dims, kind=F32):
    return jax.ShapeDtypeStruct(dims, kind)


def call(kernel, outs, name, args, scratch=(), space=pltpu.VMEM, out_spaces=None, aliases=None, limit=48):
    many = isinstance(outs, tuple)
    spaces = out_spaces or ((pltpu.VMEM,) * len(outs) if many else pltpu.VMEM)
    if isinstance(space, tuple):
        in_specs = [pl.BlockSpec(memory_space=one) for one in space]
    else:
        in_specs = [pl.BlockSpec(memory_space=space)] * len(args)
    if many:
        out_specs = tuple(pl.BlockSpec(memory_space=one) for one in spaces)
    else:
        out_specs = pl.BlockSpec(memory_space=spaces)
    return pl.pallas_call(
        kernel,
        out_shape=outs,
        in_specs=in_specs,
        out_specs=out_specs,
        scratch_shapes=list(scratch),
        input_output_aliases=aliases or {},
        name=name,
        cost_estimate=pl.CostEstimate(flops=1000000, bytes_accessed=500000, transcendentals=0),
        compiler_params=pltpu.CompilerParams(vmem_limit_bytes=limit * 1024 * 1024),
    )(*args)


def on_device(gx_size, gy_size, u_old, rhs, classes, flags, inverse, x_face, lateral_faces, inflow):
    planes, rows_y, nodes, columns = u_old.shape
    count = inverse.shape[0]
    everyone = [(x, y) for x in range(gx_size) for y in range(gy_size)]

    def at(x, y):
        return x * gy_size + y

    if gy_size == 2:
        below = above = moved(u_old, [(at(x, y), at(x, 1 - y)) for x, y in everyone])
    else:
        below = moved(u_old[:, rows_y - 1:], [(at(x, y), at(x, y + 1)) for x, y in everyone if y + 1 < gy_size])
        above = moved(u_old[:, :1], [(at(x, y), at(x, y - 1)) for x, y in everyone if y > 0])
    weights, out_rows, step, labels = call(
        params_kernel,
        (
            shape((5 * FACE, count * 256), BF16),
            shape((count * FACE, 256), BF16),
            shape((count * FACE, 128), BF16),
            shape((3 * planes * rows_y, columns)),
        ),
        "class_matrices",
        tuple(
            pltpu.with_memory_space_constraint(value, pltpu.HBM)
            for value in (classes, flags, x_face, lateral_faces, inverse)
        ),
        [
            pltpu.VMEM(classes.shape, jnp.int32),
            pltpu.VMEM(flags.shape, jnp.int32),
            pltpu.VMEM(x_face.shape, F32),
            pltpu.VMEM(lateral_faces.shape, F32),
            pltpu.VMEM((count, FACE, nodes), F32),
            pltpu.SemaphoreType.DMA((5,)),
        ],
        space=pltpu.HBM,
    )
    data, flow, linear, here = call(
        functools.partial(sources_kernel, gy_size),
        (
            shape((planes, rows_y, 128, columns), BF16),
            shape((planes, FACE, rows_y * columns)),
            shape((planes, rows_y, FACE, 256)),
            shape((rows_y, 24, 256)),
        ),
        "sources",
        (u_old, rhs, below, above, labels, out_rows, step),
    )
    inner = 4 if gx_size % 4 == 0 else 1
    outer = gx_size // inner
    power = outer & (outer - 1) == 0
    near = [here]
    for s in range(inner - 1, 0, -1):
        near.append(moved(here, [(at(x, y), at(x ^ s, y)) for x, y in everyone]))
    nodes_shape = (planes, rows_y, nodes, columns)
    writing = [pltpu.VMEM(nodes_shape, F32), pltpu.SemaphoreType.DMA((planes, rows_y))]
    local, start, chosen, offsets = call(
        local_kernel,
        (
            shape(nodes_shape),
            shape((rows_y, 8, 256)),
            shape((planes, rows_y, 2 * nodes, 256), BF16),
            shape((max(planes - 1, 1), rows_y, 8, 256)),
        ),
        "local_solve",
        (data, labels, weights, flow, inverse, inflow),
        [pltpu.VMEM((count * nodes, 256), BF16)],
    )
    total = call(
        functools.partial(group_kernel, inner, True, outer),
        shape((rows_y, 24, 256)),
        "group_maps",
        tuple(near) + (start,),
        [pltpu.VMEM((inner, rows_y, 24, 256), F32)],
    )
    blocks = [total]
    for s in range(outer - 1, 0, -1):
        if power:
            pairs = [(at(x, y), at(x ^ (s * inner), y)) for x, y in everyone]
        else:
            pairs = [(at(x, y), at((x + s * inner) % gx_size, y)) for x, y in everyone]
        blocks.append(moved(total, pairs))
    base, parts, out = call(
        functools.partial(carry_kernel, inner, True),
        (
            shape(nodes_shape),
            shape((rows_y, 2 * planes * nodes, 256), BF16),
            pltpu.HBM(nodes_shape, F32),
        ),
        "carry_maps",
        tuple(near) + (local, start, chosen, offsets, linear),
        [pltpu.VMEM((inner, rows_y, 24, 256), F32)] + writing,
        out_spaces=(pltpu.VMEM, pltpu.VMEM, pltpu.HBM),
    )
    held = [] if power and outer <= 4 else [pltpu.VMEM((outer, rows_y, 24, 256), F32)]
    args = tuple(blocks) + (start, base, parts, out)
    return call(
        functools.partial(finish_kernel, outer, inner, power),
        pltpu.HBM(nodes_shape, F32),
        "finish",
        args,
        writing + held,
        space=(pltpu.VMEM,) * (len(args) - 1) + (pltpu.HBM,),
        out_spaces=pltpu.HBM,
        aliases={len(args) - 1: 0},
    )


def solution(mesh):
    in_specs = (
        P("gx", "gy", None, None),
        P("gx", "gy", None, None),
        P("gx", "gy", None),
        P(None, "gx", "gy", None),
        P(),
        P(),
        P(),
        P("gy", None, None),
    )
    out_specs = P("gx", "gy", None, None)
    body = functools.partial(on_device, mesh.shape["gx"], mesh.shape["gy"])
    return jax.shard_map(body, mesh=mesh, in_specs=in_specs, out_specs=out_specs, check_vma=False)
```

```python
import functools

import jax
import jax.numpy as jnp
from jax import lax
from jax.experimental import pallas as pl
from jax.experimental.pallas import tpu as pltpu
from jax.sharding import PartitionSpec as P

FACE = 16
HIGH = lax.Precision.HIGHEST
F32 = jnp.float32
BF16 = jnp.bfloat16


def iota(shape, dim):
    return lax.broadcasted_iota(jnp.int32, shape, dim)


def exact(left, right):
    return jnp.dot(left, right, precision=HIGH, preferred_element_type=F32)


def split(value):
    high = value.astype(BF16)
    return high, (value - high.astype(F32)).astype(BF16)


def wanted_node(face, item):
    high, low = item // 4, item % 4
    return jnp.where(face < 2, 16 * high + low + 12 * (face == 1), 16 * high + 4 * low + 3 * (face == 3))


def dot(left, right):
    return jnp.dot(left, right, preferred_element_type=F32)


def dot_rows(left, right):
    return lax.dot_general(left, right, (((1,), (1,)), ((), ())), preferred_element_type=F32)


def applied(rows, linear):
    lane = iota((rows.shape[0], 128), 1)
    halves = []
    for begin in (0, 128):
        part, total = rows[:, begin:begin + 128], None
        for b in range(FACE):
            near = jnp.take_along_axis(part, lane // FACE * FACE + b, axis=1, mode="promise_in_bounds")
            term = near * linear[b:b + 1, begin:begin + 128]
            total = term if total is None else total + term
        halves.append(total)
    return jnp.concatenate(halves, axis=1)


def join(earlier, later):
    moved_rows = applied(earlier, later[:FACE])
    return jnp.concatenate([moved_rows[:FACE], moved_rows[FACE:] + later[FACE:]], axis=0)


def advance(trace, later):
    return applied(trace, later[:FACE]) + later[FACE:]


def encode(value):
    keep = (iota((256, 128), 0) // FACE == iota((256, 128), 1) % FACE).astype(BF16)
    spread = [jnp.concatenate([part] * 16, axis=0) * keep for part in split(value)]
    gather = (iota((8, 256), 1) % 128 // FACE == iota((8, 256), 0)).astype(BF16)
    return dot_rows(gather, jnp.concatenate(spread, axis=1))


def face_columns(inv_rows, nodes):
    at = iota((nodes, 5 * FACE), 1)
    wanted = jnp.where(at < 64, wanted_node(at // FACE, at % FACE), at - 64)
    chosen = (iota((nodes, 5 * FACE), 0) == wanted).astype(BF16)
    return dot(jnp.concatenate(split(inv_rows), axis=0), chosen).astype(BF16)


def class_products(high, low, weights):
    count = high.shape[0]
    parts = dot(jnp.concatenate([high, low], axis=0), weights)
    return -(parts[:count, :128] + parts[:count, 128:] + parts[count:, :128])


def with_inverse(inv_rows, products):
    count = inv_rows.shape[0]
    wide = jnp.concatenate([inv_rows, jnp.zeros((count, 128 - inv_rows.shape[1]), F32)], axis=1)
    return jnp.where(iota((count, 128), 1) < 64, wide, products)


def in_parts(value):
    high, low = split(value)
    return jnp.concatenate([high, low], axis=1)


def coupling_parts(products):
    high, low = split(products)
    lane = iota(products.shape, 1)
    return jnp.where(lane < 32, high.astype(F32), jnp.where(lane < 48, low.astype(F32), 0.0)).astype(BF16)


def params_kernel(cls_hbm, flag_hbm, x_hbm, lat_hbm, inv_hbm, weight_ref, out_ref, step_ref, label_ref,
                  cls_ref, flag_ref, x_ref, lat_ref, inv_ref, sems):
    pairs = ((cls_hbm, cls_ref), (flag_hbm, flag_ref), (x_hbm, x_ref), (lat_hbm, lat_ref))
    pairs += ((inv_hbm.at[:, inv_hbm.shape[1] - FACE:, :], inv_ref),)
    copies = [pltpu.make_async_copy(a, b, sems.at[i]) for i, (a, b) in enumerate(pairs)]
    for copy in copies:
        copy.start()
    count, nodes, _ = inv_hbm.shape
    planes = cls_ref.shape[0]
    item, lane = iota((FACE, 128), 0), iota((FACE, 128), 1)
    places = [(lane == 64 + FACE * f + item).astype(BF16) for f in range(4)]
    places.append(((lane < 48) & (lane % FACE == item)).astype(BF16))
    for copy in copies[:2]:
        copy.wait()
    labels = [cls_ref[x] for x in range(planes)]
    labels += [flag_ref[d, x] for d in range(2) for x in range(planes)]
    labels = jnp.concatenate(labels, axis=0).astype(F32).astype(BF16)
    tile = (iota((FACE, 128), 1) % FACE == iota((FACE, 128), 0)).astype(BF16)
    label_ref[...] = dot(labels, tile)
    for copy in copies[2:]:
        copy.wait()
    placed = []
    for f in range(5):
        rows = (lat_ref[f] if f < 4 else x_ref[...]).reshape(count * FACE, FACE)
        placed.append(dot(jnp.concatenate(split(rows), axis=0), places[f]).astype(BF16))
    inv_rows = [inv_ref[k] for k in range(count)]
    gathered = face_columns(jnp.concatenate(inv_rows, axis=0), nodes)
    outs, steps = [], []
    for k in range(count):
        columns = []
        for part in range(2):
            begin = part * count * FACE + k * FACE
            columns.append(jnp.concatenate([p[begin:begin + FACE] for p in placed], axis=0))
        weights = jnp.concatenate(columns, axis=1)
        weight_ref[:, 256 * k:256 * k + 256] = weights
        low = (count + k) * FACE
        products = class_products(gathered[k * FACE:k * FACE + FACE], gathered[low:low + FACE], weights)
        outs.append(with_inverse(inv_rows[k], products))
        steps.append(products)
    out_ref[...] = in_parts(jnp.concatenate(outs, axis=0))
    step_ref[...] = coupling_parts(jnp.concatenate(steps, axis=0))


def picked(label, count):
    wide = (iota((FACE, 256), 1) // FACE == iota((FACE, 256), 0)).astype(BF16)
    on_wide = dot(label[:, :FACE].astype(BF16), wide).astype(jnp.int32)
    row, lane = iota((count * FACE, 256), 0), iota((count * FACE, 256), 1)
    return jnp.where((row % FACE == lane % FACE) & (row // FACE == on_wide), 1.0, 0.0).astype(BF16)


def class_sum(every, label, rows):
    total = None
    for k in range(8):
        term = jnp.where(label == k, every[k * rows:(k + 1) * rows], 0.0)
        total = term if total is None else total + term
    return total


def stacked(value):
    first, second = split(value)
    rest = jnp.zeros((128 - 3 * FACE, value.shape[1]), BF16)
    return jnp.concatenate([first, second, first, rest], axis=0)


def sources_kernel(gy_size, u_ref, rhs_ref, below_ref, above_ref, label_ref, out_ref, step_ref, x_ref, flow_ref, lin_ref, map_ref):
    planes, rows_y, nodes, columns = u_ref.shape
    place = lax.axis_index("gy")
    node, item = iota((nodes, nodes), 1), iota((nodes, nodes), 0)
    chosen = (node == wanted_node(item // FACE, item % FACE)).astype(BF16)
    own = [u_ref[x, y] for x in range(planes) for y in range(rows_y)]
    other = [below_ref[x, below_ref.shape[1] - 1] for x in range(planes)] + [above_ref[x, 0] for x in range(planes)]
    step = step_ref[...]
    row, lane = iota((2 * FACE, 128), 0), iota((2 * FACE, 128), 1)
    flip = (lane == row + FACE * (row >= FACE)).astype(BF16)
    turned = dot_rows(flip, step).astype(BF16)
    faces = dot(chosen, jnp.concatenate(own + other, axis=1))
    picks = []
    for at in range(planes * rows_y):
        picks.append(picked(label_ref[pl.ds(at, 1), :], step.shape[0] // FACE))
    linear = dot(turned, jnp.concatenate(picks, axis=1))
    faces = [faces[:, i * columns:(i + 1) * columns] for i in range(len(own) + len(other))]
    z_at = iota((FACE, columns), 1) % FACE
    has_below = jnp.where(place > 0, 1.0, 0.0)
    has_above = jnp.where(place < gy_size - 1, 1.0, 0.0)
    data = []
    for x in range(planes):
        under = faces[len(own) + x][16:32] * has_below
        over = faces[len(own) + planes + x][0:16] * has_above
        for y in range(rows_y):
            at = x * rows_y + y
            y_flag = label_ref[pl.ds(planes * rows_y + at, 1), :]
            z_flag = label_ref[pl.ds(2 * planes * rows_y + at, 1), :]
            from_below = faces[at - 1][16:32] if y > 0 else under
            from_above = faces[at + 1][0:16] if y < rows_y - 1 else over
            from_front = jnp.where(z_at == 0, 0.0, pltpu.roll(faces[at][48:64], 1, 1))
            from_back = jnp.where(z_at == FACE - 1, 0.0, pltpu.roll(faces[at][32:48], columns - 1, 1))
            lateral = jnp.concatenate(
                [
                    from_below * (1.0 - y_flag),
                    from_above * y_flag,
                    from_front * (1.0 - z_flag),
                    from_back * z_flag,
                ],
                axis=0,
            ).astype(BF16)
            here = jnp.concatenate([rhs_ref[x, y], lateral], axis=0)
            x_ref[x, y] = here
            data.append(here)
    data = jnp.concatenate(data, axis=1)
    every = dot(out_ref[...], jnp.concatenate([data, data], axis=0))
    keep = (iota((256, 256), 0) // FACE == iota((256, 256), 1) // FACE).astype(BF16)
    wholes, pairs = None, None
    for x in range(planes):
        here = [linear[:, at * 256:at * 256 + 256] for at in range(x * rows_y, (x + 1) * rows_y)]
        both = [(part[:FACE].astype(BF16), part[FACE:].astype(BF16)) for part in here]
        for y in range(rows_y):
            lin_ref[x, y] = here[y][:FACE] + here[y][FACE:]
        if wholes is None:
            wholes, pairs = [part[:FACE] + part[FACE:] for part in here], both
        else:
            blocks = [[jnp.concatenate([part] * 16, axis=0) * keep for part in parts] for parts in both]
            stacks = [jnp.concatenate(pair, axis=0) for pair in pairs]
            firsts = [dot(stack, block[0]) for stack, block in zip(stacks, blocks)]
            seconds = [dot(pair[0], block[1]) for pair, block in zip(pairs, blocks)]
            wholes = [first[:FACE] + first[FACE:] + second for first, second in zip(firsts, seconds)]
            pairs = [split(whole) for whole in wholes]
    total = None
    for x in range(planes):
        begin = x * rows_y * columns
        label = jnp.concatenate([label_ref[pl.ds(x * rows_y + y, 1), :] for y in range(rows_y)], axis=1)
        flow = class_sum(every[:, begin:begin + rows_y * columns], label, FACE)
        flow_ref[x] = flow
        if total is not None:
            flow = flow + class_sum(dot(step_ref[...], stacked(total)), label, FACE)
        total = flow
    for y in range(rows_y):
        map_ref[y, 0:FACE] = wholes[y]
        map_ref[y, FACE:] = encode(total[:, y * columns:(y + 1) * columns])


def block_diagonal(linear):
    keep = (iota((256, 256), 0) // FACE == iota((256, 256), 1) // FACE).astype(BF16)
    return [jnp.concatenate([part] * 16, axis=0) * keep for part in split(linear)]


def half_weights(high, low, begin):
    keep = (iota((128, 128), 0) // FACE == iota((128, 128), 1) // FACE).astype(BF16)
    parts = [jnp.concatenate([part[:, begin:begin + 128]] * 8, axis=0) * keep for part in (high, low)]
    return jnp.concatenate(parts, axis=0)


def half_rows(high, low, begin):
    high, low = high[:, begin:begin + 128], low[:, begin:begin + 128]
    upper = jnp.concatenate([high, high], axis=1)
    return jnp.concatenate([upper, jnp.concatenate([low, jnp.zeros_like(low)], axis=1)], axis=0)


def joined_rows(pairs):
    ready = [
        (half_rows(*rows, begin), half_weights(*linear, begin)) for rows, linear in pairs for begin in (0, 128)
    ]
    sums = [dot(rows, weights) for rows, weights in ready]
    sums = [both[:both.shape[0] // 2] + both[both.shape[0] // 2:] for both in sums]
    return [jnp.concatenate(sums[i:i + 2], axis=1) for i in range(0, len(sums), 2)]


def join_many(pairs):
    rest = jnp.zeros((8, 256), F32)
    split_pairs = [(split(jnp.concatenate([first, rest], axis=0)), split(second[:FACE])) for first, second in pairs]
    joined = []
    for total, (_, later) in zip(joined_rows(split_pairs), pairs):
        joined.append(jnp.concatenate([total[:FACE], total[FACE:24] + later[FACE:]], axis=0))
    return joined


def sent_steps(size, first):
    return (2, 1) + tuple(range(3, size)) if first == 2 and size > 2 else tuple(range(1, size))


def block_slot(mine, other, size, power, first):
    step = (mine ^ other) if power else (mine - other + size) % size
    return step + 1 * (step == 1) - 1 * (step == 2) if first == 2 and size > 2 else step


def group_kernel(size, power, outer, *refs):
    blocks, total_ref, held = refs[:size], refs[size + 1], refs[size + 2]
    place = lax.axis_index("gx")
    mine = place % size
    rows_y = total_ref.shape[0]

    @pl.when(place // size < outer - 1)
    def _():
        for s in range(size):
            held[s] = blocks[s][...]
        slots = [block_slot(mine, j, size, power, 1) for j in range(size)]
        maps = [[held[slot, y] for slot in slots] for y in range(rows_y)]
        while len(maps[0]) > 1:
            length = len(maps[0])
            joined = join_many([(maps[y][i], maps[y][i + 1]) for y in range(rows_y) for i in range(0, length - 1, 2)])
            half = length // 2
            maps = [joined[y * half:y * half + half] + maps[y][2 * half:] for y in range(rows_y)]
        for y in range(rows_y):
            total_ref[y] = maps[y][0]

    @pl.when(place // size == outer - 1)
    def _():
        total_ref[...] = jnp.zeros(total_ref.shape, F32)


def carried(parts, traces, count):
    keep = (iota((128, 256), 0) % FACE == iota((128, 256), 1) // FACE).astype(BF16)
    here = []
    for trace in traces:
        rows = jnp.concatenate([jnp.broadcast_to(trace[t:t + 1], (FACE, 256)) for t in range(8)], axis=0)
        here.append([part * keep for part in split(rows)])
    by_first = [dot_rows(part, data[0]) for part, data in zip(parts, here)]
    by_second = [dot_rows(part[:count], data[1]) for part, data in zip(parts, here)]
    return [first[:count] + first[count:] + second for first, second in zip(by_first, by_second)]


def write_nodes(result_ref, out_ref, sems, base_ref, part_ref, traces):
    planes, rows_y, nodes, _ = result_ref.shape
    sums = carried([part_ref[y] for y in range(rows_y)], traces, planes * nodes)
    copies = []
    for y in range(rows_y):
        for x in range(planes):
            result_ref[x, y] = base_ref[x, y] + sums[y][x * nodes:(x + 1) * nodes]
            copies.append(pltpu.make_async_copy(result_ref.at[x, y], out_ref.at[x, y], sems.at[x, y]))
            copies[-1].start()
    for copy in copies:
        copy.wait()


def local_kernel(data_ref, label_ref, weight_ref, flow_ref, inv_ref, inflow_ref, base_ref, start_ref, chosen_ref, offset_ref, full_ref):
    planes, rows_y, nodes, columns = base_ref.shape
    coupling = jnp.zeros((nodes, 128), F32)
    count = inv_ref.shape[0]
    gathered = face_columns(inv_ref[...].reshape(count * nodes, nodes), nodes)
    for k in range(count):
        inv_rows = inv_ref[k]
        low = (count + k) * nodes
        products = class_products(
            gathered[k * nodes:k * nodes + nodes], gathered[low:low + nodes], weight_ref[:, 256 * k:256 * k + 256]
        )
        here = pl.ds(k * nodes, nodes)
        shifted = pltpu.roll(products, FACE * k, 1) if k else products
        coupling = jnp.where(iota((nodes, 128), 1) // FACE == k, shifted, coupling)
        full_ref[here, :] = in_parts(with_inverse(inv_rows, products))
    coupling = jnp.concatenate(split(coupling), axis=0)
    for y in range(rows_y):
        start_ref[y] = encode(inflow_ref[y])
    for x in range(planes):
        for y in range(rows_y):
            label = label_ref[pl.ds(x * rows_y + y, 1), :]
            data = data_ref[x, y]
            every = dot(full_ref[...], jnp.concatenate([data, data], axis=0))
            base_ref[x, y] = class_sum(every, label, nodes)
            chosen_ref[x, y] = dot(coupling, picked(label, count)).astype(BF16)
            if x < planes - 1:
                offset_ref[x, y] = encode(flow_ref[x, :, y * columns:(y + 1) * columns])


def ahead_kernel(size, power, *refs):
    blocks, ahead_ref, held = refs[:size], refs[size + 1], refs[size + 2]
    rows_y = ahead_ref.shape[0]
    for s in range(size):
        held[s] = blocks[s][...]
    mine = lax.axis_index("gx") % size
    same = (iota((24, 256), 1) % FACE == iota((24, 256), 0)).astype(F32)
    ahead = [same] * rows_y
    for j in range(size - 1):
        slot = block_slot(mine, j, size, power, 1)
        block = [held[slot, y] for y in range(rows_y)]
        joined = block if j == 0 else join_many([(ahead[y], block[y]) for y in range(rows_y)])
        ahead = [jnp.where(mine > j, joined[y], ahead[y]) for y in range(rows_y)]
    for y in range(rows_y):
        ahead_ref[y] = ahead[y]


def carry_kernel(size, swapped, ahead_ref, local_ref, start_ref, chosen_ref, offset_ref, lin_ref, base_ref, part_ref, out_ref, result_ref, sems):
    planes, rows_y, nodes, _ = base_ref.shape
    place = lax.axis_index("gx")
    if swapped:
        ahead_ref = ahead_ref.at[1 - lax.axis_index("gy") % 2]
    row_range = range(rows_y)

    def plane_map(x):
        return [jnp.concatenate([lin_ref[x, y], offset_ref[x, y]], axis=0) for y in row_range]

    @pl.when(place < size)
    def _():
        traces = [advance(start_ref[y], ahead_ref[y]) for y in row_range]
        copies = []
        for x in range(planes):
            sums = carried([chosen_ref[x, y] for y in row_range], traces, nodes)
            for y in row_range:
                result_ref[x, y] = local_ref[x, y] + sums[y]
                copies.append(pltpu.make_async_copy(result_ref.at[x, y], out_ref.at[x, y], sems.at[x, y]))
                copies[-1].start()
            if x < planes - 1:
                traces = [advance(trace, own) for trace, own in zip(traces, plane_map(x))]
        for copy in copies:
            copy.wait()

    @pl.when(place >= size)
    def _():
        ahead = [ahead_ref[y] for y in row_range]
        for x in range(planes):
            chosen = [chosen_ref[x, y] for y in row_range]
            sums = carried(chosen, [ahead[y][FACE:] for y in row_range], nodes)
            pairs = [block_diagonal(ahead[y][:FACE]) for y in row_range]
            firsts = [dot_rows(chosen[y], pairs[y][0]) for y in row_range]
            seconds = [dot_rows(chosen[y][:nodes], pairs[y][1]) for y in row_range]
            for y in row_range:
                base_ref[x, y] = local_ref[x, y] + sums[y]
                high, low = split(firsts[y][:nodes] + firsts[y][nodes:] + seconds[y])
                part_ref[y, pl.ds(x * nodes, nodes), :] = high
                part_ref[y, pl.ds((planes + x) * nodes, nodes), :] = low
            if x < planes - 1:
                ahead = join_many(list(zip(ahead, plane_map(x))))


def finish_places(places, steps, inner, *refs):
    blocks = refs[:len(steps)]
    start_ref, base_ref, part_ref, _, out_ref, result_ref, sems = refs[len(steps):]
    mine = lax.axis_index("gx") // inner
    for place in places:
        @pl.when(mine == place)
        def _():
            traces = [start_ref[y] for y in range(base_ref.shape[1])]
            for j in range(place):
                block = blocks[steps.index(place ^ j)]
                traces = [advance(trace, block[y]) for y, trace in enumerate(traces)]
            write_nodes(result_ref, out_ref, sems, base_ref, part_ref, traces)


def finish_kernel(size, inner, power, *refs):
    blocks = refs[:size]
    start_ref, base_ref, part_ref, _, out_ref, result_ref, sems = refs[size:size + 7]
    rows_y = base_ref.shape[1]
    mine = lax.axis_index("gx") // inner
    held = refs[size + 7]
    for s in range(size):
        held[s] = blocks[s][...]

    @pl.when(mine > 0)
    def _():
        traces = []
        for y in range(rows_y):
            trace = start_ref[y]
            for j in range(size - 1):
                slot = block_slot(mine, j, size, power, 2)
                trace = jnp.where(mine > j, advance(trace, held[slot, y]), trace)
            traces.append(trace)
        write_nodes(result_ref, out_ref, sems, base_ref, part_ref, traces)


def moved(value, pairs):
    return lax.ppermute(value, ("gx", "gy"), pairs)


def shape(dims, kind=F32):
    return jax.ShapeDtypeStruct(dims, kind)


def call(kernel, outs, name, args, scratch=(), space=pltpu.VMEM, out_spaces=None, aliases=None, limit=48):
    many = isinstance(outs, tuple)
    spaces = out_spaces or ((pltpu.VMEM,) * len(outs) if many else pltpu.VMEM)
    if isinstance(space, tuple):
        in_specs = [pl.BlockSpec(memory_space=one) for one in space]
    else:
        in_specs = [pl.BlockSpec(memory_space=space)] * len(args)
    if many:
        out_specs = tuple(pl.BlockSpec(memory_space=one) for one in spaces)
    else:
        out_specs = pl.BlockSpec(memory_space=spaces)
    return pl.pallas_call(
        kernel,
        out_shape=outs,
        in_specs=in_specs,
        out_specs=out_specs,
        scratch_shapes=list(scratch),
        input_output_aliases=aliases or {},
        name=name,
        cost_estimate=pl.CostEstimate(flops=1000000, bytes_accessed=500000, transcendentals=0),
        compiler_params=pltpu.CompilerParams(vmem_limit_bytes=limit * 1024 * 1024),
    )(*args)


def on_device(gx_size, gy_size, u_old, rhs, classes, flags, inverse, x_face, lateral_faces, inflow):
    planes, rows_y, nodes, columns = u_old.shape
    count = inverse.shape[0]
    everyone = [(x, y) for x in range(gx_size) for y in range(gy_size)]

    def at(x, y):
        return x * gy_size + y

    if gy_size == 2:
        below = above = moved(u_old, [(at(x, y), at(x, 1 - y)) for x, y in everyone])
    else:
        below = moved(u_old[:, rows_y - 1:], [(at(x, y), at(x, y + 1)) for x, y in everyone if y + 1 < gy_size])
        above = moved(u_old[:, :1], [(at(x, y), at(x, y - 1)) for x, y in everyone if y > 0])
    weights, out_rows, step, labels = call(
        params_kernel,
        (
            shape((5 * FACE, count * 256), BF16),
            shape((count * FACE, 256), BF16),
            shape((count * FACE, 128), BF16),
            shape((3 * planes * rows_y, columns)),
        ),
        "class_matrices",
        tuple(
            pltpu.with_memory_space_constraint(value, pltpu.HBM)
            for value in (classes, flags, x_face, lateral_faces, inverse)
        ),
        [
            pltpu.VMEM(classes.shape, jnp.int32),
            pltpu.VMEM(flags.shape, jnp.int32),
            pltpu.VMEM(x_face.shape, F32),
            pltpu.VMEM(lateral_faces.shape, F32),
            pltpu.VMEM((count, FACE, nodes), F32),
            pltpu.SemaphoreType.DMA((5,)),
        ],
        space=pltpu.HBM,
    )
    data, flow, linear, here = call(
        functools.partial(sources_kernel, gy_size),
        (
            shape((planes, rows_y, 128, columns), BF16),
            shape((planes, FACE, rows_y * columns)),
            shape((planes, rows_y, FACE, 256)),
            shape((rows_y, 24, 256)),
        ),
        "sources",
        (u_old, rhs, below, above, labels, out_rows, step),
    )
    inner = 4 if gx_size % 4 == 0 else 1
    outer = gx_size // inner
    power = outer & (outer - 1) == 0
    other = 1 if gy_size % 2 == 0 else 0

    def exchanged(value, step):
        if power or step < inner:
            return moved(value, [(at(x, y), at(x ^ step, y ^ other)) for x, y in everyone])
        return moved(value, [(at(x, y), at((x + step) % gx_size, y ^ other)) for x, y in everyone])

    near = ((exchanged(here, 0) if other else here),) + tuple(exchanged(here, s) for s in sent_steps(inner, 1))
    nodes_shape = (planes, rows_y, nodes, columns)
    writing = [pltpu.VMEM(nodes_shape, F32), pltpu.SemaphoreType.DMA((planes, rows_y))]
    local, start, chosen, offsets = call(
        local_kernel,
        (
            shape(nodes_shape),
            shape((rows_y, 8, 256)),
            shape((planes, rows_y, 2 * nodes, 256), BF16),
            shape((max(planes - 1, 1), rows_y, 8, 256)),
        ),
        "local_solve",
        (data, labels, weights, flow, inverse, inflow),
        [pltpu.VMEM((count * nodes, 256), BF16)],
    )
    total = call(
        functools.partial(group_kernel, inner, True, outer),
        shape((rows_y, 24, 256)),
        "group_maps",
        near + (start,),
        [pltpu.VMEM((inner, rows_y, 24, 256), F32)],
    )
    blocks = [total] + [exchanged(total, s * inner) for s in sent_steps(outer, 2)]
    ahead = call(
        functools.partial(ahead_kernel, inner, True),
        shape((rows_y, 24, 256)),
        "maps_ahead",
        near + (total,),
        [pltpu.VMEM((inner, rows_y, 24, 256), F32)],
    )
    if other:
        couples = [[y, y + 1] for y in range(0, gy_size, 2)]
        ahead = lax.all_gather(ahead, "gy", axis_index_groups=couples)
    base, parts, out = call(
        functools.partial(carry_kernel, inner, other == 1),
        (
            shape(nodes_shape),
            shape((rows_y, 2 * planes * nodes, 256), BF16),
            pltpu.HBM(nodes_shape, F32),
        ),
        "carry_maps",
        (ahead, local, start, chosen, offsets, linear),
        writing,
        out_spaces=(pltpu.VMEM, pltpu.VMEM, pltpu.HBM),
    )
    def written(kernel, name, args, scratch):
        return call(
            kernel,
            pltpu.HBM(nodes_shape, F32),
            name,
            args,
            scratch,
            space=(pltpu.VMEM,) * (len(args) - 1) + (pltpu.HBM,),
            out_spaces=pltpu.HBM,
            aliases={len(args) - 1: 0},
        )

    if power and outer == 4:
        steps = sent_steps(outer, 2)
        early = (3, 1)
        out = written(
            functools.partial(finish_places, (1,), early, inner),
            "finish_second",
            tuple(blocks[1 + steps.index(one)] for one in early) + (start, base, parts, out),
            writing,
        )
        return written(
            functools.partial(finish_places, (2, 3), steps, inner),
            "finish_last",
            tuple(blocks[1:]) + (start, base, parts, out),
            writing,
        )
    return written(
        functools.partial(finish_kernel, outer, inner, power),
        "finish",
        tuple(blocks) + (start, base, parts, out),
        writing + [pltpu.VMEM((outer, rows_y, 24, 256), F32)],
    )


def solution(mesh):
    in_specs = (
        P("gx", "gy", None, None),
        P("gx", "gy", None, None),
        P("gx", "gy", None),
        P(None, "gx", "gy", None),
        P(),
        P(),
        P(),
        P("gy", None, None),
    )
    out_specs = P("gx", "gy", None, None)
    body = functools.partial(on_device, mesh.shape["gx"], mesh.shape["gy"])
    return jax.shard_map(body, mesh=mesh, in_specs=in_specs, out_specs=out_specs, check_vma=False)
```

```python
import functools

import jax
import jax.numpy as jnp
from jax import lax
from jax.experimental import pallas as pl
from jax.experimental.pallas import tpu as pltpu
from jax.sharding import PartitionSpec as P

FACE = 16
HIGH = lax.Precision.HIGHEST
F32 = jnp.float32
BF16 = jnp.bfloat16


def iota(shape, dim):
    return lax.broadcasted_iota(jnp.int32, shape, dim)


def exact(left, right):
    return jnp.dot(left, right, precision=HIGH, preferred_element_type=F32)


def split(value):
    high = value.astype(BF16)
    return high, (value - high.astype(F32)).astype(BF16)


def wanted_node(face, item):
    high, low = item // 4, item % 4
    return jnp.where(face < 2, 16 * high + low + 12 * (face == 1), 16 * high + 4 * low + 3 * (face == 3))


def dot(left, right):
    return jnp.dot(left, right, preferred_element_type=F32)


def dot_rows(left, right):
    return lax.dot_general(left, right, (((1,), (1,)), ((), ())), preferred_element_type=F32)


def applied(rows, linear):
    lane = iota((rows.shape[0], 128), 1)
    halves = []
    for begin in (0, 128):
        part, total = rows[:, begin:begin + 128], None
        for b in range(FACE):
            near = jnp.take_along_axis(part, lane // FACE * FACE + b, axis=1, mode="promise_in_bounds")
            term = near * linear[b:b + 1, begin:begin + 128]
            total = term if total is None else total + term
        halves.append(total)
    return jnp.concatenate(halves, axis=1)


def join(earlier, later):
    moved_rows = applied(earlier, later[:FACE])
    return jnp.concatenate([moved_rows[:FACE], moved_rows[FACE:] + later[FACE:]], axis=0)


def advance(trace, later):
    return applied(trace, later[:FACE]) + later[FACE:]


def encode(value):
    keep = (iota((256, 128), 0) // FACE == iota((256, 128), 1) % FACE).astype(BF16)
    spread = [jnp.concatenate([part] * 16, axis=0) * keep for part in split(value)]
    gather = (iota((8, 256), 1) % 128 // FACE == iota((8, 256), 0)).astype(BF16)
    return dot_rows(gather, jnp.concatenate(spread, axis=1))


def face_columns(inv_rows, nodes):
    at = iota((nodes, 5 * FACE), 1)
    wanted = jnp.where(at < 64, wanted_node(at // FACE, at % FACE), at - 64)
    chosen = (iota((nodes, 5 * FACE), 0) == wanted).astype(BF16)
    return dot(jnp.concatenate(split(inv_rows), axis=0), chosen).astype(BF16)


def class_products(high, low, weights):
    count = high.shape[0]
    parts = dot(jnp.concatenate([high, low], axis=0), weights)
    return -(parts[:count, :128] + parts[:count, 128:] + parts[count:, :128])


def with_inverse(inv_rows, products):
    count = inv_rows.shape[0]
    wide = jnp.concatenate([inv_rows, jnp.zeros((count, 128 - inv_rows.shape[1]), F32)], axis=1)
    return jnp.where(iota((count, 128), 1) < 64, wide, products)


def in_parts(value):
    high, low = split(value)
    return jnp.concatenate([high, low], axis=1)


def coupling_parts(products):
    high, low = split(products)
    lane = iota(products.shape, 1)
    return jnp.where(lane < 32, high.astype(F32), jnp.where(lane < 48, low.astype(F32), 0.0)).astype(BF16)


def params_kernel(cls_hbm, flag_hbm, x_hbm, lat_hbm, inv_hbm, weight_ref, out_ref, step_ref, label_ref,
                  cls_ref, flag_ref, x_ref, lat_ref, inv_ref, sems):
    pairs = ((cls_hbm, cls_ref), (flag_hbm, flag_ref), (x_hbm, x_ref), (lat_hbm, lat_ref))
    pairs += ((inv_hbm.at[:, inv_hbm.shape[1] - FACE:, :], inv_ref),)
    copies = [pltpu.make_async_copy(a, b, sems.at[i]) for i, (a, b) in enumerate(pairs)]
    for copy in copies:
        copy.start()
    count, nodes, _ = inv_hbm.shape
    planes = cls_ref.shape[0]
    item, lane = iota((FACE, 128), 0), iota((FACE, 128), 1)
    places = [(lane == 64 + FACE * f + item).astype(BF16) for f in range(4)]
    places.append(((lane < 48) & (lane % FACE == item)).astype(BF16))
    for copy in copies[:2]:
        copy.wait()
    labels = [cls_ref[x] for x in range(planes)]
    labels += [flag_ref[d, x] for d in range(2) for x in range(planes)]
    labels = jnp.concatenate(labels, axis=0).astype(F32).astype(BF16)
    tile = (iota((FACE, 128), 1) % FACE == iota((FACE, 128), 0)).astype(BF16)
    label_ref[...] = dot(labels, tile)
    for copy in copies[2:]:
        copy.wait()
    placed = []
    for f in range(5):
        rows = (lat_ref[f] if f < 4 else x_ref[...]).reshape(count * FACE, FACE)
        placed.append(dot(jnp.concatenate(split(rows), axis=0), places[f]).astype(BF16))
    inv_rows = [inv_ref[k] for k in range(count)]
    gathered = face_columns(jnp.concatenate(inv_rows, axis=0), nodes)
    outs, steps = [], []
    for k in range(count):
        columns = []
        for part in range(2):
            begin = part * count * FACE + k * FACE
            columns.append(jnp.concatenate([p[begin:begin + FACE] for p in placed], axis=0))
        weights = jnp.concatenate(columns, axis=1)
        weight_ref[:, 256 * k:256 * k + 256] = weights
        low = (count + k) * FACE
        products = class_products(gathered[k * FACE:k * FACE + FACE], gathered[low:low + FACE], weights)
        outs.append(with_inverse(inv_rows[k], products))
        steps.append(products)
    out_ref[...] = in_parts(jnp.concatenate(outs, axis=0))
    step_ref[...] = coupling_parts(jnp.concatenate(steps, axis=0))


def picked(label, count):
    wide = (iota((FACE, 256), 1) // FACE == iota((FACE, 256), 0)).astype(BF16)
    on_wide = dot(label[:, :FACE].astype(BF16), wide).astype(jnp.int32)
    row, lane = iota((count * FACE, 256), 0), iota((count * FACE, 256), 1)
    return jnp.where((row % FACE == lane % FACE) & (row // FACE == on_wide), 1.0, 0.0).astype(BF16)


def class_sum(every, label, rows):
    total = None
    for k in range(8):
        term = jnp.where(label == k, every[k * rows:(k + 1) * rows], 0.0)
        total = term if total is None else total + term
    return total


def stacked(value):
    first, second = split(value)
    rest = jnp.zeros((128 - 3 * FACE, value.shape[1]), BF16)
    return jnp.concatenate([first, second, first, rest], axis=0)


def sources_kernel(gy_size, u_ref, rhs_ref, below_ref, above_ref, label_ref, out_ref, step_ref, x_ref, flow_ref, lin_ref, map_ref):
    planes, rows_y, nodes, columns = u_ref.shape
    place = lax.axis_index("gy")
    node, item = iota((nodes, nodes), 1), iota((nodes, nodes), 0)
    chosen = (node == wanted_node(item // FACE, item % FACE)).astype(BF16)
    own = [u_ref[x, y] for x in range(planes) for y in range(rows_y)]
    other = [below_ref[x, below_ref.shape[1] - 1] for x in range(planes)] + [above_ref[x, 0] for x in range(planes)]
    step = step_ref[...]
    row, lane = iota((2 * FACE, 128), 0), iota((2 * FACE, 128), 1)
    flip = (lane == row + FACE * (row >= FACE)).astype(BF16)
    turned = dot_rows(flip, step).astype(BF16)
    faces = dot(chosen, jnp.concatenate(own + other, axis=1))
    picks = []
    for at in range(planes * rows_y):
        picks.append(picked(label_ref[pl.ds(at, 1), :], step.shape[0] // FACE))
    linear = dot(turned, jnp.concatenate(picks, axis=1))
    faces = [faces[:, i * columns:(i + 1) * columns] for i in range(len(own) + len(other))]
    z_at = iota((FACE, columns), 1) % FACE
    has_below = jnp.where(place > 0, 1.0, 0.0)
    has_above = jnp.where(place < gy_size - 1, 1.0, 0.0)
    data = []
    for x in range(planes):
        under = faces[len(own) + x][16:32] * has_below
        over = faces[len(own) + planes + x][0:16] * has_above
        for y in range(rows_y):
            at = x * rows_y + y
            y_flag = label_ref[pl.ds(planes * rows_y + at, 1), :]
            z_flag = label_ref[pl.ds(2 * planes * rows_y + at, 1), :]
            from_below = faces[at - 1][16:32] if y > 0 else under
            from_above = faces[at + 1][0:16] if y < rows_y - 1 else over
            from_front = jnp.where(z_at == 0, 0.0, pltpu.roll(faces[at][48:64], 1, 1))
            from_back = jnp.where(z_at == FACE - 1, 0.0, pltpu.roll(faces[at][32:48], columns - 1, 1))
            lateral = jnp.concatenate(
                [
                    from_below * (1.0 - y_flag),
                    from_above * y_flag,
                    from_front * (1.0 - z_flag),
                    from_back * z_flag,
                ],
                axis=0,
            ).astype(BF16)
            here = jnp.concatenate([rhs_ref[x, y], lateral], axis=0)
            x_ref[x, y] = here
            data.append(here)
    data = jnp.concatenate(data, axis=1)
    every = dot(out_ref[...], jnp.concatenate([data, data], axis=0))
    keep = (iota((256, 256), 0) // FACE == iota((256, 256), 1) // FACE).astype(BF16)
    wholes, pairs = None, None
    for x in range(planes):
        here = [linear[:, at * 256:at * 256 + 256] for at in range(x * rows_y, (x + 1) * rows_y)]
        both = [(part[:FACE].astype(BF16), part[FACE:].astype(BF16)) for part in here]
        for y in range(rows_y):
            lin_ref[x, y] = here[y][:FACE] + here[y][FACE:]
        if wholes is None:
            wholes, pairs = [part[:FACE] + part[FACE:] for part in here], both
        else:
            blocks = [[jnp.concatenate([part] * 16, axis=0) * keep for part in parts] for parts in both]
            stacks = [jnp.concatenate(pair, axis=0) for pair in pairs]
            firsts = [dot(stack, block[0]) for stack, block in zip(stacks, blocks)]
            seconds = [dot(pair[0], block[1]) for pair, block in zip(pairs, blocks)]
            wholes = [first[:FACE] + first[FACE:] + second for first, second in zip(firsts, seconds)]
            pairs = [split(whole) for whole in wholes]
    total = None
    for x in range(planes):
        begin = x * rows_y * columns
        label = jnp.concatenate([label_ref[pl.ds(x * rows_y + y, 1), :] for y in range(rows_y)], axis=1)
        flow = class_sum(every[:, begin:begin + rows_y * columns], label, FACE)
        flow_ref[x] = flow
        if total is not None:
            flow = flow + class_sum(dot(step_ref[...], stacked(total)), label, FACE)
        total = flow
    for y in range(rows_y):
        map_ref[y, 0:FACE] = wholes[y]
        map_ref[y, FACE:] = encode(total[:, y * columns:(y + 1) * columns])


def block_diagonal(linear):
    keep = (iota((256, 256), 0) // FACE == iota((256, 256), 1) // FACE).astype(BF16)
    return [jnp.concatenate([part] * 16, axis=0) * keep for part in split(linear)]


def half_weights(high, low, begin):
    keep = (iota((128, 128), 0) // FACE == iota((128, 128), 1) // FACE).astype(BF16)
    parts = [jnp.concatenate([part[:, begin:begin + 128]] * 8, axis=0) * keep for part in (high, low)]
    return jnp.concatenate(parts, axis=0)


def half_rows(high, low, begin):
    high, low = high[:, begin:begin + 128], low[:, begin:begin + 128]
    upper = jnp.concatenate([high, high], axis=1)
    return jnp.concatenate([upper, jnp.concatenate([low, jnp.zeros_like(low)], axis=1)], axis=0)


def joined_rows(pairs):
    ready = [
        (half_rows(*rows, begin), half_weights(*linear, begin)) for rows, linear in pairs for begin in (0, 128)
    ]
    sums = [dot(rows, weights) for rows, weights in ready]
    sums = [both[:both.shape[0] // 2] + both[both.shape[0] // 2:] for both in sums]
    return [jnp.concatenate(sums[i:i + 2], axis=1) for i in range(0, len(sums), 2)]


def join_many(pairs):
    rest = jnp.zeros((8, 256), F32)
    split_pairs = [(split(jnp.concatenate([first, rest], axis=0)), split(second[:FACE])) for first, second in pairs]
    joined = []
    for total, (_, later) in zip(joined_rows(split_pairs), pairs):
        joined.append(jnp.concatenate([total[:FACE], total[FACE:24] + later[FACE:]], axis=0))
    return joined


def sent_steps(size, first):
    return (2, 1) + tuple(range(3, size)) if first == 2 and size > 2 else tuple(range(1, size))


def advance_many(traces, maps):
    rest = jnp.zeros((8, 256), F32)
    pairs = [(split(jnp.concatenate([trace, rest], axis=0)), split(one[:FACE])) for trace, one in zip(traces, maps)]
    return [total[:8] + one[FACE:] for total, one in zip(joined_rows(pairs), maps)]


def block_slot(mine, other, size, power, first):
    step = (mine ^ other) if power else (mine - other + size) % size
    return step + 1 * (step == 1) - 1 * (step == 2) if first == 2 and size > 2 else step


def group_kernel(size, power, outer, *refs):
    blocks, total_ref, held = refs[:size], refs[size + 1], refs[size + 2]
    place = lax.axis_index("gx")
    mine = place % size
    rows_y = total_ref.shape[0]

    @pl.when(place // size < outer - 1)
    def _():
        for s in range(size):
            held[s] = blocks[s][...]
        slots = [block_slot(mine, j, size, power, 1) for j in range(size)]
        maps = [[held[slot, y] for slot in slots] for y in range(rows_y)]
        while len(maps[0]) > 1:
            length = len(maps[0])
            joined = join_many([(maps[y][i], maps[y][i + 1]) for y in range(rows_y) for i in range(0, length - 1, 2)])
            half = length // 2
            maps = [joined[y * half:y * half + half] + maps[y][2 * half:] for y in range(rows_y)]
        for y in range(rows_y):
            total_ref[y] = maps[y][0]

    @pl.when(place // size == outer - 1)
    def _():
        total_ref[...] = jnp.zeros(total_ref.shape, F32)


def carried(parts, traces, count):
    keep = (iota((128, 256), 0) % FACE == iota((128, 256), 1) // FACE).astype(BF16)
    here = []
    for trace in traces:
        rows = jnp.concatenate([jnp.broadcast_to(trace[t:t + 1], (FACE, 256)) for t in range(8)], axis=0)
        here.append([part * keep for part in split(rows)])
    by_first = [dot_rows(part, data[0]) for part, data in zip(parts, here)]
    by_second = [dot_rows(part[:count], data[1]) for part, data in zip(parts, here)]
    return [first[:count] + first[count:] + second for first, second in zip(by_first, by_second)]


def write_nodes(result_ref, out_ref, sems, base_ref, part_ref, traces):
    planes, rows_y, nodes, _ = result_ref.shape
    sums = carried([part_ref[y] for y in range(rows_y)], traces, planes * nodes)
    copies = []
    for y in range(rows_y):
        for x in range(planes):
            result_ref[x, y] = base_ref[x, y] + sums[y][x * nodes:(x + 1) * nodes]
            copies.append(pltpu.make_async_copy(result_ref.at[x, y], out_ref.at[x, y], sems.at[x, y]))
            copies[-1].start()
    for copy in copies:
        copy.wait()


def local_kernel(data_ref, label_ref, weight_ref, flow_ref, inv_ref, inflow_ref, base_ref, start_ref, chosen_ref, offset_ref, full_ref):
    planes, rows_y, nodes, columns = base_ref.shape
    coupling = jnp.zeros((nodes, 128), F32)
    count = inv_ref.shape[0]
    gathered = face_columns(inv_ref[...].reshape(count * nodes, nodes), nodes)
    for k in range(count):
        inv_rows = inv_ref[k]
        low = (count + k) * nodes
        products = class_products(
            gathered[k * nodes:k * nodes + nodes], gathered[low:low + nodes], weight_ref[:, 256 * k:256 * k + 256]
        )
        here = pl.ds(k * nodes, nodes)
        shifted = pltpu.roll(products, FACE * k, 1) if k else products
        coupling = jnp.where(iota((nodes, 128), 1) // FACE == k, shifted, coupling)
        full_ref[here, :] = in_parts(with_inverse(inv_rows, products))
    coupling = jnp.concatenate(split(coupling), axis=0)
    for y in range(rows_y):
        start_ref[y] = encode(inflow_ref[y])
    for x in range(planes):
        for y in range(rows_y):
            label = label_ref[pl.ds(x * rows_y + y, 1), :]
            data = data_ref[x, y]
            every = dot(full_ref[...], jnp.concatenate([data, data], axis=0))
            base_ref[x, y] = class_sum(every, label, nodes)
            chosen_ref[x, y] = dot(coupling, picked(label, count)).astype(BF16)
            if x < planes - 1:
                offset_ref[x, y] = encode(flow_ref[x, :, y * columns:(y + 1) * columns])


def ahead_kernel(size, power, *refs):
    blocks, ahead_ref, held = refs[:size], refs[size + 1], refs[size + 2]
    rows_y = ahead_ref.shape[0]
    for s in range(size):
        held[s] = blocks[s][...]
    mine = lax.axis_index("gx") % size
    same = (iota((24, 256), 1) % FACE == iota((24, 256), 0)).astype(F32)
    ahead = [same] * rows_y
    for j in range(size - 1):
        slot = block_slot(mine, j, size, power, 1)
        block = [held[slot, y] for y in range(rows_y)]
        joined = block if j == 0 else join_many([(ahead[y], block[y]) for y in range(rows_y)])
        ahead = [jnp.where(mine > j, joined[y], ahead[y]) for y in range(rows_y)]
    for y in range(rows_y):
        ahead_ref[y] = ahead[y]


def carry_kernel(size, swapped, ahead_ref, local_ref, start_ref, chosen_ref, offset_ref, lin_ref, base_ref, part_ref, out_ref, result_ref, sems):
    planes, rows_y, nodes, _ = base_ref.shape
    place = lax.axis_index("gx")
    if swapped:
        ahead_ref = ahead_ref.at[1 - lax.axis_index("gy") % 2]
    row_range = range(rows_y)

    def plane_map(x):
        return [jnp.concatenate([lin_ref[x, y], offset_ref[x, y]], axis=0) for y in row_range]

    @pl.when(place < size)
    def _():
        traces = advance_many([start_ref[y] for y in row_range], [ahead_ref[y] for y in row_range])
        entering = list(traces)
        for x in range(planes - 1):
            traces = advance_many(traces, plane_map(x))
            entering += traces
        sums = carried([chosen_ref[x, y] for x in range(planes) for y in row_range], entering, nodes)
        copies = []
        for x in range(planes):
            for y in row_range:
                result_ref[x, y] = local_ref[x, y] + sums[x * rows_y + y]
                copies.append(pltpu.make_async_copy(result_ref.at[x, y], out_ref.at[x, y], sems.at[x, y]))
                copies[-1].start()
        for copy in copies:
            copy.wait()

    @pl.when(place >= size)
    def _():
        ahead = [ahead_ref[y] for y in row_range]
        for x in range(planes):
            chosen = [chosen_ref[x, y] for y in row_range]
            sums = carried(chosen, [ahead[y][FACE:] for y in row_range], nodes)
            pairs = [block_diagonal(ahead[y][:FACE]) for y in row_range]
            firsts = [dot_rows(chosen[y], pairs[y][0]) for y in row_range]
            seconds = [dot_rows(chosen[y][:nodes], pairs[y][1]) for y in row_range]
            for y in row_range:
                base_ref[x, y] = local_ref[x, y] + sums[y]
                high, low = split(firsts[y][:nodes] + firsts[y][nodes:] + seconds[y])
                part_ref[y, pl.ds(x * nodes, nodes), :] = high
                part_ref[y, pl.ds((planes + x) * nodes, nodes), :] = low
            if x < planes - 1:
                ahead = join_many(list(zip(ahead, plane_map(x))))


def finish_places(places, steps, inner, *refs):
    blocks = refs[:len(steps)]
    start_ref, base_ref, part_ref, _, out_ref, result_ref, sems = refs[len(steps):]
    mine = lax.axis_index("gx") // inner
    for place in places:
        @pl.when(mine == place)
        def _():
            traces = [start_ref[y] for y in range(base_ref.shape[1])]
            for j in range(place):
                block = blocks[steps.index(place ^ j)]
                traces = advance_many(traces, [block[y] for y in range(len(traces))])
            write_nodes(result_ref, out_ref, sems, base_ref, part_ref, traces)


def finish_kernel(size, inner, power, *refs):
    blocks = refs[:size]
    start_ref, base_ref, part_ref, _, out_ref, result_ref, sems = refs[size:size + 7]
    rows_y = base_ref.shape[1]
    mine = lax.axis_index("gx") // inner
    held = refs[size + 7]
    for s in range(size):
        held[s] = blocks[s][...]

    @pl.when(mine > 0)
    def _():
        traces = []
        for y in range(rows_y):
            trace = start_ref[y]
            for j in range(size - 1):
                slot = block_slot(mine, j, size, power, 2)
                trace = jnp.where(mine > j, advance(trace, held[slot, y]), trace)
            traces.append(trace)
        write_nodes(result_ref, out_ref, sems, base_ref, part_ref, traces)


def moved(value, pairs):
    return lax.ppermute(value, ("gx", "gy"), pairs)


def shape(dims, kind=F32):
    return jax.ShapeDtypeStruct(dims, kind)


def call(kernel, outs, name, args, scratch=(), space=pltpu.VMEM, out_spaces=None, aliases=None, limit=48):
    many = isinstance(outs, tuple)
    spaces = out_spaces or ((pltpu.VMEM,) * len(outs) if many else pltpu.VMEM)
    if isinstance(space, tuple):
        in_specs = [pl.BlockSpec(memory_space=one) for one in space]
    else:
        in_specs = [pl.BlockSpec(memory_space=space)] * len(args)
    if many:
        out_specs = tuple(pl.BlockSpec(memory_space=one) for one in spaces)
    else:
        out_specs = pl.BlockSpec(memory_space=spaces)
    return pl.pallas_call(
        kernel,
        out_shape=outs,
        in_specs=in_specs,
        out_specs=out_specs,
        scratch_shapes=list(scratch),
        input_output_aliases=aliases or {},
        name=name,
        cost_estimate=pl.CostEstimate(flops=1000000, bytes_accessed=500000, transcendentals=0),
        compiler_params=pltpu.CompilerParams(vmem_limit_bytes=limit * 1024 * 1024),
    )(*args)


def on_device(gx_size, gy_size, u_old, rhs, classes, flags, inverse, x_face, lateral_faces, inflow):
    planes, rows_y, nodes, columns = u_old.shape
    count = inverse.shape[0]
    everyone = [(x, y) for x in range(gx_size) for y in range(gy_size)]

    def at(x, y):
        return x * gy_size + y

    if gy_size == 2:
        below = above = moved(u_old, [(at(x, y), at(x, 1 - y)) for x, y in everyone])
    else:
        below = moved(u_old[:, rows_y - 1:], [(at(x, y), at(x, y + 1)) for x, y in everyone if y + 1 < gy_size])
        above = moved(u_old[:, :1], [(at(x, y), at(x, y - 1)) for x, y in everyone if y > 0])
    weights, out_rows, step, labels = call(
        params_kernel,
        (
            shape((5 * FACE, count * 256), BF16),
            shape((count * FACE, 256), BF16),
            shape((count * FACE, 128), BF16),
            shape((3 * planes * rows_y, columns)),
        ),
        "class_matrices",
        tuple(
            pltpu.with_memory_space_constraint(value, pltpu.HBM)
            for value in (classes, flags, x_face, lateral_faces, inverse)
        ),
        [
            pltpu.VMEM(classes.shape, jnp.int32),
            pltpu.VMEM(flags.shape, jnp.int32),
            pltpu.VMEM(x_face.shape, F32),
            pltpu.VMEM(lateral_faces.shape, F32),
            pltpu.VMEM((count, FACE, nodes), F32),
            pltpu.SemaphoreType.DMA((5,)),
        ],
        space=pltpu.HBM,
    )
    data, flow, linear, here = call(
        functools.partial(sources_kernel, gy_size),
        (
            shape((planes, rows_y, 128, columns), BF16),
            shape((planes, FACE, rows_y * columns)),
            shape((planes, rows_y, FACE, 256)),
            shape((rows_y, 24, 256)),
        ),
        "sources",
        (u_old, rhs, below, above, labels, out_rows, step),
    )
    inner = 4 if gx_size % 4 == 0 else 1
    outer = gx_size // inner
    power = outer & (outer - 1) == 0
    other = 1 if gy_size % 2 == 0 else 0

    def exchanged(value, step):
        if power or step < inner:
            return moved(value, [(at(x, y), at(x ^ step, y ^ other)) for x, y in everyone])
        return moved(value, [(at(x, y), at((x + step) % gx_size, y ^ other)) for x, y in everyone])

    near = ((exchanged(here, 0) if other else here),) + tuple(exchanged(here, s) for s in sent_steps(inner, 1))
    nodes_shape = (planes, rows_y, nodes, columns)
    writing = [pltpu.VMEM(nodes_shape, F32), pltpu.SemaphoreType.DMA((planes, rows_y))]
    local, start, chosen, offsets = call(
        local_kernel,
        (
            shape(nodes_shape),
            shape((rows_y, 8, 256)),
            shape((planes, rows_y, 2 * nodes, 256), BF16),
            shape((max(planes - 1, 1), rows_y, 8, 256)),
        ),
        "local_solve",
        (data, labels, weights, flow, inverse, inflow),
        [pltpu.VMEM((count * nodes, 256), BF16)],
    )
    total = call(
        functools.partial(group_kernel, inner, True, outer),
        shape((rows_y, 24, 256)),
        "group_maps",
        near + (start,),
        [pltpu.VMEM((inner, rows_y, 24, 256), F32)],
    )
    blocks = [total] + [exchanged(total, s * inner) for s in sent_steps(outer, 2)]
    ahead = call(
        functools.partial(ahead_kernel, inner, True),
        shape((rows_y, 24, 256)),
        "maps_ahead",
        near + (total,),
        [pltpu.VMEM((inner, rows_y, 24, 256), F32)],
    )
    if other:
        couples = [[y, y + 1] for y in range(0, gy_size, 2)]
        ahead = lax.all_gather(ahead, "gy", axis_index_groups=couples)
    base, parts, out = call(
        functools.partial(carry_kernel, inner, other == 1),
        (
            shape(nodes_shape),
            shape((rows_y, 2 * planes * nodes, 256), BF16),
            pltpu.HBM(nodes_shape, F32),
        ),
        "carry_maps",
        (ahead, local, start, chosen, offsets, linear),
        writing,
        out_spaces=(pltpu.VMEM, pltpu.VMEM, pltpu.HBM),
    )
    def written(kernel, name, args, scratch):
        return call(
            kernel,
            pltpu.HBM(nodes_shape, F32),
            name,
            args,
            scratch,
            space=(pltpu.VMEM,) * (len(args) - 1) + (pltpu.HBM,),
            out_spaces=pltpu.HBM,
            aliases={len(args) - 1: 0},
        )

    if power and outer == 4:
        steps = sent_steps(outer, 2)
        early = (3, 1)
        out = written(
            functools.partial(finish_places, (1,), early, inner),
            "finish_second",
            tuple(blocks[1 + steps.index(one)] for one in early) + (start, base, parts, out),
            writing,
        )
        return written(
            functools.partial(finish_places, (2, 3), steps, inner),
            "finish_last",
            tuple(blocks[1:]) + (start, base, parts, out),
            writing,
        )
    return written(
        functools.partial(finish_kernel, outer, inner, power),
        "finish",
        tuple(blocks) + (start, base, parts, out),
        writing + [pltpu.VMEM((outer, rows_y, 24, 256), F32)],
    )


def solution(mesh):
    in_specs = (
        P("gx", "gy", None, None),
        P("gx", "gy", None, None),
        P("gx", "gy", None),
        P(None, "gx", "gy", None),
        P(),
        P(),
        P(),
        P("gy", None, None),
    )
    out_specs = P("gx", "gy", None, None)
    body = functools.partial(on_device, mesh.shape["gx"], mesh.shape["gy"])
    return jax.shard_map(body, mesh=mesh, in_specs=in_specs, out_specs=out_specs, check_vma=False)
```

```python
import functools

import jax
import jax.numpy as jnp
from jax import lax
from jax.experimental import pallas as pl
from jax.experimental.pallas import tpu as pltpu
from jax.sharding import PartitionSpec as P

FACE = 16
HIGH = lax.Precision.HIGHEST
F32 = jnp.float32
BF16 = jnp.bfloat16


def iota(shape, dim):
    return lax.broadcasted_iota(jnp.int32, shape, dim)


def exact(left, right):
    return jnp.dot(left, right, precision=HIGH, preferred_element_type=F32)


def split(value):
    high = value.astype(BF16)
    return high, (value - high.astype(F32)).astype(BF16)


def wanted_node(face, item):
    high, low = item // 4, item % 4
    return jnp.where(face < 2, 16 * high + low + 12 * (face == 1), 16 * high + 4 * low + 3 * (face == 3))


def dot(left, right):
    return jnp.dot(left, right, preferred_element_type=F32)


def dot_rows(left, right):
    return lax.dot_general(left, right, (((1,), (1,)), ((), ())), preferred_element_type=F32)


def applied(rows, linear):
    lane = iota((rows.shape[0], 128), 1)
    halves = []
    for begin in (0, 128):
        part, total = rows[:, begin:begin + 128], None
        for b in range(FACE):
            near = jnp.take_along_axis(part, lane // FACE * FACE + b, axis=1, mode="promise_in_bounds")
            term = near * linear[b:b + 1, begin:begin + 128]
            total = term if total is None else total + term
        halves.append(total)
    return jnp.concatenate(halves, axis=1)


def join(earlier, later):
    moved_rows = applied(earlier, later[:FACE])
    return jnp.concatenate([moved_rows[:FACE], moved_rows[FACE:] + later[FACE:]], axis=0)


def advance(trace, later):
    return applied(trace, later[:FACE]) + later[FACE:]


def encode(value):
    keep = (iota((256, 128), 0) // FACE == iota((256, 128), 1) % FACE).astype(BF16)
    spread = [jnp.concatenate([part] * 16, axis=0) * keep for part in split(value)]
    gather = (iota((8, 256), 1) % 128 // FACE == iota((8, 256), 0)).astype(BF16)
    return dot_rows(gather, jnp.concatenate(spread, axis=1))


def face_columns(inv_rows, nodes):
    at = iota((nodes, 5 * FACE), 1)
    wanted = jnp.where(at < 64, wanted_node(at // FACE, at % FACE), at - 64)
    chosen = (iota((nodes, 5 * FACE), 0) == wanted).astype(BF16)
    return dot(jnp.concatenate(split(inv_rows), axis=0), chosen).astype(BF16)


def class_products(high, low, weights):
    count = high.shape[0]
    parts = dot(jnp.concatenate([high, low], axis=0), weights)
    return -(parts[:count, :128] + parts[:count, 128:] + parts[count:, :128])


def with_inverse(inv_rows, products):
    count = inv_rows.shape[0]
    wide = jnp.concatenate([inv_rows, jnp.zeros((count, 128 - inv_rows.shape[1]), F32)], axis=1)
    return jnp.where(iota((count, 128), 1) < 64, wide, products)


def in_parts(value):
    high, low = split(value)
    return jnp.concatenate([high, low], axis=1)


def coupling_parts(products):
    high, low = split(products)
    lane = iota(products.shape, 1)
    return jnp.where(lane < 32, high.astype(F32), jnp.where(lane < 48, low.astype(F32), 0.0)).astype(BF16)


def params_kernel(cls_hbm, flag_hbm, x_hbm, lat_hbm, inv_hbm, weight_ref, out_ref, step_ref, label_ref,
                  cls_ref, flag_ref, x_ref, lat_ref, inv_ref, sems):
    pairs = ((cls_hbm, cls_ref), (flag_hbm, flag_ref), (x_hbm, x_ref), (lat_hbm, lat_ref))
    pairs += ((inv_hbm.at[:, inv_hbm.shape[1] - FACE:, :], inv_ref),)
    copies = [pltpu.make_async_copy(a, b, sems.at[i]) for i, (a, b) in enumerate(pairs)]
    for copy in copies[::-1]:
        copy.start()
    count, nodes, _ = inv_hbm.shape
    planes = cls_ref.shape[0]
    item, lane = iota((FACE, 128), 0), iota((FACE, 128), 1)
    places = [(lane == 64 + FACE * f + item).astype(BF16) for f in range(4)]
    places.append(((lane < 48) & (lane % FACE == item)).astype(BF16))
    for copy in copies[:2]:
        copy.wait()
    labels = [cls_ref[x] for x in range(planes)]
    labels += [flag_ref[d, x] for d in range(2) for x in range(planes)]
    labels = jnp.concatenate(labels, axis=0).astype(F32).astype(BF16)
    tile = (iota((FACE, 128), 1) % FACE == iota((FACE, 128), 0)).astype(BF16)
    label_ref[...] = dot(labels, tile)
    for copy in copies[2:]:
        copy.wait()
    placed = []
    for f in range(5):
        rows = (lat_ref[f] if f < 4 else x_ref[...]).reshape(count * FACE, FACE)
        placed.append(dot(jnp.concatenate(split(rows), axis=0), places[f]).astype(BF16))
    inv_rows = [inv_ref[k] for k in range(count)]
    gathered = face_columns(jnp.concatenate(inv_rows, axis=0), nodes)
    outs, steps = [], []
    for k in range(count):
        columns = []
        for part in range(2):
            begin = part * count * FACE + k * FACE
            columns.append(jnp.concatenate([p[begin:begin + FACE] for p in placed], axis=0))
        weights = jnp.concatenate(columns, axis=1)
        weight_ref[:, 256 * k:256 * k + 256] = weights
        low = (count + k) * FACE
        products = class_products(gathered[k * FACE:k * FACE + FACE], gathered[low:low + FACE], weights)
        outs.append(with_inverse(inv_rows[k], products))
        steps.append(products)
    out_ref[...] = in_parts(jnp.concatenate(outs, axis=0))
    step_ref[...] = coupling_parts(jnp.concatenate(steps, axis=0))


def picked(label, count):
    wide = (iota((FACE, 256), 1) // FACE == iota((FACE, 256), 0)).astype(BF16)
    on_wide = dot(label[:, :FACE].astype(BF16), wide).astype(jnp.int32)
    row, lane = iota((count * FACE, 256), 0), iota((count * FACE, 256), 1)
    return jnp.where((row % FACE == lane % FACE) & (row // FACE == on_wide), 1.0, 0.0).astype(BF16)


def class_sum(every, label, rows):
    total = None
    for k in range(8):
        term = jnp.where(label == k, every[k * rows:(k + 1) * rows], 0.0)
        total = term if total is None else total + term
    return total


def stacked(value):
    first, second = split(value)
    rest = jnp.zeros((128 - 3 * FACE, value.shape[1]), BF16)
    return jnp.concatenate([first, second, first, rest], axis=0)


def sources_kernel(gx_size, gy_size, *refs):
    place = lax.axis_index("gx")

    @pl.when(place < gx_size - 1)
    def _():
        gather_sources(gy_size, True, *refs)

    @pl.when(place == gx_size - 1)
    def _():
        gather_sources(gy_size, False, *refs)


def gather_sources(gy_size, mapped, u_ref, rhs_ref, below_ref, above_ref, label_ref, out_ref, step_ref, x_ref, flow_ref, lin_ref, map_ref):
    planes, rows_y, nodes, columns = u_ref.shape
    place = lax.axis_index("gy")
    node, item = iota((nodes, nodes), 1), iota((nodes, nodes), 0)
    chosen = (node == wanted_node(item // FACE, item % FACE)).astype(BF16)
    own = [u_ref[x, y] for x in range(planes) for y in range(rows_y)]
    other = [below_ref[x, below_ref.shape[1] - 1] for x in range(planes)] + [above_ref[x, 0] for x in range(planes)]
    step = step_ref[...]
    row, lane = iota((2 * FACE, 128), 0), iota((2 * FACE, 128), 1)
    flip = (lane == row + FACE * (row >= FACE)).astype(BF16)
    turned = dot_rows(flip, step).astype(BF16)
    faces = dot(chosen, jnp.concatenate(own + other, axis=1))
    picks = []
    for at in range(planes * rows_y):
        picks.append(picked(label_ref[pl.ds(at, 1), :], step.shape[0] // FACE))
    linear = dot(turned, jnp.concatenate(picks, axis=1))
    faces = [faces[:, i * columns:(i + 1) * columns] for i in range(len(own) + len(other))]
    z_at = iota((FACE, columns), 1) % FACE
    has_below = jnp.where(place > 0, 1.0, 0.0)
    has_above = jnp.where(place < gy_size - 1, 1.0, 0.0)
    data = []
    for x in range(planes):
        under = faces[len(own) + x][16:32] * has_below
        over = faces[len(own) + planes + x][0:16] * has_above
        for y in range(rows_y):
            at = x * rows_y + y
            y_flag = label_ref[pl.ds(planes * rows_y + at, 1), :]
            z_flag = label_ref[pl.ds(2 * planes * rows_y + at, 1), :]
            from_below = faces[at - 1][16:32] if y > 0 else under
            from_above = faces[at + 1][0:16] if y < rows_y - 1 else over
            from_front = jnp.where(z_at == 0, 0.0, pltpu.roll(faces[at][48:64], 1, 1))
            from_back = jnp.where(z_at == FACE - 1, 0.0, pltpu.roll(faces[at][32:48], columns - 1, 1))
            lateral = jnp.concatenate(
                [
                    from_below * (1.0 - y_flag),
                    from_above * y_flag,
                    from_front * (1.0 - z_flag),
                    from_back * z_flag,
                ],
                axis=0,
            ).astype(BF16)
            here = jnp.concatenate([rhs_ref[x, y], lateral], axis=0)
            x_ref[x, y] = here
            data.append(here)
    data = jnp.concatenate(data, axis=1)
    every = dot(out_ref[...], jnp.concatenate([data, data], axis=0))
    keep = (iota((256, 256), 0) // FACE == iota((256, 256), 1) // FACE).astype(BF16)
    wholes, pairs = None, None
    for x in range(planes):
        here = [linear[:, at * 256:at * 256 + 256] for at in range(x * rows_y, (x + 1) * rows_y)]
        both = [(part[:FACE].astype(BF16), part[FACE:].astype(BF16)) for part in here]
        for y in range(rows_y):
            lin_ref[x, y] = here[y][:FACE] + here[y][FACE:]
        if wholes is None:
            wholes, pairs = [part[:FACE] + part[FACE:] for part in here], both
        elif mapped:
            blocks = [[jnp.concatenate([part] * 16, axis=0) * keep for part in parts] for parts in both]
            stacks = [jnp.concatenate(pair, axis=0) for pair in pairs]
            firsts = [dot(stack, block[0]) for stack, block in zip(stacks, blocks)]
            seconds = [dot(pair[0], block[1]) for pair, block in zip(pairs, blocks)]
            wholes = [first[:FACE] + first[FACE:] + second for first, second in zip(firsts, seconds)]
            pairs = [split(whole) for whole in wholes]
    total = None
    for x in range(planes):
        begin = x * rows_y * columns
        label = jnp.concatenate([label_ref[pl.ds(x * rows_y + y, 1), :] for y in range(rows_y)], axis=1)
        flow = class_sum(every[:, begin:begin + rows_y * columns], label, FACE)
        flow_ref[x] = flow
        if total is not None and (mapped or x < planes - 1):
            flow = flow + class_sum(dot(step_ref[...], stacked(total)), label, FACE)
        total = flow
    if not mapped:
        map_ref[...] = jnp.zeros(map_ref.shape, F32)
        return
    for y in range(rows_y):
        map_ref[y, 0:FACE] = wholes[y]
        map_ref[y, FACE:] = encode(total[:, y * columns:(y + 1) * columns])


def block_diagonal(linear):
    keep = (iota((256, 256), 0) // FACE == iota((256, 256), 1) // FACE).astype(BF16)
    return [jnp.concatenate([part] * 16, axis=0) * keep for part in split(linear)]


def half_weights(high, low, begin):
    keep = (iota((128, 128), 0) // FACE == iota((128, 128), 1) // FACE).astype(BF16)
    parts = [jnp.concatenate([part[:, begin:begin + 128]] * 8, axis=0) * keep for part in (high, low)]
    return jnp.concatenate(parts, axis=0)


def half_rows(high, low, begin):
    high, low = high[:, begin:begin + 128], low[:, begin:begin + 128]
    upper = jnp.concatenate([high, high], axis=1)
    return jnp.concatenate([upper, jnp.concatenate([low, jnp.zeros_like(low)], axis=1)], axis=0)


def joined_rows(pairs):
    ready = [
        (half_rows(*rows, begin), half_weights(*linear, begin)) for rows, linear in pairs for begin in (0, 128)
    ]
    sums = [dot(rows, weights) for rows, weights in ready]
    sums = [both[:both.shape[0] // 2] + both[both.shape[0] // 2:] for both in sums]
    return [jnp.concatenate(sums[i:i + 2], axis=1) for i in range(0, len(sums), 2)]


def join_many(pairs):
    rest = jnp.zeros((8, 256), F32)
    split_pairs = [(split(jnp.concatenate([first, rest], axis=0)), split(second[:FACE])) for first, second in pairs]
    joined = []
    for total, (_, later) in zip(joined_rows(split_pairs), pairs):
        joined.append(jnp.concatenate([total[:FACE], total[FACE:24] + later[FACE:]], axis=0))
    return joined


def sent_steps(size, first):
    if first == 2:
        return (2, 1) + tuple(range(3, size)) if size > 2 else tuple(range(1, size))
    return (1, 3, 2) + tuple(range(4, size)) if size > 3 else tuple(range(1, size))


def advance_many(traces, maps):
    rest = jnp.zeros((8, 256), F32)
    pairs = [(split(jnp.concatenate([trace, rest], axis=0)), split(one[:FACE])) for trace, one in zip(traces, maps)]
    return [total[:8] + one[FACE:] for total, one in zip(joined_rows(pairs), maps)]


def block_slot(mine, other, size, power, first):
    step = (mine ^ other) if power else (mine - other + size) % size
    if first == 2:
        return step + 1 * (step == 1) - 1 * (step == 2) if size > 2 else step
    return step + 1 * (step == 2) - 1 * (step == 3) if size > 3 else step


def group_kernel(size, power, outer, *refs):
    blocks, total_ref, held = refs[:size], refs[size + 1], refs[size + 2]
    place = lax.axis_index("gx")
    mine = place % size
    rows_y = total_ref.shape[0]

    @pl.when(place // size < outer - 1)
    def _():
        for s in range(size):
            held[s] = blocks[s][...]
        slots = [block_slot(mine, j, size, power, 1) for j in range(size)]
        maps = [[held[slot, y] for slot in slots] for y in range(rows_y)]
        while len(maps[0]) > 1:
            length = len(maps[0])
            joined = join_many([(maps[y][i], maps[y][i + 1]) for y in range(rows_y) for i in range(0, length - 1, 2)])
            half = length // 2
            maps = [joined[y * half:y * half + half] + maps[y][2 * half:] for y in range(rows_y)]
        for y in range(rows_y):
            total_ref[y] = maps[y][0]

    @pl.when(place // size == outer - 1)
    def _():
        total_ref[...] = jnp.zeros(total_ref.shape, F32)


def carried(parts, traces, count):
    keep = (iota((128, 256), 0) % FACE == iota((128, 256), 1) // FACE).astype(BF16)
    here = []
    for trace in traces:
        rows = jnp.concatenate([jnp.broadcast_to(trace[t:t + 1], (FACE, 256)) for t in range(8)], axis=0)
        here.append([part * keep for part in split(rows)])
    by_first = [dot_rows(part, data[0]) for part, data in zip(parts, here)]
    by_second = [dot_rows(part[:count], data[1]) for part, data in zip(parts, here)]
    return [first[:count] + first[count:] + second for first, second in zip(by_first, by_second)]


def write_nodes(result_ref, out_ref, sems, base_ref, part_ref, traces):
    planes, rows_y, nodes, _ = result_ref.shape
    sums = carried([part_ref[y] for y in range(rows_y)], traces, planes * nodes)
    copies = []
    for y in range(rows_y):
        for x in range(planes):
            result_ref[x, y] = base_ref[x, y] + sums[y][x * nodes:(x + 1) * nodes]
            copies.append(pltpu.make_async_copy(result_ref.at[x, y], out_ref.at[x, y], sems.at[x, y]))
            copies[-1].start()
    for copy in copies:
        copy.wait()


def local_kernel(data_ref, label_ref, weight_ref, flow_ref, inv_ref, inflow_ref, base_ref, start_ref, chosen_ref, offset_ref, full_ref):
    planes, rows_y, nodes, columns = base_ref.shape
    coupling = jnp.zeros((nodes, 128), F32)
    count = inv_ref.shape[0]
    gathered = face_columns(inv_ref[...].reshape(count * nodes, nodes), nodes)
    for k in range(count):
        inv_rows = inv_ref[k]
        low = (count + k) * nodes
        products = class_products(
            gathered[k * nodes:k * nodes + nodes], gathered[low:low + nodes], weight_ref[:, 256 * k:256 * k + 256]
        )
        here = pl.ds(k * nodes, nodes)
        shifted = pltpu.roll(products, FACE * k, 1) if k else products
        coupling = jnp.where(iota((nodes, 128), 1) // FACE == k, shifted, coupling)
        full_ref[here, :] = in_parts(with_inverse(inv_rows, products))
    coupling = jnp.concatenate(split(coupling), axis=0)
    for y in range(rows_y):
        start_ref[y] = encode(inflow_ref[y])
    for x in range(planes):
        for y in range(rows_y):
            label = label_ref[pl.ds(x * rows_y + y, 1), :]
            data = data_ref[x, y]
            every = dot(full_ref[...], jnp.concatenate([data, data], axis=0))
            base_ref[x, y] = class_sum(every, label, nodes)
            chosen_ref[x, y] = dot(coupling, picked(label, count)).astype(BF16)
            if x < planes - 1:
                offset_ref[x, y] = encode(flow_ref[x, :, y * columns:(y + 1) * columns])


def ahead_kernel(size, power, *refs):
    blocks, ahead_ref, held = refs[:size], refs[size + 1], refs[size + 2]
    rows_y = ahead_ref.shape[0]
    for s in range(size):
        held[s] = blocks[s][...]
    mine = lax.axis_index("gx") % size
    same = (iota((24, 256), 1) % FACE == iota((24, 256), 0)).astype(F32)
    ahead = [same] * rows_y
    for j in range(size - 1):
        slot = block_slot(mine, j, size, power, 1)
        block = [held[slot, y] for y in range(rows_y)]
        joined = block if j == 0 else join_many([(ahead[y], block[y]) for y in range(rows_y)])
        ahead = [jnp.where(mine > j, joined[y], ahead[y]) for y in range(rows_y)]
    for y in range(rows_y):
        ahead_ref[y] = ahead[y]


def carry_kernel(size, swapped, ahead_ref, local_ref, start_ref, chosen_ref, offset_ref, lin_ref, base_ref, part_ref, out_ref, result_ref, sems):
    planes, rows_y, nodes, _ = base_ref.shape
    place = lax.axis_index("gx")
    if swapped:
        ahead_ref = ahead_ref.at[1 - lax.axis_index("gy") % 2]
    row_range = range(rows_y)

    def plane_map(x):
        return [jnp.concatenate([lin_ref[x, y], offset_ref[x, y]], axis=0) for y in row_range]

    @pl.when(place < size)
    def _():
        traces = advance_many([start_ref[y] for y in row_range], [ahead_ref[y] for y in row_range])
        entering = list(traces)
        for x in range(planes - 1):
            traces = advance_many(traces, plane_map(x))
            entering += traces
        sums = carried([chosen_ref[x, y] for x in range(planes) for y in row_range], entering, nodes)
        copies = []
        for x in range(planes):
            for y in row_range:
                result_ref[x, y] = local_ref[x, y] + sums[x * rows_y + y]
                copies.append(pltpu.make_async_copy(result_ref.at[x, y], out_ref.at[x, y], sems.at[x, y]))
                copies[-1].start()
        for copy in copies:
            copy.wait()

    @pl.when(place >= size)
    def _():
        ahead = [ahead_ref[y] for y in row_range]
        for x in range(planes):
            chosen = [chosen_ref[x, y] for y in row_range]
            sums = carried(chosen, [ahead[y][FACE:] for y in row_range], nodes)
            pairs = [block_diagonal(ahead[y][:FACE]) for y in row_range]
            firsts = [dot_rows(chosen[y], pairs[y][0]) for y in row_range]
            seconds = [dot_rows(chosen[y][:nodes], pairs[y][1]) for y in row_range]
            for y in row_range:
                base_ref[x, y] = local_ref[x, y] + sums[y]
                high, low = split(firsts[y][:nodes] + firsts[y][nodes:] + seconds[y])
                part_ref[y, pl.ds(x * nodes, nodes), :] = high
                part_ref[y, pl.ds((planes + x) * nodes, nodes), :] = low
            if x < planes - 1:
                ahead = join_many(list(zip(ahead, plane_map(x))))


def finish_places(places, steps, inner, *refs):
    blocks = refs[:len(steps)]
    start_ref, base_ref, part_ref, _, out_ref, result_ref, sems = refs[len(steps):]
    mine = lax.axis_index("gx") // inner
    for place in places:
        @pl.when(mine == place)
        def _():
            traces = [start_ref[y] for y in range(base_ref.shape[1])]
            for j in range(place):
                block = blocks[steps.index(place ^ j)]
                traces = advance_many(traces, [block[y] for y in range(len(traces))])
            write_nodes(result_ref, out_ref, sems, base_ref, part_ref, traces)


def finish_kernel(size, inner, power, *refs):
    blocks = refs[:size]
    start_ref, base_ref, part_ref, _, out_ref, result_ref, sems = refs[size:size + 7]
    rows_y = base_ref.shape[1]
    mine = lax.axis_index("gx") // inner
    held = refs[size + 7]
    for s in range(size):
        held[s] = blocks[s][...]

    @pl.when(mine > 0)
    def _():
        traces = []
        for y in range(rows_y):
            trace = start_ref[y]
            for j in range(size - 1):
                slot = block_slot(mine, j, size, power, 2)
                trace = jnp.where(mine > j, advance(trace, held[slot, y]), trace)
            traces.append(trace)
        write_nodes(result_ref, out_ref, sems, base_ref, part_ref, traces)


def moved(value, pairs):
    return lax.ppermute(value, ("gx", "gy"), pairs)


def shape(dims, kind=F32):
    return jax.ShapeDtypeStruct(dims, kind)


def call(kernel, outs, name, args, scratch=(), space=pltpu.VMEM, out_spaces=None, aliases=None, limit=48):
    many = isinstance(outs, tuple)
    spaces = out_spaces or ((pltpu.VMEM,) * len(outs) if many else pltpu.VMEM)
    if isinstance(space, tuple):
        in_specs = [pl.BlockSpec(memory_space=one) for one in space]
    else:
        in_specs = [pl.BlockSpec(memory_space=space)] * len(args)
    if many:
        out_specs = tuple(pl.BlockSpec(memory_space=one) for one in spaces)
    else:
        out_specs = pl.BlockSpec(memory_space=spaces)
    return pl.pallas_call(
        kernel,
        out_shape=outs,
        in_specs=in_specs,
        out_specs=out_specs,
        scratch_shapes=list(scratch),
        input_output_aliases=aliases or {},
        name=name,
        cost_estimate=pl.CostEstimate(flops=1000000, bytes_accessed=500000, transcendentals=0),
        compiler_params=pltpu.CompilerParams(vmem_limit_bytes=limit * 1024 * 1024),
    )(*args)


def on_device(gx_size, gy_size, u_old, rhs, classes, flags, inverse, x_face, lateral_faces, inflow):
    planes, rows_y, nodes, columns = u_old.shape
    count = inverse.shape[0]
    everyone = [(x, y) for x in range(gx_size) for y in range(gy_size)]

    def at(x, y):
        return x * gy_size + y

    if gy_size == 2:
        below = above = moved(u_old, [(at(x, y), at(x, 1 - y)) for x, y in everyone])
    else:
        below = moved(u_old[:, rows_y - 1:], [(at(x, y), at(x, y + 1)) for x, y in everyone if y + 1 < gy_size])
        above = moved(u_old[:, :1], [(at(x, y), at(x, y - 1)) for x, y in everyone if y > 0])
    weights, out_rows, step, labels = call(
        params_kernel,
        (
            shape((5 * FACE, count * 256), BF16),
            shape((count * FACE, 256), BF16),
            shape((count * FACE, 128), BF16),
            shape((3 * planes * rows_y, columns)),
        ),
        "class_matrices",
        tuple(
            pltpu.with_memory_space_constraint(value, pltpu.HBM)
            for value in (classes, flags, x_face, lateral_faces, inverse)
        ),
        [
            pltpu.VMEM(classes.shape, jnp.int32),
            pltpu.VMEM(flags.shape, jnp.int32),
            pltpu.VMEM(x_face.shape, F32),
            pltpu.VMEM(lateral_faces.shape, F32),
            pltpu.VMEM((count, FACE, nodes), F32),
            pltpu.SemaphoreType.DMA((5,)),
        ],
        space=pltpu.HBM,
    )
    data, flow, linear, here = call(
        functools.partial(sources_kernel, gx_size, gy_size),
        (
            shape((planes, rows_y, 128, columns), BF16),
            shape((planes, FACE, rows_y * columns)),
            shape((planes, rows_y, FACE, 256)),
            shape((rows_y, 24, 256)),
        ),
        "sources",
        (u_old, rhs, below, above, labels, out_rows, step),
    )
    inner = 4 if gx_size % 4 == 0 else 1
    outer = gx_size // inner
    power = outer & (outer - 1) == 0
    other = 1 if gy_size % 2 == 0 else 0

    def exchanged(value, step):
        if power or step < inner:
            return moved(value, [(at(x, y), at(x ^ step, y ^ other)) for x, y in everyone])
        return moved(value, [(at(x, y), at((x + step) % gx_size, y ^ other)) for x, y in everyone])

    near = ((exchanged(here, 0) if other else here),) + tuple(exchanged(here, s) for s in sent_steps(inner, 1))
    nodes_shape = (planes, rows_y, nodes, columns)
    writing = [pltpu.VMEM(nodes_shape, F32), pltpu.SemaphoreType.DMA((planes, rows_y))]
    local, start, chosen, offsets = call(
        local_kernel,
        (
            shape(nodes_shape),
            shape((rows_y, 8, 256)),
            shape((planes, rows_y, 2 * nodes, 256), BF16),
            shape((max(planes - 1, 1), rows_y, 8, 256)),
        ),
        "local_solve",
        (data, labels, weights, flow, inverse, inflow),
        [pltpu.VMEM((count * nodes, 256), BF16)],
    )
    total = call(
        functools.partial(group_kernel, inner, True, outer),
        shape((rows_y, 24, 256)),
        "group_maps",
        near + (start,),
        [pltpu.VMEM((inner, rows_y, 24, 256), F32)],
    )
    blocks = [total] + [exchanged(total, s * inner) for s in sent_steps(outer, 2)]
    ahead = call(
        functools.partial(ahead_kernel, inner, True),
        shape((rows_y, 24, 256)),
        "maps_ahead",
        near + (total,),
        [pltpu.VMEM((inner, rows_y, 24, 256), F32)],
    )
    if other:
        couples = [[y, y + 1] for y in range(0, gy_size, 2)]
        ahead = lax.all_gather(ahead, "gy", axis_index_groups=couples)
    base, parts, out = call(
        functools.partial(carry_kernel, inner, other == 1),
        (
            shape(nodes_shape),
            shape((rows_y, 2 * planes * nodes, 256), BF16),
            pltpu.HBM(nodes_shape, F32),
        ),
        "carry_maps",
        (ahead, local, start, chosen, offsets, linear),
        writing,
        out_spaces=(pltpu.VMEM, pltpu.VMEM, pltpu.HBM),
    )
    def written(kernel, name, args, scratch):
        return call(
            kernel,
            pltpu.HBM(nodes_shape, F32),
            name,
            args,
            scratch,
            space=(pltpu.VMEM,) * (len(args) - 1) + (pltpu.HBM,),
            out_spaces=pltpu.HBM,
            aliases={len(args) - 1: 0},
        )

    if power and outer == 4:
        steps = sent_steps(outer, 2)
        early = (3, 1)
        out = written(
            functools.partial(finish_places, (1,), early, inner),
            "finish_second",
            tuple(blocks[1 + steps.index(one)] for one in early) + (start, base, parts, out),
            writing,
        )
        return written(
            functools.partial(finish_places, (2, 3), steps, inner),
            "finish_last",
            tuple(blocks[1:]) + (start, base, parts, out),
            writing,
        )
    return written(
        functools.partial(finish_kernel, outer, inner, power),
        "finish",
        tuple(blocks) + (start, base, parts, out),
        writing + [pltpu.VMEM((outer, rows_y, 24, 256), F32)],
    )


def solution(mesh):
    in_specs = (
        P("gx", "gy", None, None),
        P("gx", "gy", None, None),
        P("gx", "gy", None),
        P(None, "gx", "gy", None),
        P(),
        P(),
        P(),
        P("gy", None, None),
    )
    out_specs = P("gx", "gy", None, None)
    body = functools.partial(on_device, mesh.shape["gx"], mesh.shape["gy"])
    return jax.shard_map(body, mesh=mesh, in_specs=in_specs, out_specs=out_specs, check_vma=False)
```

```python
import functools

import jax
import jax.numpy as jnp
from jax import lax
from jax.experimental import pallas as pl
from jax.experimental.pallas import tpu as pltpu
from jax.sharding import PartitionSpec as P

FACE = 16
HIGH = lax.Precision.HIGHEST
F32 = jnp.float32
BF16 = jnp.bfloat16


def iota(shape, dim):
    return lax.broadcasted_iota(jnp.int32, shape, dim)


def exact(left, right):
    return jnp.dot(left, right, precision=HIGH, preferred_element_type=F32)


def split(value):
    high = value.astype(BF16)
    return high, (value - high.astype(F32)).astype(BF16)


def wanted_node(face, item):
    high, low = item // 4, item % 4
    return jnp.where(face < 2, 16 * high + low + 12 * (face == 1), 16 * high + 4 * low + 3 * (face == 3))


def dot(left, right):
    return jnp.dot(left, right, preferred_element_type=F32)


def dot_rows(left, right):
    return lax.dot_general(left, right, (((1,), (1,)), ((), ())), preferred_element_type=F32)


def applied(rows, linear):
    lane = iota((rows.shape[0], 128), 1)
    halves = []
    for begin in (0, 128):
        part, total = rows[:, begin:begin + 128], None
        for b in range(FACE):
            near = jnp.take_along_axis(part, lane // FACE * FACE + b, axis=1, mode="promise_in_bounds")
            term = near * linear[b:b + 1, begin:begin + 128]
            total = term if total is None else total + term
        halves.append(total)
    return jnp.concatenate(halves, axis=1)


def join(earlier, later):
    moved_rows = applied(earlier, later[:FACE])
    return jnp.concatenate([moved_rows[:FACE], moved_rows[FACE:] + later[FACE:]], axis=0)


def advance(trace, later):
    return applied(trace, later[:FACE]) + later[FACE:]


def encode(value):
    keep = (iota((256, 128), 0) // FACE == iota((256, 128), 1) % FACE).astype(BF16)
    spread = [jnp.concatenate([part] * 16, axis=0) * keep for part in split(value)]
    gather = (iota((8, 256), 1) % 128 // FACE == iota((8, 256), 0)).astype(BF16)
    return dot_rows(gather, jnp.concatenate(spread, axis=1))


def face_columns(inv_rows, nodes):
    at = iota((nodes, 5 * FACE), 1)
    wanted = jnp.where(at < 64, wanted_node(at // FACE, at % FACE), at - 64)
    chosen = (iota((nodes, 5 * FACE), 0) == wanted).astype(BF16)
    return dot(jnp.concatenate(split(inv_rows), axis=0), chosen).astype(BF16)


def class_products(high, low, weights):
    count = high.shape[0]
    parts = dot(jnp.concatenate([high, low], axis=0), weights)
    return -(parts[:count, :128] + parts[:count, 128:] + parts[count:, :128])


def with_inverse(inv_rows, products):
    count = inv_rows.shape[0]
    wide = jnp.concatenate([inv_rows, jnp.zeros((count, 128 - inv_rows.shape[1]), F32)], axis=1)
    return jnp.where(iota((count, 128), 1) < 64, wide, products)


def in_parts(value):
    high, low = split(value)
    return jnp.concatenate([high, low], axis=1)


def coupling_parts(products):
    high, low = split(products)
    lane = iota(products.shape, 1)
    return jnp.where(lane < 32, high.astype(F32), jnp.where(lane < 48, low.astype(F32), 0.0)).astype(BF16)


def params_kernel(cls_hbm, flag_hbm, x_hbm, lat_hbm, inv_hbm, weight_ref, out_ref, step_ref, label_ref,
                  cls_ref, flag_ref, x_ref, lat_ref, inv_ref, sems):
    pairs = ((cls_hbm, cls_ref), (flag_hbm, flag_ref), (x_hbm, x_ref), (lat_hbm, lat_ref))
    pairs += ((inv_hbm.at[:, inv_hbm.shape[1] - FACE:, :], inv_ref),)
    copies = [pltpu.make_async_copy(a, b, sems.at[i]) for i, (a, b) in enumerate(pairs)]
    for copy in copies:
        copy.start()
    count, nodes, _ = inv_hbm.shape
    planes = cls_ref.shape[0]
    item, lane = iota((FACE, 128), 0), iota((FACE, 128), 1)
    places = [(lane == 64 + FACE * f + item).astype(BF16) for f in range(4)]
    places.append(((lane < 48) & (lane % FACE == item)).astype(BF16))
    for copy in copies[:2]:
        copy.wait()
    labels = [cls_ref[x] for x in range(planes)]
    labels += [flag_ref[d, x] for d in range(2) for x in range(planes)]
    labels = jnp.concatenate(labels, axis=0).astype(F32).astype(BF16)
    tile = (iota((FACE, 128), 1) % FACE == iota((FACE, 128), 0)).astype(BF16)
    label_ref[...] = dot(labels, tile)
    for copy in copies[2:]:
        copy.wait()
    placed = []
    for f in range(5):
        rows = (lat_ref[f] if f < 4 else x_ref[...]).reshape(count * FACE, FACE)
        placed.append(dot(jnp.concatenate(split(rows), axis=0), places[f]).astype(BF16))
    inv_rows = [inv_ref[k] for k in range(count)]
    gathered = face_columns(jnp.concatenate(inv_rows, axis=0), nodes)
    outs, steps = [], []
    for k in range(count):
        columns = []
        for part in range(2):
            begin = part * count * FACE + k * FACE
            columns.append(jnp.concatenate([p[begin:begin + FACE] for p in placed], axis=0))
        weights = jnp.concatenate(columns, axis=1)
        weight_ref[:, 256 * k:256 * k + 256] = weights
        low = (count + k) * FACE
        products = class_products(gathered[k * FACE:k * FACE + FACE], gathered[low:low + FACE], weights)
        outs.append(with_inverse(inv_rows[k], products))
        steps.append(products)
    out_ref[...] = in_parts(jnp.concatenate(outs, axis=0))
    step_ref[...] = coupling_parts(jnp.concatenate(steps, axis=0))


def picked(label, count):
    wide = (iota((FACE, 256), 1) // FACE == iota((FACE, 256), 0)).astype(BF16)
    on_wide = dot(label[:, :FACE].astype(BF16), wide).astype(jnp.int32)
    row, lane = iota((count * FACE, 256), 0), iota((count * FACE, 256), 1)
    return jnp.where((row % FACE == lane % FACE) & (row // FACE == on_wide), 1.0, 0.0).astype(BF16)


def class_sum(every, label, rows):
    total = None
    for k in range(8):
        term = jnp.where(label == k, every[k * rows:(k + 1) * rows], 0.0)
        total = term if total is None else total + term
    return total


def stacked(value):
    first, second = split(value)
    rest = jnp.zeros((128 - 3 * FACE, value.shape[1]), BF16)
    return jnp.concatenate([first, second, first, rest], axis=0)


def sources_kernel(gy_size, u_ref, rhs_ref, below_ref, above_ref, label_ref, out_ref, step_ref, x_ref, flow_ref, lin_ref, map_ref):
    planes, rows_y, nodes, columns = u_ref.shape
    place = lax.axis_index("gy")
    node, item = iota((nodes, nodes), 1), iota((nodes, nodes), 0)
    chosen = (node == wanted_node(item // FACE, item % FACE)).astype(BF16)
    own = [u_ref[x, y] for x in range(planes) for y in range(rows_y)]
    pair = gy_size == 2
    if pair:
        row = jnp.where(place > 0, below_ref.shape[1] - 1, 0)
        other = [below_ref[x, row] for x in range(planes)]
    else:
        other = [below_ref[x, below_ref.shape[1] - 1] for x in range(planes)] + [above_ref[x, 0] for x in range(planes)]
    step = step_ref[...]
    row, lane = iota((2 * FACE, 128), 0), iota((2 * FACE, 128), 1)
    flip = (lane == row + FACE * (row >= FACE)).astype(BF16)
    turned = dot_rows(flip, step).astype(BF16)
    faces = dot(chosen, jnp.concatenate(own + other, axis=1))
    picks = []
    for at in range(planes * rows_y):
        picks.append(picked(label_ref[pl.ds(at, 1), :], step.shape[0] // FACE))
    linear = dot(turned, jnp.concatenate(picks, axis=1))
    faces = [faces[:, i * columns:(i + 1) * columns] for i in range(len(own) + len(other))]
    z_at = iota((FACE, columns), 1) % FACE
    has_below = jnp.where(place > 0, 1.0, 0.0)
    has_above = jnp.where(place < gy_size - 1, 1.0, 0.0)
    data = []
    for x in range(planes):
        under = faces[len(own) + x][16:32] * has_below
        over = faces[len(own) + (0 if pair else planes) + x][0:16] * has_above
        for y in range(rows_y):
            at = x * rows_y + y
            y_flag = label_ref[pl.ds(planes * rows_y + at, 1), :]
            z_flag = label_ref[pl.ds(2 * planes * rows_y + at, 1), :]
            from_below = faces[at - 1][16:32] if y > 0 else under
            from_above = faces[at + 1][0:16] if y < rows_y - 1 else over
            from_front = jnp.where(z_at == 0, 0.0, pltpu.roll(faces[at][48:64], 1, 1))
            from_back = jnp.where(z_at == FACE - 1, 0.0, pltpu.roll(faces[at][32:48], columns - 1, 1))
            lateral = jnp.concatenate(
                [
                    from_below * (1.0 - y_flag),
                    from_above * y_flag,
                    from_front * (1.0 - z_flag),
                    from_back * z_flag,
                ],
                axis=0,
            ).astype(BF16)
            here = jnp.concatenate([rhs_ref[x, y], lateral], axis=0)
            x_ref[x, y] = here
            data.append(here)
    data = jnp.concatenate(data, axis=1)
    every = dot(out_ref[...], jnp.concatenate([data, data], axis=0))
    keep = (iota((256, 256), 0) // FACE == iota((256, 256), 1) // FACE).astype(BF16)
    wholes, pairs = None, None
    for x in range(planes):
        here = [linear[:, at * 256:at * 256 + 256] for at in range(x * rows_y, (x + 1) * rows_y)]
        both = [(part[:FACE].astype(BF16), part[FACE:].astype(BF16)) for part in here]
        for y in range(rows_y):
            lin_ref[x, y] = here[y][:FACE] + here[y][FACE:]
        if wholes is None:
            wholes, pairs = [part[:FACE] + part[FACE:] for part in here], both
        else:
            blocks = [[jnp.concatenate([part] * 16, axis=0) * keep for part in parts] for parts in both]
            stacks = [jnp.concatenate(pair, axis=0) for pair in pairs]
            firsts = [dot(stack, block[0]) for stack, block in zip(stacks, blocks)]
            seconds = [dot(pair[0], block[1]) for pair, block in zip(pairs, blocks)]
            wholes = [first[:FACE] + first[FACE:] + second for first, second in zip(firsts, seconds)]
            pairs = [split(whole) for whole in wholes]
    total = None
    for x in range(planes):
        begin = x * rows_y * columns
        label = jnp.concatenate([label_ref[pl.ds(x * rows_y + y, 1), :] for y in range(rows_y)], axis=1)
        flow = class_sum(every[:, begin:begin + rows_y * columns], label, FACE)
        flow_ref[x] = flow
        if total is not None:
            flow = flow + class_sum(dot(step_ref[...], stacked(total)), label, FACE)
        total = flow
    for y in range(rows_y):
        map_ref[y, 0:FACE] = wholes[y]
        map_ref[y, FACE:] = encode(total[:, y * columns:(y + 1) * columns])


def block_diagonal(linear):
    keep = (iota((256, 256), 0) // FACE == iota((256, 256), 1) // FACE).astype(BF16)
    return [jnp.concatenate([part] * 16, axis=0) * keep for part in split(linear)]


def half_weights(high, low, begin):
    keep = (iota((128, 128), 0) // FACE == iota((128, 128), 1) // FACE).astype(BF16)
    parts = [jnp.concatenate([part[:, begin:begin + 128]] * 8, axis=0) * keep for part in (high, low)]
    return jnp.concatenate(parts, axis=0)


def half_rows(high, low, begin):
    high, low = high[:, begin:begin + 128], low[:, begin:begin + 128]
    upper = jnp.concatenate([high, high], axis=1)
    return jnp.concatenate([upper, jnp.concatenate([low, jnp.zeros_like(low)], axis=1)], axis=0)


def joined_rows(pairs):
    ready = [
        (half_rows(*rows, begin), half_weights(*linear, begin)) for rows, linear in pairs for begin in (0, 128)
    ]
    sums = [dot(rows, weights) for rows, weights in ready]
    sums = [both[:both.shape[0] // 2] + both[both.shape[0] // 2:] for both in sums]
    return [jnp.concatenate(sums[i:i + 2], axis=1) for i in range(0, len(sums), 2)]


def join_many(pairs):
    rest = jnp.zeros((8, 256), F32)
    split_pairs = [(split(jnp.concatenate([first, rest], axis=0)), split(second[:FACE])) for first, second in pairs]
    joined = []
    for total, (_, later) in zip(joined_rows(split_pairs), pairs):
        joined.append(jnp.concatenate([total[:FACE], total[FACE:24] + later[FACE:]], axis=0))
    return joined


def sent_steps(size, first):
    return (2, 1) + tuple(range(3, size)) if first == 2 and size > 2 else tuple(range(1, size))


def advance_many(traces, maps):
    rest = jnp.zeros((8, 256), F32)
    pairs = [(split(jnp.concatenate([trace, rest], axis=0)), split(one[:FACE])) for trace, one in zip(traces, maps)]
    return [total[:8] + one[FACE:] for total, one in zip(joined_rows(pairs), maps)]


def block_slot(mine, other, size, power, first):
    step = (mine ^ other) if power else (mine - other + size) % size
    return step + 1 * (step == 1) - 1 * (step == 2) if first == 2 and size > 2 else step


def group_kernel(size, power, outer, *refs):
    blocks, total_ref, held = refs[:size], refs[size + 1], refs[size + 2]
    place = lax.axis_index("gx")
    mine = place % size
    rows_y = total_ref.shape[0]

    @pl.when(place // size < outer - 1)
    def _():
        for s in range(size):
            held[s] = blocks[s][...]
        slots = [block_slot(mine, j, size, power, 1) for j in range(size)]
        maps = [[held[slot, y] for slot in slots] for y in range(rows_y)]
        while len(maps[0]) > 1:
            length = len(maps[0])
            joined = join_many([(maps[y][i], maps[y][i + 1]) for y in range(rows_y) for i in range(0, length - 1, 2)])
            half = length // 2
            maps = [joined[y * half:y * half + half] + maps[y][2 * half:] for y in range(rows_y)]
        for y in range(rows_y):
            total_ref[y] = maps[y][0]

    @pl.when(place // size == outer - 1)
    def _():
        total_ref[...] = jnp.zeros(total_ref.shape, F32)


def carried(parts, traces, count):
    keep = (iota((128, 256), 0) % FACE == iota((128, 256), 1) // FACE).astype(BF16)
    here = []
    for trace in traces:
        rows = jnp.concatenate([jnp.broadcast_to(trace[t:t + 1], (FACE, 256)) for t in range(8)], axis=0)
        here.append([part * keep for part in split(rows)])
    by_first = [dot_rows(part, data[0]) for part, data in zip(parts, here)]
    by_second = [dot_rows(part[:count], data[1]) for part, data in zip(parts, here)]
    return [first[:count] + first[count:] + second for first, second in zip(by_first, by_second)]


def write_nodes(result_ref, out_ref, sems, base_ref, part_ref, traces):
    planes, rows_y, nodes, _ = result_ref.shape
    sums = carried([part_ref[y] for y in range(rows_y)], traces, planes * nodes)
    copies = []
    for y in range(rows_y):
        for x in range(planes):
            result_ref[x, y] = base_ref[x, y] + sums[y][x * nodes:(x + 1) * nodes]
            copies.append(pltpu.make_async_copy(result_ref.at[x, y], out_ref.at[x, y], sems.at[x, y]))
            copies[-1].start()
    for copy in copies:
        copy.wait()


def local_kernel(data_ref, label_ref, weight_ref, flow_ref, inv_ref, inflow_ref, base_ref, start_ref, chosen_ref, offset_ref, full_ref):
    planes, rows_y, nodes, columns = base_ref.shape
    coupling = jnp.zeros((nodes, 128), F32)
    count = inv_ref.shape[0]
    gathered = face_columns(inv_ref[...].reshape(count * nodes, nodes), nodes)
    for k in range(count):
        inv_rows = inv_ref[k]
        low = (count + k) * nodes
        products = class_products(
            gathered[k * nodes:k * nodes + nodes], gathered[low:low + nodes], weight_ref[:, 256 * k:256 * k + 256]
        )
        here = pl.ds(k * nodes, nodes)
        shifted = pltpu.roll(products, FACE * k, 1) if k else products
        coupling = jnp.where(iota((nodes, 128), 1) // FACE == k, shifted, coupling)
        full_ref[here, :] = in_parts(with_inverse(inv_rows, products))
    coupling = jnp.concatenate(split(coupling), axis=0)
    for y in range(rows_y):
        start_ref[y] = encode(inflow_ref[y])
    for x in range(planes):
        for y in range(rows_y):
            label = label_ref[pl.ds(x * rows_y + y, 1), :]
            data = data_ref[x, y]
            every = dot(full_ref[...], jnp.concatenate([data, data], axis=0))
            base_ref[x, y] = class_sum(every, label, nodes)
            chosen_ref[x, y] = dot(coupling, picked(label, count)).astype(BF16)
            if x < planes - 1:
                offset_ref[x, y] = encode(flow_ref[x, :, y * columns:(y + 1) * columns])


def ahead_kernel(size, power, *refs):
    blocks, ahead_ref, held = refs[:size], refs[size + 1], refs[size + 2]
    rows_y = ahead_ref.shape[0]
    for s in range(size):
        held[s] = blocks[s][...]
    mine = lax.axis_index("gx") % size
    same = (iota((24, 256), 1) % FACE == iota((24, 256), 0)).astype(F32)
    ahead = [same] * rows_y
    for j in range(size - 1):
        slot = block_slot(mine, j, size, power, 1)
        block = [held[slot, y] for y in range(rows_y)]
        joined = block if j == 0 else join_many([(ahead[y], block[y]) for y in range(rows_y)])
        ahead = [jnp.where(mine > j, joined[y], ahead[y]) for y in range(rows_y)]
    for y in range(rows_y):
        ahead_ref[y] = ahead[y]


def carry_kernel(size, swapped, ahead_ref, local_ref, start_ref, chosen_ref, offset_ref, lin_ref, base_ref, part_ref, out_ref, result_ref, sems):
    planes, rows_y, nodes, _ = base_ref.shape
    place = lax.axis_index("gx")
    if swapped:
        ahead_ref = ahead_ref.at[1 - lax.axis_index("gy") % 2]
    row_range = range(rows_y)

    def plane_map(x):
        return [jnp.concatenate([lin_ref[x, y], offset_ref[x, y]], axis=0) for y in row_range]

    @pl.when(place < size)
    def _():
        traces = advance_many([start_ref[y] for y in row_range], [ahead_ref[y] for y in row_range])
        entering = list(traces)
        for x in range(planes - 1):
            traces = advance_many(traces, plane_map(x))
            entering += traces
        sums = carried([chosen_ref[x, y] for x in range(planes) for y in row_range], entering, nodes)
        copies = []
        for x in range(planes):
            for y in row_range:
                result_ref[x, y] = local_ref[x, y] + sums[x * rows_y + y]
                copies.append(pltpu.make_async_copy(result_ref.at[x, y], out_ref.at[x, y], sems.at[x, y]))
                copies[-1].start()
        for copy in copies:
            copy.wait()

    @pl.when(place >= size)
    def _():
        ahead = [ahead_ref[y] for y in row_range]
        for x in range(planes):
            chosen = [chosen_ref[x, y] for y in row_range]
            sums = carried(chosen, [ahead[y][FACE:] for y in row_range], nodes)
            pairs = [block_diagonal(ahead[y][:FACE]) for y in row_range]
            firsts = [dot_rows(chosen[y], pairs[y][0]) for y in row_range]
            seconds = [dot_rows(chosen[y][:nodes], pairs[y][1]) for y in row_range]
            for y in row_range:
                base_ref[x, y] = local_ref[x, y] + sums[y]
                high, low = split(firsts[y][:nodes] + firsts[y][nodes:] + seconds[y])
                part_ref[y, pl.ds(x * nodes, nodes), :] = high
                part_ref[y, pl.ds((planes + x) * nodes, nodes), :] = low
            if x < planes - 1:
                ahead = join_many(list(zip(ahead, plane_map(x))))


def finish_places(places, steps, inner, *refs):
    blocks = refs[:len(steps)]
    start_ref, base_ref, part_ref, _, out_ref, result_ref, sems = refs[len(steps):]
    mine = lax.axis_index("gx") // inner
    for place in places:
        @pl.when(mine == place)
        def _():
            traces = [start_ref[y] for y in range(base_ref.shape[1])]
            for j in range(place):
                block = blocks[steps.index(place ^ j)]
                traces = advance_many(traces, [block[y] for y in range(len(traces))])
            write_nodes(result_ref, out_ref, sems, base_ref, part_ref, traces)


def finish_kernel(size, inner, power, *refs):
    blocks = refs[:size]
    start_ref, base_ref, part_ref, _, out_ref, result_ref, sems = refs[size:size + 7]
    rows_y = base_ref.shape[1]
    mine = lax.axis_index("gx") // inner
    held = refs[size + 7]
    for s in range(size):
        held[s] = blocks[s][...]

    @pl.when(mine > 0)
    def _():
        traces = []
        for y in range(rows_y):
            trace = start_ref[y]
            for j in range(size - 1):
                slot = block_slot(mine, j, size, power, 2)
                trace = jnp.where(mine > j, advance(trace, held[slot, y]), trace)
            traces.append(trace)
        write_nodes(result_ref, out_ref, sems, base_ref, part_ref, traces)


def moved(value, pairs):
    return lax.ppermute(value, ("gx", "gy"), pairs)


def shape(dims, kind=F32):
    return jax.ShapeDtypeStruct(dims, kind)


def call(kernel, outs, name, args, scratch=(), space=pltpu.VMEM, out_spaces=None, aliases=None, limit=48):
    many = isinstance(outs, tuple)
    spaces = out_spaces or ((pltpu.VMEM,) * len(outs) if many else pltpu.VMEM)
    if isinstance(space, tuple):
        in_specs = [pl.BlockSpec(memory_space=one) for one in space]
    else:
        in_specs = [pl.BlockSpec(memory_space=space)] * len(args)
    if many:
        out_specs = tuple(pl.BlockSpec(memory_space=one) for one in spaces)
    else:
        out_specs = pl.BlockSpec(memory_space=spaces)
    return pl.pallas_call(
        kernel,
        out_shape=outs,
        in_specs=in_specs,
        out_specs=out_specs,
        scratch_shapes=list(scratch),
        input_output_aliases=aliases or {},
        name=name,
        cost_estimate=pl.CostEstimate(flops=1000000, bytes_accessed=500000, transcendentals=0),
        compiler_params=pltpu.CompilerParams(vmem_limit_bytes=limit * 1024 * 1024),
    )(*args)


def on_device(gx_size, gy_size, u_old, rhs, classes, flags, inverse, x_face, lateral_faces, inflow):
    planes, rows_y, nodes, columns = u_old.shape
    count = inverse.shape[0]
    everyone = [(x, y) for x in range(gx_size) for y in range(gy_size)]

    def at(x, y):
        return x * gy_size + y

    if gy_size == 2:
        below = above = moved(u_old, [(at(x, y), at(x, 1 - y)) for x, y in everyone])
    else:
        below = moved(u_old[:, rows_y - 1:], [(at(x, y), at(x, y + 1)) for x, y in everyone if y + 1 < gy_size])
        above = moved(u_old[:, :1], [(at(x, y), at(x, y - 1)) for x, y in everyone if y > 0])
    weights, out_rows, step, labels = call(
        params_kernel,
        (
            shape((5 * FACE, count * 256), BF16),
            shape((count * FACE, 256), BF16),
            shape((count * FACE, 128), BF16),
            shape((3 * planes * rows_y, columns)),
        ),
        "class_matrices",
        tuple(
            pltpu.with_memory_space_constraint(value, pltpu.HBM)
            for value in (classes, flags, x_face, lateral_faces, inverse)
        ),
        [
            pltpu.VMEM(classes.shape, jnp.int32),
            pltpu.VMEM(flags.shape, jnp.int32),
            pltpu.VMEM(x_face.shape, F32),
            pltpu.VMEM(lateral_faces.shape, F32),
            pltpu.VMEM((count, FACE, nodes), F32),
            pltpu.SemaphoreType.DMA((5,)),
        ],
        space=pltpu.HBM,
    )
    data, flow, linear, here = call(
        functools.partial(sources_kernel, gy_size),
        (
            shape((planes, rows_y, 128, columns), BF16),
            shape((planes, FACE, rows_y * columns)),
            shape((planes, rows_y, FACE, 256)),
            shape((rows_y, 24, 256)),
        ),
        "sources",
        (u_old, rhs, below, above, labels, out_rows, step),
    )
    inner = 4 if gx_size % 4 == 0 else 1
    outer = gx_size // inner
    power = outer & (outer - 1) == 0
    other = 1 if gy_size % 2 == 0 else 0

    def exchanged(value, step):
        if power or step < inner:
            return moved(value, [(at(x, y), at(x ^ step, y ^ other)) for x, y in everyone])
        return moved(value, [(at(x, y), at((x + step) % gx_size, y ^ other)) for x, y in everyone])

    near = ((exchanged(here, 0) if other else here),) + tuple(exchanged(here, s) for s in sent_steps(inner, 1))
    nodes_shape = (planes, rows_y, nodes, columns)
    writing = [pltpu.VMEM(nodes_shape, F32), pltpu.SemaphoreType.DMA((planes, rows_y))]
    local, start, chosen, offsets = call(
        local_kernel,
        (
            shape(nodes_shape),
            shape((rows_y, 8, 256)),
            shape((planes, rows_y, 2 * nodes, 256), BF16),
            shape((max(planes - 1, 1), rows_y, 8, 256)),
        ),
        "local_solve",
        (data, labels, weights, flow, inverse, inflow),
        [pltpu.VMEM((count * nodes, 256), BF16)],
    )
    total = call(
        functools.partial(group_kernel, inner, True, outer),
        shape((rows_y, 24, 256)),
        "group_maps",
        near + (start,),
        [pltpu.VMEM((inner, rows_y, 24, 256), F32)],
    )
    blocks = [total] + [exchanged(total, s * inner) for s in sent_steps(outer, 2)]
    ahead = call(
        functools.partial(ahead_kernel, inner, True),
        shape((rows_y, 24, 256)),
        "maps_ahead",
        near + (total,),
        [pltpu.VMEM((inner, rows_y, 24, 256), F32)],
    )
    if other:
        couples = [[y, y + 1] for y in range(0, gy_size, 2)]
        ahead = lax.all_gather(ahead, "gy", axis_index_groups=couples)
    base, parts, out = call(
        functools.partial(carry_kernel, inner, other == 1),
        (
            shape(nodes_shape),
            shape((rows_y, 2 * planes * nodes, 256), BF16),
            pltpu.HBM(nodes_shape, F32),
        ),
        "carry_maps",
        (ahead, local, start, chosen, offsets, linear),
        writing,
        out_spaces=(pltpu.VMEM, pltpu.VMEM, pltpu.HBM),
    )
    def written(kernel, name, args, scratch):
        return call(
            kernel,
            pltpu.HBM(nodes_shape, F32),
            name,
            args,
            scratch,
            space=(pltpu.VMEM,) * (len(args) - 1) + (pltpu.HBM,),
            out_spaces=pltpu.HBM,
            aliases={len(args) - 1: 0},
        )

    if power and outer == 4:
        steps = sent_steps(outer, 2)
        early = (3, 1)
        out = written(
            functools.partial(finish_places, (1,), early, inner),
            "finish_second",
            tuple(blocks[1 + steps.index(one)] for one in early) + (start, base, parts, out),
            writing,
        )
        return written(
            functools.partial(finish_places, (2, 3), steps, inner),
            "finish_last",
            tuple(blocks[1:]) + (start, base, parts, out),
            writing,
        )
    return written(
        functools.partial(finish_kernel, outer, inner, power),
        "finish",
        tuple(blocks) + (start, base, parts, out),
        writing + [pltpu.VMEM((outer, rows_y, 24, 256), F32)],
    )


def solution(mesh):
    in_specs = (
        P("gx", "gy", None, None),
        P("gx", "gy", None, None),
        P("gx", "gy", None),
        P(None, "gx", "gy", None),
        P(),
        P(),
        P(),
        P("gy", None, None),
    )
    out_specs = P("gx", "gy", None, None)
    body = functools.partial(on_device, mesh.shape["gx"], mesh.shape["gy"])
    return jax.shard_map(body, mesh=mesh, in_specs=in_specs, out_specs=out_specs, check_vma=False)
```

```python
import functools

import jax
import jax.numpy as jnp
from jax import lax
from jax.experimental import pallas as pl
from jax.experimental.pallas import tpu as pltpu
from jax.sharding import PartitionSpec as P

FACE = 16
HIGH = lax.Precision.HIGHEST
F32 = jnp.float32
BF16 = jnp.bfloat16


def iota(shape, dim):
    return lax.broadcasted_iota(jnp.int32, shape, dim)


def exact(left, right):
    return jnp.dot(left, right, precision=HIGH, preferred_element_type=F32)


def split(value):
    high = value.astype(BF16)
    return high, (value - high.astype(F32)).astype(BF16)


def wanted_node(face, item):
    high, low = item // 4, item % 4
    return jnp.where(face < 2, 16 * high + low + 12 * (face == 1), 16 * high + 4 * low + 3 * (face == 3))


def dot(left, right):
    return jnp.dot(left, right, preferred_element_type=F32)


def dot_rows(left, right):
    return lax.dot_general(left, right, (((1,), (1,)), ((), ())), preferred_element_type=F32)


def applied(rows, linear):
    lane = iota((rows.shape[0], 128), 1)
    halves = []
    for begin in (0, 128):
        part, total = rows[:, begin:begin + 128], None
        for b in range(FACE):
            near = jnp.take_along_axis(part, lane // FACE * FACE + b, axis=1, mode="promise_in_bounds")
            term = near * linear[b:b + 1, begin:begin + 128]
            total = term if total is None else total + term
        halves.append(total)
    return jnp.concatenate(halves, axis=1)


def join(earlier, later):
    moved_rows = applied(earlier, later[:FACE])
    return jnp.concatenate([moved_rows[:FACE], moved_rows[FACE:] + later[FACE:]], axis=0)


def advance(trace, later):
    return applied(trace, later[:FACE]) + later[FACE:]


def encode(value):
    keep = (iota((256, 128), 0) // FACE == iota((256, 128), 1) % FACE).astype(BF16)
    spread = [jnp.concatenate([part] * 16, axis=0) * keep for part in split(value)]
    gather = (iota((8, 256), 1) % 128 // FACE == iota((8, 256), 0)).astype(BF16)
    return dot_rows(gather, jnp.concatenate(spread, axis=1))


def face_columns(inv_rows, nodes):
    at = iota((nodes, 5 * FACE), 1)
    wanted = jnp.where(at < 64, wanted_node(at // FACE, at % FACE), at - 64)
    chosen = (iota((nodes, 5 * FACE), 0) == wanted).astype(BF16)
    return dot(jnp.concatenate(split(inv_rows), axis=0), chosen).astype(BF16)


def class_products(high, low, weights):
    count = high.shape[0]
    parts = dot(jnp.concatenate([high, low], axis=0), weights)
    return -(parts[:count, :128] + parts[:count, 128:] + parts[count:, :128])


def with_inverse(inv_rows, products):
    count = inv_rows.shape[0]
    wide = jnp.concatenate([inv_rows, jnp.zeros((count, 128 - inv_rows.shape[1]), F32)], axis=1)
    return jnp.where(iota((count, 128), 1) < 64, wide, products)


def in_parts(value):
    high, low = split(value)
    return jnp.concatenate([high, low], axis=1)


def coupling_parts(products):
    high, low = split(products)
    lane = iota(products.shape, 1)
    return jnp.where(lane < 32, high.astype(F32), jnp.where(lane < 48, low.astype(F32), 0.0)).astype(BF16)


def params_kernel(cls_hbm, flag_hbm, x_hbm, lat_hbm, inv_hbm, weight_ref, out_ref, step_ref, label_ref,
                  cls_ref, flag_ref, x_ref, lat_ref, inv_ref, sems):
    pairs = ((cls_hbm, cls_ref), (flag_hbm, flag_ref), (x_hbm, x_ref), (lat_hbm, lat_ref))
    pairs += ((inv_hbm.at[:, inv_hbm.shape[1] - FACE:, :], inv_ref),)
    copies = [pltpu.make_async_copy(a, b, sems.at[i]) for i, (a, b) in enumerate(pairs)]
    for copy in copies[::-1]:
        copy.start()
    count, nodes, _ = inv_hbm.shape
    planes = cls_ref.shape[0]
    item, lane = iota((FACE, 128), 0), iota((FACE, 128), 1)
    places = [(lane == 64 + FACE * f + item).astype(BF16) for f in range(4)]
    places.append(((lane < 48) & (lane % FACE == item)).astype(BF16))
    for copy in copies[:2]:
        copy.wait()
    labels = [cls_ref[x] for x in range(planes)]
    labels += [flag_ref[d, x] for d in range(2) for x in range(planes)]
    labels = jnp.concatenate(labels, axis=0).astype(F32).astype(BF16)
    tile = (iota((FACE, 128), 1) % FACE == iota((FACE, 128), 0)).astype(BF16)
    label_ref[...] = dot(labels, tile)
    for copy in copies[2:]:
        copy.wait()
    placed = []
    for f in range(5):
        rows = (lat_ref[f] if f < 4 else x_ref[...]).reshape(count * FACE, FACE)
        placed.append(dot(jnp.concatenate(split(rows), axis=0), places[f]).astype(BF16))
    inv_rows = [inv_ref[k] for k in range(count)]
    gathered = face_columns(jnp.concatenate(inv_rows, axis=0), nodes)
    outs, steps = [], []
    for k in range(count):
        columns = []
        for part in range(2):
            begin = part * count * FACE + k * FACE
            columns.append(jnp.concatenate([p[begin:begin + FACE] for p in placed], axis=0))
        weights = jnp.concatenate(columns, axis=1)
        weight_ref[:, 256 * k:256 * k + 256] = weights
        low = (count + k) * FACE
        products = class_products(gathered[k * FACE:k * FACE + FACE], gathered[low:low + FACE], weights)
        outs.append(with_inverse(inv_rows[k], products))
        steps.append(products)
    out_ref[...] = in_parts(jnp.concatenate(outs, axis=0))
    step_ref[...] = coupling_parts(jnp.concatenate(steps, axis=0))


def picked(label, count):
    wide = (iota((FACE, 256), 1) // FACE == iota((FACE, 256), 0)).astype(BF16)
    on_wide = dot(label[:, :FACE].astype(BF16), wide).astype(jnp.int32)
    row, lane = iota((count * FACE, 256), 0), iota((count * FACE, 256), 1)
    return jnp.where((row % FACE == lane % FACE) & (row // FACE == on_wide), 1.0, 0.0).astype(BF16)


def class_sum(every, label, rows):
    total = None
    for k in range(8):
        term = jnp.where(label == k, every[k * rows:(k + 1) * rows], 0.0)
        total = term if total is None else total + term
    return total


def stacked(value):
    first, second = split(value)
    rest = jnp.zeros((128 - 3 * FACE, value.shape[1]), BF16)
    return jnp.concatenate([first, second, first, rest], axis=0)


def sources_kernel(gy_size, u_ref, rhs_ref, below_ref, above_ref, label_ref, out_ref, step_ref, x_ref, flow_ref, lin_ref, map_ref):
    planes, rows_y, nodes, columns = u_ref.shape
    place = lax.axis_index("gy")
    node, item = iota((nodes, nodes), 1), iota((nodes, nodes), 0)
    chosen = (node == wanted_node(item // FACE, item % FACE)).astype(BF16)
    own = [u_ref[x, y] for x in range(planes) for y in range(rows_y)]
    pair = gy_size == 2
    if pair:
        row = jnp.where(place > 0, below_ref.shape[1] - 1, 0)
        other = [below_ref[x, row] for x in range(planes)]
    else:
        other = [below_ref[x, below_ref.shape[1] - 1] for x in range(planes)] + [above_ref[x, 0] for x in range(planes)]
    step = step_ref[...]
    row, lane = iota((2 * FACE, 128), 0), iota((2 * FACE, 128), 1)
    flip = (lane == row + FACE * (row >= FACE)).astype(BF16)
    turned = dot_rows(flip, step).astype(BF16)
    faces = dot(chosen, jnp.concatenate(own + other, axis=1))
    picks = []
    for at in range(planes * rows_y):
        picks.append(picked(label_ref[pl.ds(at, 1), :], step.shape[0] // FACE))
    linear = dot(turned, jnp.concatenate(picks, axis=1))
    faces = [faces[:, i * columns:(i + 1) * columns] for i in range(len(own) + len(other))]
    z_at = iota((FACE, columns), 1) % FACE
    has_below = jnp.where(place > 0, 1.0, 0.0)
    has_above = jnp.where(place < gy_size - 1, 1.0, 0.0)
    data = []
    for x in range(planes):
        under = faces[len(own) + x][16:32] * has_below
        over = faces[len(own) + (0 if pair else planes) + x][0:16] * has_above
        for y in range(rows_y):
            at = x * rows_y + y
            y_flag = label_ref[pl.ds(planes * rows_y + at, 1), :]
            z_flag = label_ref[pl.ds(2 * planes * rows_y + at, 1), :]
            from_below = faces[at - 1][16:32] if y > 0 else under
            from_above = faces[at + 1][0:16] if y < rows_y - 1 else over
            from_front = jnp.where(z_at == 0, 0.0, pltpu.roll(faces[at][48:64], 1, 1))
            from_back = jnp.where(z_at == FACE - 1, 0.0, pltpu.roll(faces[at][32:48], columns - 1, 1))
            lateral = jnp.concatenate(
                [
                    from_below * (1.0 - y_flag),
                    from_above * y_flag,
                    from_front * (1.0 - z_flag),
                    from_back * z_flag,
                ],
                axis=0,
            ).astype(BF16)
            here = jnp.concatenate([rhs_ref[x, y], lateral], axis=0)
            x_ref[x, y] = here
            data.append(here)
    data = jnp.concatenate(data, axis=1)
    every = dot(out_ref[...], jnp.concatenate([data, data], axis=0))
    keep = (iota((256, 256), 0) // FACE == iota((256, 256), 1) // FACE).astype(BF16)
    wholes, pairs = None, None
    for x in range(planes):
        here = [linear[:, at * 256:at * 256 + 256] for at in range(x * rows_y, (x + 1) * rows_y)]
        both = [(part[:FACE].astype(BF16), part[FACE:].astype(BF16)) for part in here]
        for y in range(rows_y):
            lin_ref[x, y] = here[y][:FACE] + here[y][FACE:]
        if wholes is None:
            wholes, pairs = [part[:FACE] + part[FACE:] for part in here], both
        else:
            blocks = [[jnp.concatenate([part] * 16, axis=0) * keep for part in parts] for parts in both]
            stacks = [jnp.concatenate(pair, axis=0) for pair in pairs]
            firsts = [dot(stack, block[0]) for stack, block in zip(stacks, blocks)]
            seconds = [dot(pair[0], block[1]) for pair, block in zip(pairs, blocks)]
            wholes = [first[:FACE] + first[FACE:] + second for first, second in zip(firsts, seconds)]
            pairs = [split(whole) for whole in wholes]
    total = None
    for x in range(planes):
        begin = x * rows_y * columns
        label = jnp.concatenate([label_ref[pl.ds(x * rows_y + y, 1), :] for y in range(rows_y)], axis=1)
        flow = class_sum(every[:, begin:begin + rows_y * columns], label, FACE)
        flow_ref[x] = flow
        if total is not None:
            flow = flow + class_sum(dot(step_ref[...], stacked(total)), label, FACE)
        total = flow
    for y in range(rows_y):
        map_ref[y, 0:FACE] = wholes[y]
        map_ref[y, FACE:] = encode(total[:, y * columns:(y + 1) * columns])


def block_diagonal(linear):
    keep = (iota((256, 256), 0) // FACE == iota((256, 256), 1) // FACE).astype(BF16)
    return [jnp.concatenate([part] * 16, axis=0) * keep for part in split(linear)]


def half_weights(high, low, begin):
    keep = (iota((128, 128), 0) // FACE == iota((128, 128), 1) // FACE).astype(BF16)
    parts = [jnp.concatenate([part[:, begin:begin + 128]] * 8, axis=0) * keep for part in (high, low)]
    return jnp.concatenate(parts, axis=0)


def half_rows(high, low, begin):
    high, low = high[:, begin:begin + 128], low[:, begin:begin + 128]
    upper = jnp.concatenate([high, high], axis=1)
    return jnp.concatenate([upper, jnp.concatenate([low, jnp.zeros_like(low)], axis=1)], axis=0)


def joined_rows(pairs):
    ready = [
        (half_rows(*rows, begin), half_weights(*linear, begin)) for rows, linear in pairs for begin in (0, 128)
    ]
    sums = [dot(rows, weights) for rows, weights in ready]
    sums = [both[:both.shape[0] // 2] + both[both.shape[0] // 2:] for both in sums]
    return [jnp.concatenate(sums[i:i + 2], axis=1) for i in range(0, len(sums), 2)]


def join_many(pairs):
    rest = jnp.zeros((8, 256), F32)
    split_pairs = [(split(jnp.concatenate([first, rest], axis=0)), split(second[:FACE])) for first, second in pairs]
    joined = []
    for total, (_, later) in zip(joined_rows(split_pairs), pairs):
        joined.append(jnp.concatenate([total[:FACE], total[FACE:24] + later[FACE:]], axis=0))
    return joined


def sent_steps(size, first):
    if first == 2:
        return (2, 1) + tuple(range(3, size)) if size > 2 else tuple(range(1, size))
    return (1, 3, 2) + tuple(range(4, size)) if size > 3 else tuple(range(1, size))


def advance_many(traces, maps):
    rest = jnp.zeros((8, 256), F32)
    pairs = [(split(jnp.concatenate([trace, rest], axis=0)), split(one[:FACE])) for trace, one in zip(traces, maps)]
    return [total[:8] + one[FACE:] for total, one in zip(joined_rows(pairs), maps)]


def block_slot(mine, other, size, power, first):
    step = (mine ^ other) if power else (mine - other + size) % size
    if first == 2:
        return step + 1 * (step == 1) - 1 * (step == 2) if size > 2 else step
    return step + 1 * (step == 2) - 1 * (step == 3) if size > 3 else step


def group_kernel(size, power, outer, *refs):
    blocks, total_ref, held = refs[:size], refs[size + 1], refs[size + 2]
    place = lax.axis_index("gx")
    mine = place % size
    rows_y = total_ref.shape[0]

    @pl.when(place // size < outer - 1)
    def _():
        for s in range(size):
            held[s] = blocks[s][...]
        slots = [block_slot(mine, j, size, power, 1) for j in range(size)]
        maps = [[held[slot, y] for slot in slots] for y in range(rows_y)]
        while len(maps[0]) > 1:
            length = len(maps[0])
            joined = join_many([(maps[y][i], maps[y][i + 1]) for y in range(rows_y) for i in range(0, length - 1, 2)])
            half = length // 2
            maps = [joined[y * half:y * half + half] + maps[y][2 * half:] for y in range(rows_y)]
        for y in range(rows_y):
            total_ref[y] = maps[y][0]

    @pl.when(place // size == outer - 1)
    def _():
        total_ref[...] = jnp.zeros(total_ref.shape, F32)


def carried(parts, traces, count):
    keep = (iota((128, 256), 0) % FACE == iota((128, 256), 1) // FACE).astype(BF16)
    here = []
    for trace in traces:
        rows = jnp.concatenate([jnp.broadcast_to(trace[t:t + 1], (FACE, 256)) for t in range(8)], axis=0)
        here.append([part * keep for part in split(rows)])
    by_first = [dot_rows(part, data[0]) for part, data in zip(parts, here)]
    by_second = [dot_rows(part[:count], data[1]) for part, data in zip(parts, here)]
    return [first[:count] + first[count:] + second for first, second in zip(by_first, by_second)]


def write_nodes(result_ref, out_ref, sems, base_ref, part_ref, traces):
    planes, rows_y, nodes, _ = result_ref.shape
    sums = carried([part_ref[y] for y in range(rows_y)], traces, planes * nodes)
    copies = []
    for y in range(rows_y):
        for x in range(planes):
            result_ref[x, y] = base_ref[x, y] + sums[y][x * nodes:(x + 1) * nodes]
            copies.append(pltpu.make_async_copy(result_ref.at[x, y], out_ref.at[x, y], sems.at[x, y]))
            copies[-1].start()
    for copy in copies:
        copy.wait()


def local_kernel(data_ref, label_ref, weight_ref, flow_ref, inv_ref, inflow_ref, base_ref, start_ref, chosen_ref, offset_ref, full_ref):
    planes, rows_y, nodes, columns = base_ref.shape
    coupling = jnp.zeros((nodes, 128), F32)
    count = inv_ref.shape[0]
    gathered = face_columns(inv_ref[...].reshape(count * nodes, nodes), nodes)
    for k in range(count):
        inv_rows = inv_ref[k]
        low = (count + k) * nodes
        products = class_products(
            gathered[k * nodes:k * nodes + nodes], gathered[low:low + nodes], weight_ref[:, 256 * k:256 * k + 256]
        )
        here = pl.ds(k * nodes, nodes)
        shifted = pltpu.roll(products, FACE * k, 1) if k else products
        coupling = jnp.where(iota((nodes, 128), 1) // FACE == k, shifted, coupling)
        full_ref[here, :] = in_parts(with_inverse(inv_rows, products))
    coupling = jnp.concatenate(split(coupling), axis=0)
    for y in range(rows_y):
        start_ref[y] = encode(inflow_ref[y])
    for x in range(planes):
        for y in range(rows_y):
            label = label_ref[pl.ds(x * rows_y + y, 1), :]
            data = data_ref[x, y]
            every = dot(full_ref[...], jnp.concatenate([data, data], axis=0))
            base_ref[x, y] = class_sum(every, label, nodes)
            chosen_ref[x, y] = dot(coupling, picked(label, count)).astype(BF16)
            if x < planes - 1:
                offset_ref[x, y] = encode(flow_ref[x, :, y * columns:(y + 1) * columns])


def ahead_kernel(size, power, *refs):
    blocks, ahead_ref, held = refs[:size], refs[size + 1], refs[size + 2]
    rows_y = ahead_ref.shape[0]
    for s in range(size):
        held[s] = blocks[s][...]
    mine = lax.axis_index("gx") % size
    same = (iota((24, 256), 1) % FACE == iota((24, 256), 0)).astype(F32)
    ahead = [same] * rows_y
    for j in range(size - 1):
        slot = block_slot(mine, j, size, power, 1)
        block = [held[slot, y] for y in range(rows_y)]
        joined = block if j == 0 else join_many([(ahead[y], block[y]) for y in range(rows_y)])
        ahead = [jnp.where(mine > j, joined[y], ahead[y]) for y in range(rows_y)]
    for y in range(rows_y):
        ahead_ref[y] = ahead[y]


def carry_kernel(size, swapped, ahead_ref, local_ref, start_ref, chosen_ref, offset_ref, lin_ref, base_ref, part_ref, out_ref, result_ref, sems):
    planes, rows_y, nodes, _ = base_ref.shape
    place = lax.axis_index("gx")
    if swapped:
        ahead_ref = ahead_ref.at[1 - lax.axis_index("gy") % 2]
    row_range = range(rows_y)

    def plane_map(x):
        return [jnp.concatenate([lin_ref[x, y], offset_ref[x, y]], axis=0) for y in row_range]

    @pl.when(place < size)
    def _():
        traces = advance_many([start_ref[y] for y in row_range], [ahead_ref[y] for y in row_range])
        entering = list(traces)
        for x in range(planes - 1):
            traces = advance_many(traces, plane_map(x))
            entering += traces
        sums = carried([chosen_ref[x, y] for x in range(planes) for y in row_range], entering, nodes)
        copies = []
        for x in range(planes):
            for y in row_range:
                result_ref[x, y] = local_ref[x, y] + sums[x * rows_y + y]
                copies.append(pltpu.make_async_copy(result_ref.at[x, y], out_ref.at[x, y], sems.at[x, y]))
                copies[-1].start()
        for copy in copies:
            copy.wait()

    @pl.when(place >= size)
    def _():
        ahead = [ahead_ref[y] for y in row_range]
        for x in range(planes):
            chosen = [chosen_ref[x, y] for y in row_range]
            sums = carried(chosen, [ahead[y][FACE:] for y in row_range], nodes)
            pairs = [block_diagonal(ahead[y][:FACE]) for y in row_range]
            firsts = [dot_rows(chosen[y], pairs[y][0]) for y in row_range]
            seconds = [dot_rows(chosen[y][:nodes], pairs[y][1]) for y in row_range]
            for y in row_range:
                base_ref[x, y] = local_ref[x, y] + sums[y]
                high, low = split(firsts[y][:nodes] + firsts[y][nodes:] + seconds[y])
                part_ref[y, pl.ds(x * nodes, nodes), :] = high
                part_ref[y, pl.ds((planes + x) * nodes, nodes), :] = low
            if x < planes - 1:
                ahead = join_many(list(zip(ahead, plane_map(x))))


def finish_places(places, steps, inner, *refs):
    blocks = refs[:len(steps)]
    start_ref, base_ref, part_ref, _, out_ref, result_ref, sems = refs[len(steps):]
    mine = lax.axis_index("gx") // inner
    for place in places:
        @pl.when(mine == place)
        def _():
            traces = [start_ref[y] for y in range(base_ref.shape[1])]
            for j in range(place):
                block = blocks[steps.index(place ^ j)]
                traces = advance_many(traces, [block[y] for y in range(len(traces))])
            write_nodes(result_ref, out_ref, sems, base_ref, part_ref, traces)


def finish_kernel(size, inner, power, *refs):
    blocks = refs[:size]
    start_ref, base_ref, part_ref, _, out_ref, result_ref, sems = refs[size:size + 7]
    rows_y = base_ref.shape[1]
    mine = lax.axis_index("gx") // inner
    held = refs[size + 7]
    for s in range(size):
        held[s] = blocks[s][...]

    @pl.when(mine > 0)
    def _():
        traces = []
        for y in range(rows_y):
            trace = start_ref[y]
            for j in range(size - 1):
                slot = block_slot(mine, j, size, power, 2)
                trace = jnp.where(mine > j, advance(trace, held[slot, y]), trace)
            traces.append(trace)
        write_nodes(result_ref, out_ref, sems, base_ref, part_ref, traces)


def moved(value, pairs):
    return lax.ppermute(value, ("gx", "gy"), pairs)


def shape(dims, kind=F32):
    return jax.ShapeDtypeStruct(dims, kind)


def call(kernel, outs, name, args, scratch=(), space=pltpu.VMEM, out_spaces=None, aliases=None, limit=48):
    many = isinstance(outs, tuple)
    spaces = out_spaces or ((pltpu.VMEM,) * len(outs) if many else pltpu.VMEM)
    if isinstance(space, tuple):
        in_specs = [pl.BlockSpec(memory_space=one) for one in space]
    else:
        in_specs = [pl.BlockSpec(memory_space=space)] * len(args)
    if many:
        out_specs = tuple(pl.BlockSpec(memory_space=one) for one in spaces)
    else:
        out_specs = pl.BlockSpec(memory_space=spaces)
    return pl.pallas_call(
        kernel,
        out_shape=outs,
        in_specs=in_specs,
        out_specs=out_specs,
        scratch_shapes=list(scratch),
        input_output_aliases=aliases or {},
        name=name,
        cost_estimate=pl.CostEstimate(flops=1000000, bytes_accessed=500000, transcendentals=0),
        compiler_params=pltpu.CompilerParams(vmem_limit_bytes=limit * 1024 * 1024),
    )(*args)


def on_device(gx_size, gy_size, u_old, rhs, classes, flags, inverse, x_face, lateral_faces, inflow):
    planes, rows_y, nodes, columns = u_old.shape
    count = inverse.shape[0]
    everyone = [(x, y) for x in range(gx_size) for y in range(gy_size)]

    def at(x, y):
        return x * gy_size + y

    if gy_size == 2:
        below = above = moved(u_old, [(at(x, y), at(x, 1 - y)) for x, y in everyone])
    else:
        below = moved(u_old[:, rows_y - 1:], [(at(x, y), at(x, y + 1)) for x, y in everyone if y + 1 < gy_size])
        above = moved(u_old[:, :1], [(at(x, y), at(x, y - 1)) for x, y in everyone if y > 0])
    weights, out_rows, step, labels = call(
        params_kernel,
        (
            shape((5 * FACE, count * 256), BF16),
            shape((count * FACE, 256), BF16),
            shape((count * FACE, 128), BF16),
            shape((3 * planes * rows_y, columns)),
        ),
        "class_matrices",
        tuple(
            pltpu.with_memory_space_constraint(value, pltpu.HBM)
            for value in (classes, flags, x_face, lateral_faces, inverse)
        ),
        [
            pltpu.VMEM(classes.shape, jnp.int32),
            pltpu.VMEM(flags.shape, jnp.int32),
            pltpu.VMEM(x_face.shape, F32),
            pltpu.VMEM(lateral_faces.shape, F32),
            pltpu.VMEM((count, FACE, nodes), F32),
            pltpu.SemaphoreType.DMA((5,)),
        ],
        space=pltpu.HBM,
    )
    data, flow, linear, here = call(
        functools.partial(sources_kernel, gy_size),
        (
            shape((planes, rows_y, 128, columns), BF16),
            shape((planes, FACE, rows_y * columns)),
            shape((planes, rows_y, FACE, 256)),
            shape((rows_y, 24, 256)),
        ),
        "sources",
        (u_old, rhs, below, above, labels, out_rows, step),
    )
    inner = 4 if gx_size % 4 == 0 else 1
    outer = gx_size // inner
    power = outer & (outer - 1) == 0
    other = 1 if gy_size % 2 == 0 else 0

    def exchanged(value, step):
        if power or step < inner:
            return moved(value, [(at(x, y), at(x ^ step, y ^ other)) for x, y in everyone])
        return moved(value, [(at(x, y), at((x + step) % gx_size, y ^ other)) for x, y in everyone])

    near = ((exchanged(here, 0) if other else here),) + tuple(exchanged(here, s) for s in sent_steps(inner, 1))
    nodes_shape = (planes, rows_y, nodes, columns)
    writing = [pltpu.VMEM(nodes_shape, F32), pltpu.SemaphoreType.DMA((planes, rows_y))]
    local, start, chosen, offsets = call(
        local_kernel,
        (
            shape(nodes_shape),
            shape((rows_y, 8, 256)),
            shape((planes, rows_y, 2 * nodes, 256), BF16),
            shape((max(planes - 1, 1), rows_y, 8, 256)),
        ),
        "local_solve",
        (data, labels, weights, flow, inverse, inflow),
        [pltpu.VMEM((count * nodes, 256), BF16)],
    )
    total = call(
        functools.partial(group_kernel, inner, True, outer),
        shape((rows_y, 24, 256)),
        "group_maps",
        near + (start,),
        [pltpu.VMEM((inner, rows_y, 24, 256), F32)],
    )
    blocks = [total] + [exchanged(total, s * inner) for s in sent_steps(outer, 2)]
    ahead = call(
        functools.partial(ahead_kernel, inner, True),
        shape((rows_y, 24, 256)),
        "maps_ahead",
        near + (total,),
        [pltpu.VMEM((inner, rows_y, 24, 256), F32)],
    )
    if other:
        couples = [[y, y + 1] for y in range(0, gy_size, 2)]
        ahead = lax.all_gather(ahead, "gy", axis_index_groups=couples)
    base, parts, out = call(
        functools.partial(carry_kernel, inner, other == 1),
        (
            shape(nodes_shape),
            shape((rows_y, 2 * planes * nodes, 256), BF16),
            pltpu.HBM(nodes_shape, F32),
        ),
        "carry_maps",
        (ahead, local, start, chosen, offsets, linear),
        writing,
        out_spaces=(pltpu.VMEM, pltpu.VMEM, pltpu.HBM),
    )
    def written(kernel, name, args, scratch):
        return call(
            kernel,
            pltpu.HBM(nodes_shape, F32),
            name,
            args,
            scratch,
            space=(pltpu.VMEM,) * (len(args) - 1) + (pltpu.HBM,),
            out_spaces=pltpu.HBM,
            aliases={len(args) - 1: 0},
        )

    if power and outer == 4:
        steps = sent_steps(outer, 2)
        early = (3, 1)
        out = written(
            functools.partial(finish_places, (1,), early, inner),
            "finish_second",
            tuple(blocks[1 + steps.index(one)] for one in early) + (start, base, parts, out),
            writing,
        )
        return written(
            functools.partial(finish_places, (2, 3), steps, inner),
            "finish_last",
            tuple(blocks[1:]) + (start, base, parts, out),
            writing,
        )
    return written(
        functools.partial(finish_kernel, outer, inner, power),
        "finish",
        tuple(blocks) + (start, base, parts, out),
        writing + [pltpu.VMEM((outer, rows_y, 24, 256), F32)],
    )


def solution(mesh):
    in_specs = (
        P("gx", "gy", None, None),
        P("gx", "gy", None, None),
        P("gx", "gy", None),
        P(None, "gx", "gy", None),
        P(),
        P(),
        P(),
        P("gy", None, None),
    )
    out_specs = P("gx", "gy", None, None)
    body = functools.partial(on_device, mesh.shape["gx"], mesh.shape["gy"])
    return jax.shard_map(body, mesh=mesh, in_specs=in_specs, out_specs=out_specs, check_vma=False)
```

```python
import functools

import jax
import jax.numpy as jnp
from jax import lax
from jax.experimental import pallas as pl
from jax.experimental.pallas import tpu as pltpu
from jax.sharding import PartitionSpec as P

FACE = 16
HIGH = lax.Precision.HIGHEST
F32 = jnp.float32
BF16 = jnp.bfloat16


def iota(shape, dim):
    return lax.broadcasted_iota(jnp.int32, shape, dim)


def exact(left, right):
    return jnp.dot(left, right, precision=HIGH, preferred_element_type=F32)


def split(value):
    high = value.astype(BF16)
    return high, (value - high.astype(F32)).astype(BF16)


def wanted_node(face, item):
    high, low = item // 4, item % 4
    return jnp.where(face < 2, 16 * high + low + 12 * (face == 1), 16 * high + 4 * low + 3 * (face == 3))


def dot(left, right):
    return jnp.dot(left, right, preferred_element_type=F32)


def dot_rows(left, right):
    return lax.dot_general(left, right, (((1,), (1,)), ((), ())), preferred_element_type=F32)


def applied(rows, linear):
    lane = iota((rows.shape[0], 128), 1)
    halves = []
    for begin in (0, 128):
        part, total = rows[:, begin:begin + 128], None
        for b in range(FACE):
            near = jnp.take_along_axis(part, lane // FACE * FACE + b, axis=1, mode="promise_in_bounds")
            term = near * linear[b:b + 1, begin:begin + 128]
            total = term if total is None else total + term
        halves.append(total)
    return jnp.concatenate(halves, axis=1)


def join(earlier, later):
    moved_rows = applied(earlier, later[:FACE])
    return jnp.concatenate([moved_rows[:FACE], moved_rows[FACE:] + later[FACE:]], axis=0)


def advance(trace, later):
    return applied(trace, later[:FACE]) + later[FACE:]


def encode(value):
    keep = (iota((256, 128), 0) // FACE == iota((256, 128), 1) % FACE).astype(BF16)
    spread = [jnp.concatenate([part] * 16, axis=0) * keep for part in split(value)]
    gather = (iota((8, 256), 1) % 128 // FACE == iota((8, 256), 0)).astype(BF16)
    return dot_rows(gather, jnp.concatenate(spread, axis=1))


def face_columns(inv_rows, nodes):
    at = iota((nodes, 5 * FACE), 1)
    wanted = jnp.where(at < 64, wanted_node(at // FACE, at % FACE), at - 64)
    chosen = (iota((nodes, 5 * FACE), 0) == wanted).astype(BF16)
    return dot(jnp.concatenate(split(inv_rows), axis=0), chosen).astype(BF16)


def class_products(high, low, weights):
    count = high.shape[0]
    parts = dot(jnp.concatenate([high, low], axis=0), weights)
    return -(parts[:count, :128] + parts[:count, 128:] + parts[count:, :128])


def with_inverse(inv_rows, products):
    count = inv_rows.shape[0]
    wide = jnp.concatenate([inv_rows, jnp.zeros((count, 128 - inv_rows.shape[1]), F32)], axis=1)
    return jnp.where(iota((count, 128), 1) < 64, wide, products)


def in_parts(value):
    high, low = split(value)
    return jnp.concatenate([high, low], axis=1)


def coupling_parts(products):
    high, low = split(products)
    lane = iota(products.shape, 1)
    return jnp.where(lane < 32, high.astype(F32), jnp.where(lane < 48, low.astype(F32), 0.0)).astype(BF16)


def params_kernel(cls_hbm, flag_hbm, x_hbm, lat_hbm, inv_hbm, weight_ref, out_ref, step_ref, label_ref,
                  cls_ref, flag_ref, x_ref, lat_ref, inv_ref, sems):
    pairs = ((cls_hbm, cls_ref), (flag_hbm, flag_ref), (x_hbm, x_ref), (lat_hbm, lat_ref))
    pairs += ((inv_hbm.at[:, inv_hbm.shape[1] - FACE:, :], inv_ref),)
    copies = [pltpu.make_async_copy(a, b, sems.at[i]) for i, (a, b) in enumerate(pairs)]
    for copy in copies[::-1]:
        copy.start()
    count, nodes, _ = inv_hbm.shape
    planes = cls_ref.shape[0]
    item, lane = iota((FACE, 128), 0), iota((FACE, 128), 1)
    places = [(lane == 64 + FACE * f + item).astype(BF16) for f in range(4)]
    places.append(((lane < 48) & (lane % FACE == item)).astype(BF16))
    for copy in copies[:2]:
        copy.wait()
    labels = [cls_ref[x] for x in range(planes)]
    labels += [flag_ref[d, x] for d in range(2) for x in range(planes)]
    labels = jnp.concatenate(labels, axis=0).astype(F32).astype(BF16)
    tile = (iota((FACE, 128), 1) % FACE == iota((FACE, 128), 0)).astype(BF16)
    label_ref[...] = dot(labels, tile)
    for copy in copies[2:]:
        copy.wait()
    placed = []
    for f in range(5):
        rows = (lat_ref[f] if f < 4 else x_ref[...]).reshape(count * FACE, FACE)
        placed.append(dot(jnp.concatenate(split(rows), axis=0), places[f]).astype(BF16))
    inv_rows = [inv_ref[k] for k in range(count)]
    gathered = face_columns(jnp.concatenate(inv_rows, axis=0), nodes)
    outs, steps = [], []
    for k in range(count):
        columns = []
        for part in range(2):
            begin = part * count * FACE + k * FACE
            columns.append(jnp.concatenate([p[begin:begin + FACE] for p in placed], axis=0))
        weights = jnp.concatenate(columns, axis=1)
        weight_ref[:, 256 * k:256 * k + 256] = weights
        low = (count + k) * FACE
        products = class_products(gathered[k * FACE:k * FACE + FACE], gathered[low:low + FACE], weights)
        outs.append(with_inverse(inv_rows[k], products))
        steps.append(products)
    out_ref[...] = in_parts(jnp.concatenate(outs, axis=0))
    step_ref[...] = coupling_parts(jnp.concatenate(steps, axis=0))


def picked(label, count):
    wide = (iota((FACE, 256), 1) // FACE == iota((FACE, 256), 0)).astype(BF16)
    on_wide = dot(label[:, :FACE].astype(BF16), wide).astype(jnp.int32)
    row, lane = iota((count * FACE, 256), 0), iota((count * FACE, 256), 1)
    return jnp.where((row % FACE == lane % FACE) & (row // FACE == on_wide), 1.0, 0.0).astype(BF16)


def class_sum(every, label, rows):
    total = None
    for k in range(8):
        term = jnp.where(label == k, every[k * rows:(k + 1) * rows], 0.0)
        total = term if total is None else total + term
    return total


def stacked(value):
    first, second = split(value)
    rest = jnp.zeros((128 - 3 * FACE, value.shape[1]), BF16)
    return jnp.concatenate([first, second, first, rest], axis=0)


def sources_kernel(gx_size, gy_size, *refs):
    place = lax.axis_index("gx")

    @pl.when(place < gx_size - 1)
    def _():
        gather_sources(gy_size, True, *refs)

    @pl.when(place == gx_size - 1)
    def _():
        gather_sources(gy_size, False, *refs)


def gather_sources(gy_size, mapped, u_ref, rhs_ref, below_ref, above_ref, label_ref, out_ref, step_ref, x_ref, flow_ref, lin_ref, map_ref):
    planes, rows_y, nodes, columns = u_ref.shape
    place = lax.axis_index("gy")
    node, item = iota((nodes, nodes), 1), iota((nodes, nodes), 0)
    chosen = (node == wanted_node(item // FACE, item % FACE)).astype(BF16)
    own = [u_ref[x, y] for x in range(planes) for y in range(rows_y)]
    pair = gy_size == 2
    if pair:
        row = jnp.where(place > 0, below_ref.shape[1] - 1, 0)
        other = [below_ref[x, row] for x in range(planes)]
    else:
        other = [below_ref[x, below_ref.shape[1] - 1] for x in range(planes)] + [above_ref[x, 0] for x in range(planes)]
    step = step_ref[...]
    row, lane = iota((2 * FACE, 128), 0), iota((2 * FACE, 128), 1)
    flip = (lane == row + FACE * (row >= FACE)).astype(BF16)
    turned = dot_rows(flip, step).astype(BF16)
    faces = dot(chosen, jnp.concatenate(own + other, axis=1))
    picks = []
    for at in range(planes * rows_y):
        picks.append(picked(label_ref[pl.ds(at, 1), :], step.shape[0] // FACE))
    linear = dot(turned, jnp.concatenate(picks, axis=1))
    faces = [faces[:, i * columns:(i + 1) * columns] for i in range(len(own) + len(other))]
    z_at = iota((FACE, columns), 1) % FACE
    has_below = jnp.where(place > 0, 1.0, 0.0)
    has_above = jnp.where(place < gy_size - 1, 1.0, 0.0)
    data = []
    for x in range(planes):
        under = faces[len(own) + x][16:32] * has_below
        over = faces[len(own) + (0 if pair else planes) + x][0:16] * has_above
        for y in range(rows_y):
            at = x * rows_y + y
            y_flag = label_ref[pl.ds(planes * rows_y + at, 1), :]
            z_flag = label_ref[pl.ds(2 * planes * rows_y + at, 1), :]
            from_below = faces[at - 1][16:32] if y > 0 else under
            from_above = faces[at + 1][0:16] if y < rows_y - 1 else over
            from_front = jnp.where(z_at == 0, 0.0, pltpu.roll(faces[at][48:64], 1, 1))
            from_back = jnp.where(z_at == FACE - 1, 0.0, pltpu.roll(faces[at][32:48], columns - 1, 1))
            lateral = jnp.concatenate(
                [
                    from_below * (1.0 - y_flag),
                    from_above * y_flag,
                    from_front * (1.0 - z_flag),
                    from_back * z_flag,
                ],
                axis=0,
            ).astype(BF16)
            here = jnp.concatenate([rhs_ref[x, y], lateral], axis=0)
            x_ref[x, y] = here
            data.append(here)
    data = jnp.concatenate(data, axis=1)
    every = dot(out_ref[...], jnp.concatenate([data, data], axis=0))
    keep = (iota((256, 256), 0) // FACE == iota((256, 256), 1) // FACE).astype(BF16)
    wholes, pairs = None, None
    for x in range(planes):
        here = [linear[:, at * 256:at * 256 + 256] for at in range(x * rows_y, (x + 1) * rows_y)]
        both = [(part[:FACE].astype(BF16), part[FACE:].astype(BF16)) for part in here]
        for y in range(rows_y):
            lin_ref[x, y] = here[y][:FACE] + here[y][FACE:]
        if wholes is None:
            wholes, pairs = [part[:FACE] + part[FACE:] for part in here], both
        elif mapped:
            blocks = [[jnp.concatenate([part] * 16, axis=0) * keep for part in parts] for parts in both]
            stacks = [jnp.concatenate(pair, axis=0) for pair in pairs]
            firsts = [dot(stack, block[0]) for stack, block in zip(stacks, blocks)]
            seconds = [dot(pair[0], block[1]) for pair, block in zip(pairs, blocks)]
            wholes = [first[:FACE] + first[FACE:] + second for first, second in zip(firsts, seconds)]
            pairs = [split(whole) for whole in wholes]
    total = None
    for x in range(planes):
        begin = x * rows_y * columns
        label = jnp.concatenate([label_ref[pl.ds(x * rows_y + y, 1), :] for y in range(rows_y)], axis=1)
        flow = class_sum(every[:, begin:begin + rows_y * columns], label, FACE)
        flow_ref[x] = flow
        if total is not None and (mapped or x < planes - 1):
            flow = flow + class_sum(dot(step_ref[...], stacked(total)), label, FACE)
        total = flow
    if not mapped:
        map_ref[...] = jnp.zeros(map_ref.shape, F32)
        return
    for y in range(rows_y):
        map_ref[y, 0:FACE] = wholes[y]
        map_ref[y, FACE:] = encode(total[:, y * columns:(y + 1) * columns])


def block_diagonal(linear):
    keep = (iota((256, 256), 0) // FACE == iota((256, 256), 1) // FACE).astype(BF16)
    return [jnp.concatenate([part] * 16, axis=0) * keep for part in split(linear)]


def half_weights(high, low, begin):
    keep = (iota((128, 128), 0) // FACE == iota((128, 128), 1) // FACE).astype(BF16)
    parts = [jnp.concatenate([part[:, begin:begin + 128]] * 8, axis=0) * keep for part in (high, low)]
    return jnp.concatenate(parts, axis=0)


def half_rows(high, low, begin):
    high, low = high[:, begin:begin + 128], low[:, begin:begin + 128]
    upper = jnp.concatenate([high, high], axis=1)
    return jnp.concatenate([upper, jnp.concatenate([low, jnp.zeros_like(low)], axis=1)], axis=0)


def joined_rows(pairs):
    ready = [
        (half_rows(*rows, begin), half_weights(*linear, begin)) for rows, linear in pairs for begin in (0, 128)
    ]
    sums = [dot(rows, weights) for rows, weights in ready]
    sums = [both[:both.shape[0] // 2] + both[both.shape[0] // 2:] for both in sums]
    return [jnp.concatenate(sums[i:i + 2], axis=1) for i in range(0, len(sums), 2)]


def join_many(pairs):
    rest = jnp.zeros((8, 256), F32)
    split_pairs = [(split(jnp.concatenate([first, rest], axis=0)), split(second[:FACE])) for first, second in pairs]
    joined = []
    for total, (_, later) in zip(joined_rows(split_pairs), pairs):
        joined.append(jnp.concatenate([total[:FACE], total[FACE:24] + later[FACE:]], axis=0))
    return joined


def sent_steps(size, first):
    if first == 2:
        return (2, 1) + tuple(range(3, size)) if size > 2 else tuple(range(1, size))
    return (1, 3, 2) + tuple(range(4, size)) if size > 3 else tuple(range(1, size))


def advance_many(traces, maps):
    rest = jnp.zeros((8, 256), F32)
    pairs = [(split(jnp.concatenate([trace, rest], axis=0)), split(one[:FACE])) for trace, one in zip(traces, maps)]
    return [total[:8] + one[FACE:] for total, one in zip(joined_rows(pairs), maps)]


def block_slot(mine, other, size, power, first):
    step = (mine ^ other) if power else (mine - other + size) % size
    if first == 2:
        return step + 1 * (step == 1) - 1 * (step == 2) if size > 2 else step
    return step + 1 * (step == 2) - 1 * (step == 3) if size > 3 else step


def group_kernel(size, power, outer, *refs):
    blocks, total_ref, held = refs[:size], refs[size + 1], refs[size + 2]
    place = lax.axis_index("gx")
    mine = place % size
    rows_y = total_ref.shape[0]

    @pl.when(place // size < outer - 1)
    def _():
        for s in range(size):
            held[s] = blocks[s][...]
        slots = [block_slot(mine, j, size, power, 1) for j in range(size)]
        maps = [[held[slot, y] for slot in slots] for y in range(rows_y)]
        while len(maps[0]) > 1:
            length = len(maps[0])
            joined = join_many([(maps[y][i], maps[y][i + 1]) for y in range(rows_y) for i in range(0, length - 1, 2)])
            half = length // 2
            maps = [joined[y * half:y * half + half] + maps[y][2 * half:] for y in range(rows_y)]
        for y in range(rows_y):
            total_ref[y] = maps[y][0]

    @pl.when(place // size == outer - 1)
    def _():
        total_ref[...] = jnp.zeros(total_ref.shape, F32)


def carried(parts, traces, count):
    keep = (iota((128, 256), 0) % FACE == iota((128, 256), 1) // FACE).astype(BF16)
    here = []
    for trace in traces:
        rows = jnp.concatenate([jnp.broadcast_to(trace[t:t + 1], (FACE, 256)) for t in range(8)], axis=0)
        here.append([part * keep for part in split(rows)])
    by_first = [dot_rows(part, data[0]) for part, data in zip(parts, here)]
    by_second = [dot_rows(part[:count], data[1]) for part, data in zip(parts, here)]
    return [first[:count] + first[count:] + second for first, second in zip(by_first, by_second)]


def write_nodes(result_ref, out_ref, sems, base_ref, part_ref, traces):
    planes, rows_y, nodes, _ = result_ref.shape
    sums = carried([part_ref[y] for y in range(rows_y)], traces, planes * nodes)
    copies = []
    for y in range(rows_y):
        for x in range(planes):
            result_ref[x, y] = base_ref[x, y] + sums[y][x * nodes:(x + 1) * nodes]
            copies.append(pltpu.make_async_copy(result_ref.at[x, y], out_ref.at[x, y], sems.at[x, y]))
            copies[-1].start()
    for copy in copies:
        copy.wait()


def local_kernel(data_ref, label_ref, weight_ref, flow_ref, inv_ref, inflow_ref, base_ref, start_ref, chosen_ref, offset_ref, full_ref):
    planes, rows_y, nodes, columns = base_ref.shape
    coupling = jnp.zeros((nodes, 128), F32)
    count = inv_ref.shape[0]
    gathered = face_columns(inv_ref[...].reshape(count * nodes, nodes), nodes)
    for k in range(count):
        inv_rows = inv_ref[k]
        low = (count + k) * nodes
        products = class_products(
            gathered[k * nodes:k * nodes + nodes], gathered[low:low + nodes], weight_ref[:, 256 * k:256 * k + 256]
        )
        here = pl.ds(k * nodes, nodes)
        shifted = pltpu.roll(products, FACE * k, 1) if k else products
        coupling = jnp.where(iota((nodes, 128), 1) // FACE == k, shifted, coupling)
        full_ref[here, :] = in_parts(with_inverse(inv_rows, products))
    coupling = jnp.concatenate(split(coupling), axis=0)
    for y in range(rows_y):
        start_ref[y] = encode(inflow_ref[y])
    for x in range(planes):
        for y in range(rows_y):
            label = label_ref[pl.ds(x * rows_y + y, 1), :]
            data = data_ref[x, y]
            every = dot(full_ref[...], jnp.concatenate([data, data], axis=0))
            base_ref[x, y] = class_sum(every, label, nodes)
            chosen_ref[x, y] = dot(coupling, picked(label, count)).astype(BF16)
            if x < planes - 1:
                offset_ref[x, y] = encode(flow_ref[x, :, y * columns:(y + 1) * columns])


def ahead_kernel(size, power, *refs):
    blocks, ahead_ref, held = refs[:size], refs[size + 1], refs[size + 2]
    rows_y = ahead_ref.shape[0]
    for s in range(size):
        held[s] = blocks[s][...]
    mine = lax.axis_index("gx") % size
    same = (iota((24, 256), 1) % FACE == iota((24, 256), 0)).astype(F32)
    ahead = [same] * rows_y
    for j in range(size - 1):
        slot = block_slot(mine, j, size, power, 1)
        block = [held[slot, y] for y in range(rows_y)]
        joined = block if j == 0 else join_many([(ahead[y], block[y]) for y in range(rows_y)])
        ahead = [jnp.where(mine > j, joined[y], ahead[y]) for y in range(rows_y)]
    for y in range(rows_y):
        ahead_ref[y] = ahead[y]


def carry_kernel(size, swapped, ahead_ref, local_ref, start_ref, chosen_ref, offset_ref, lin_ref, base_ref, part_ref, out_ref, result_ref, sems):
    planes, rows_y, nodes, _ = base_ref.shape
    place = lax.axis_index("gx")
    if swapped:
        ahead_ref = ahead_ref.at[1 - lax.axis_index("gy") % 2]
    row_range = range(rows_y)

    def plane_map(x):
        return [jnp.concatenate([lin_ref[x, y], offset_ref[x, y]], axis=0) for y in row_range]

    @pl.when(place < size)
    def _():
        traces = advance_many([start_ref[y] for y in row_range], [ahead_ref[y] for y in row_range])
        entering = list(traces)
        for x in range(planes - 1):
            traces = advance_many(traces, plane_map(x))
            entering += traces
        sums = carried([chosen_ref[x, y] for x in range(planes) for y in row_range], entering, nodes)
        copies = []
        for x in range(planes):
            for y in row_range:
                result_ref[x, y] = local_ref[x, y] + sums[x * rows_y + y]
                copies.append(pltpu.make_async_copy(result_ref.at[x, y], out_ref.at[x, y], sems.at[x, y]))
                copies[-1].start()
        for copy in copies:
            copy.wait()

    @pl.when(place >= size)
    def _():
        ahead = [ahead_ref[y] for y in row_range]
        for x in range(planes):
            chosen = [chosen_ref[x, y] for y in row_range]
            sums = carried(chosen, [ahead[y][FACE:] for y in row_range], nodes)
            pairs = [block_diagonal(ahead[y][:FACE]) for y in row_range]
            firsts = [dot_rows(chosen[y], pairs[y][0]) for y in row_range]
            seconds = [dot_rows(chosen[y][:nodes], pairs[y][1]) for y in row_range]
            for y in row_range:
                base_ref[x, y] = local_ref[x, y] + sums[y]
                high, low = split(firsts[y][:nodes] + firsts[y][nodes:] + seconds[y])
                part_ref[y, pl.ds(x * nodes, nodes), :] = high
                part_ref[y, pl.ds((planes + x) * nodes, nodes), :] = low
            if x < planes - 1:
                ahead = join_many(list(zip(ahead, plane_map(x))))


def finish_places(places, steps, inner, *refs):
    blocks = refs[:len(steps)]
    start_ref, base_ref, part_ref, _, out_ref, result_ref, sems = refs[len(steps):]
    mine = lax.axis_index("gx") // inner
    for place in places:
        @pl.when(mine == place)
        def _():
            traces = [start_ref[y] for y in range(base_ref.shape[1])]
            for j in range(place):
                block = blocks[steps.index(place ^ j)]
                traces = advance_many(traces, [block[y] for y in range(len(traces))])
            write_nodes(result_ref, out_ref, sems, base_ref, part_ref, traces)


def finish_kernel(size, inner, power, *refs):
    blocks = refs[:size]
    start_ref, base_ref, part_ref, _, out_ref, result_ref, sems = refs[size:size + 7]
    rows_y = base_ref.shape[1]
    mine = lax.axis_index("gx") // inner
    held = refs[size + 7]
    for s in range(size):
        held[s] = blocks[s][...]

    @pl.when(mine > 0)
    def _():
        traces = []
        for y in range(rows_y):
            trace = start_ref[y]
            for j in range(size - 1):
                slot = block_slot(mine, j, size, power, 2)
                trace = jnp.where(mine > j, advance(trace, held[slot, y]), trace)
            traces.append(trace)
        write_nodes(result_ref, out_ref, sems, base_ref, part_ref, traces)


def moved(value, pairs):
    return lax.ppermute(value, ("gx", "gy"), pairs)


def shape(dims, kind=F32):
    return jax.ShapeDtypeStruct(dims, kind)


def call(kernel, outs, name, args, scratch=(), space=pltpu.VMEM, out_spaces=None, aliases=None, limit=48):
    many = isinstance(outs, tuple)
    spaces = out_spaces or ((pltpu.VMEM,) * len(outs) if many else pltpu.VMEM)
    if isinstance(space, tuple):
        in_specs = [pl.BlockSpec(memory_space=one) for one in space]
    else:
        in_specs = [pl.BlockSpec(memory_space=space)] * len(args)
    if many:
        out_specs = tuple(pl.BlockSpec(memory_space=one) for one in spaces)
    else:
        out_specs = pl.BlockSpec(memory_space=spaces)
    return pl.pallas_call(
        kernel,
        out_shape=outs,
        in_specs=in_specs,
        out_specs=out_specs,
        scratch_shapes=list(scratch),
        input_output_aliases=aliases or {},
        name=name,
        cost_estimate=pl.CostEstimate(flops=1000000, bytes_accessed=500000, transcendentals=0),
        compiler_params=pltpu.CompilerParams(vmem_limit_bytes=limit * 1024 * 1024),
    )(*args)


def on_device(gx_size, gy_size, u_old, rhs, classes, flags, inverse, x_face, lateral_faces, inflow):
    planes, rows_y, nodes, columns = u_old.shape
    count = inverse.shape[0]
    everyone = [(x, y) for x in range(gx_size) for y in range(gy_size)]

    def at(x, y):
        return x * gy_size + y

    if gy_size == 2:
        below = above = moved(u_old, [(at(x, y), at(x, 1 - y)) for x, y in everyone])
    else:
        below = moved(u_old[:, rows_y - 1:], [(at(x, y), at(x, y + 1)) for x, y in everyone if y + 1 < gy_size])
        above = moved(u_old[:, :1], [(at(x, y), at(x, y - 1)) for x, y in everyone if y > 0])
    weights, out_rows, step, labels = call(
        params_kernel,
        (
            shape((5 * FACE, count * 256), BF16),
            shape((count * FACE, 256), BF16),
            shape((count * FACE, 128), BF16),
            shape((3 * planes * rows_y, columns)),
        ),
        "class_matrices",
        tuple(
            pltpu.with_memory_space_constraint(value, pltpu.HBM)
            for value in (classes, flags, x_face, lateral_faces, inverse)
        ),
        [
            pltpu.VMEM(classes.shape, jnp.int32),
            pltpu.VMEM(flags.shape, jnp.int32),
            pltpu.VMEM(x_face.shape, F32),
            pltpu.VMEM(lateral_faces.shape, F32),
            pltpu.VMEM((count, FACE, nodes), F32),
            pltpu.SemaphoreType.DMA((5,)),
        ],
        space=pltpu.HBM,
    )
    data, flow, linear, here = call(
        functools.partial(sources_kernel, gx_size, gy_size),
        (
            shape((planes, rows_y, 128, columns), BF16),
            shape((planes, FACE, rows_y * columns)),
            shape((planes, rows_y, FACE, 256)),
            shape((rows_y, 24, 256)),
        ),
        "sources",
        (u_old, rhs, below, above, labels, out_rows, step),
    )
    inner = 4 if gx_size % 4 == 0 else 1
    outer = gx_size // inner
    power = outer & (outer - 1) == 0
    other = 1 if gy_size % 2 == 0 else 0

    def exchanged(value, step):
        if power or step < inner:
            return moved(value, [(at(x, y), at(x ^ step, y ^ other)) for x, y in everyone])
        return moved(value, [(at(x, y), at((x + step) % gx_size, y ^ other)) for x, y in everyone])

    near = ((exchanged(here, 0) if other else here),) + tuple(exchanged(here, s) for s in sent_steps(inner, 1))
    nodes_shape = (planes, rows_y, nodes, columns)
    writing = [pltpu.VMEM(nodes_shape, F32), pltpu.SemaphoreType.DMA((planes, rows_y))]
    local, start, chosen, offsets = call(
        local_kernel,
        (
            shape(nodes_shape),
            shape((rows_y, 8, 256)),
            shape((planes, rows_y, 2 * nodes, 256), BF16),
            shape((max(planes - 1, 1), rows_y, 8, 256)),
        ),
        "local_solve",
        (data, labels, weights, flow, inverse, inflow),
        [pltpu.VMEM((count * nodes, 256), BF16)],
    )
    total = call(
        functools.partial(group_kernel, inner, True, outer),
        shape((rows_y, 24, 256)),
        "group_maps",
        near + (start,),
        [pltpu.VMEM((inner, rows_y, 24, 256), F32)],
    )
    blocks = [total] + [exchanged(total, s * inner) for s in sent_steps(outer, 2)]
    ahead = call(
        functools.partial(ahead_kernel, inner, True),
        shape((rows_y, 24, 256)),
        "maps_ahead",
        near + (total,),
        [pltpu.VMEM((inner, rows_y, 24, 256), F32)],
    )
    if other:
        couples = [[y, y + 1] for y in range(0, gy_size, 2)]
        ahead = lax.all_gather(ahead, "gy", axis_index_groups=couples)
    base, parts, out = call(
        functools.partial(carry_kernel, inner, other == 1),
        (
            shape(nodes_shape),
            shape((rows_y, 2 * planes * nodes, 256), BF16),
            pltpu.HBM(nodes_shape, F32),
        ),
        "carry_maps",
        (ahead, local, start, chosen, offsets, linear),
        writing,
        out_spaces=(pltpu.VMEM, pltpu.VMEM, pltpu.HBM),
    )
    def written(kernel, name, args, scratch):
        return call(
            kernel,
            pltpu.HBM(nodes_shape, F32),
            name,
            args,
            scratch,
            space=(pltpu.VMEM,) * (len(args) - 1) + (pltpu.HBM,),
            out_spaces=pltpu.HBM,
            aliases={len(args) - 1: 0},
        )

    if power and outer == 4:
        steps = sent_steps(outer, 2)
        early = (3, 1)
        out = written(
            functools.partial(finish_places, (1,), early, inner),
            "finish_second",
            tuple(blocks[1 + steps.index(one)] for one in early) + (start, base, parts, out),
            writing,
        )
        return written(
            functools.partial(finish_places, (2, 3), steps, inner),
            "finish_last",
            tuple(blocks[1:]) + (start, base, parts, out),
            writing,
        )
    return written(
        functools.partial(finish_kernel, outer, inner, power),
        "finish",
        tuple(blocks) + (start, base, parts, out),
        writing + [pltpu.VMEM((outer, rows_y, 24, 256), F32)],
    )


def solution(mesh):
    in_specs = (
        P("gx", "gy", None, None),
        P("gx", "gy", None, None),
        P("gx", "gy", None),
        P(None, "gx", "gy", None),
        P(),
        P(),
        P(),
        P("gy", None, None),
    )
    out_specs = P("gx", "gy", None, None)
    body = functools.partial(on_device, mesh.shape["gx"], mesh.shape["gy"])
    return jax.shard_map(body, mesh=mesh, in_specs=in_specs, out_specs=out_specs, check_vma=False)
```

```python
import functools

import jax
import jax.numpy as jnp
from jax import lax
from jax.experimental import pallas as pl
from jax.experimental.pallas import tpu as pltpu
from jax.sharding import PartitionSpec as P

FACE = 16
HIGH = lax.Precision.HIGHEST
F32 = jnp.float32
BF16 = jnp.bfloat16


def iota(shape, dim):
    return lax.broadcasted_iota(jnp.int32, shape, dim)


def exact(left, right):
    return jnp.dot(left, right, precision=HIGH, preferred_element_type=F32)


def split(value):
    high = value.astype(BF16)
    return high, (value - high.astype(F32)).astype(BF16)


def wanted_node(face, item):
    high, low = item // 4, item % 4
    return jnp.where(face < 2, 16 * high + low + 12 * (face == 1), 16 * high + 4 * low + 3 * (face == 3))


def dot(left, right):
    return jnp.dot(left, right, preferred_element_type=F32)


def dot_rows(left, right):
    return lax.dot_general(left, right, (((1,), (1,)), ((), ())), preferred_element_type=F32)


def applied(rows, linear):
    lane = iota((rows.shape[0], 128), 1)
    halves = []
    for begin in (0, 128):
        part, total = rows[:, begin:begin + 128], None
        for b in range(FACE):
            near = jnp.take_along_axis(part, lane // FACE * FACE + b, axis=1, mode="promise_in_bounds")
            term = near * linear[b:b + 1, begin:begin + 128]
            total = term if total is None else total + term
        halves.append(total)
    return jnp.concatenate(halves, axis=1)


def join(earlier, later):
    moved_rows = applied(earlier, later[:FACE])
    return jnp.concatenate([moved_rows[:FACE], moved_rows[FACE:] + later[FACE:]], axis=0)


def advance(trace, later):
    return applied(trace, later[:FACE]) + later[FACE:]


def encode(value):
    keep = (iota((256, 128), 0) // FACE == iota((256, 128), 1) % FACE).astype(BF16)
    spread = [jnp.concatenate([part] * 16, axis=0) * keep for part in split(value)]
    gather = (iota((8, 256), 1) % 128 // FACE == iota((8, 256), 0)).astype(BF16)
    return dot_rows(gather, jnp.concatenate(spread, axis=1))


def face_columns(inv_rows, nodes):
    at = iota((nodes, 5 * FACE), 1)
    wanted = jnp.where(at < 64, wanted_node(at // FACE, at % FACE), at - 64)
    chosen = (iota((nodes, 5 * FACE), 0) == wanted).astype(BF16)
    return dot(jnp.concatenate(split(inv_rows), axis=0), chosen).astype(BF16)


def class_products(high, low, weights):
    count = high.shape[0]
    parts = dot(jnp.concatenate([high, low], axis=0), weights)
    return -(parts[:count, :128] + parts[:count, 128:] + parts[count:, :128])


def with_inverse(inv_rows, products):
    count = inv_rows.shape[0]
    wide = jnp.concatenate([inv_rows, jnp.zeros((count, 128 - inv_rows.shape[1]), F32)], axis=1)
    return jnp.where(iota((count, 128), 1) < 64, wide, products)


def in_parts(value):
    high, low = split(value)
    return jnp.concatenate([high, low], axis=1)


def coupling_parts(products):
    high, low = split(products)
    lane = iota(products.shape, 1)
    return jnp.where(lane < 32, high.astype(F32), jnp.where(lane < 48, low.astype(F32), 0.0)).astype(BF16)


def params_kernel(cls_hbm, flag_hbm, x_hbm, lat_hbm, inv_hbm, weight_ref, out_ref, step_ref, label_ref,
                  cls_ref, flag_ref, x_ref, lat_ref, inv_ref, sems):
    pairs = ((cls_hbm, cls_ref), (flag_hbm, flag_ref), (x_hbm, x_ref), (lat_hbm, lat_ref))
    pairs += ((inv_hbm.at[:, inv_hbm.shape[1] - FACE:, :], inv_ref),)
    copies = [pltpu.make_async_copy(a, b, sems.at[i]) for i, (a, b) in enumerate(pairs)]
    for copy in copies[::-1]:
        copy.start()
    count, nodes, _ = inv_hbm.shape
    planes = cls_ref.shape[0]
    item, lane = iota((FACE, 128), 0), iota((FACE, 128), 1)
    places = [(lane == 64 + FACE * f + item).astype(BF16) for f in range(4)]
    places.append(((lane < 48) & (lane % FACE == item)).astype(BF16))
    for copy in copies[:2]:
        copy.wait()
    labels = [cls_ref[x] for x in range(planes)]
    labels += [flag_ref[d, x] for d in range(2) for x in range(planes)]
    labels = jnp.concatenate(labels, axis=0).astype(F32).astype(BF16)
    tile = (iota((FACE, 128), 1) % FACE == iota((FACE, 128), 0)).astype(BF16)
    label_ref[...] = dot(labels, tile)
    for copy in copies[2:]:
        copy.wait()
    placed = []
    for f in range(5):
        rows = (lat_ref[f] if f < 4 else x_ref[...]).reshape(count * FACE, FACE)
        placed.append(dot(jnp.concatenate(split(rows), axis=0), places[f]).astype(BF16))
    inv_rows = [inv_ref[k] for k in range(count)]
    gathered = face_columns(jnp.concatenate(inv_rows, axis=0), nodes)
    outs, steps = [], []
    for k in range(count):
        columns = []
        for part in range(2):
            begin = part * count * FACE + k * FACE
            columns.append(jnp.concatenate([p[begin:begin + FACE] for p in placed], axis=0))
        weights = jnp.concatenate(columns, axis=1)
        weight_ref[:, 256 * k:256 * k + 256] = weights
        low = (count + k) * FACE
        products = class_products(gathered[k * FACE:k * FACE + FACE], gathered[low:low + FACE], weights)
        outs.append(with_inverse(inv_rows[k], products))
        steps.append(products)
    out_ref[...] = in_parts(jnp.concatenate(outs, axis=0))
    step_ref[...] = coupling_parts(jnp.concatenate(steps, axis=0))


def picked(label, count):
    wide = (iota((FACE, 256), 1) // FACE == iota((FACE, 256), 0)).astype(BF16)
    on_wide = dot(label[:, :FACE].astype(BF16), wide).astype(jnp.int32)
    row, lane = iota((count * FACE, 256), 0), iota((count * FACE, 256), 1)
    return jnp.where((row % FACE == lane % FACE) & (row // FACE == on_wide), 1.0, 0.0).astype(BF16)


def class_sum(every, label, rows):
    total = None
    for k in range(8):
        term = jnp.where(label == k, every[k * rows:(k + 1) * rows], 0.0)
        total = term if total is None else total + term
    return total


def stacked(value):
    first, second = split(value)
    rest = jnp.zeros((128 - 3 * FACE, value.shape[1]), BF16)
    return jnp.concatenate([first, second, first, rest], axis=0)


def sources_kernel(gy_size, u_ref, rhs_ref, below_ref, above_ref, label_ref, out_ref, step_ref, x_ref, flow_ref, lin_ref, map_ref):
    planes, rows_y, nodes, columns = u_ref.shape
    place = lax.axis_index("gy")
    node, item = iota((nodes, nodes), 1), iota((nodes, nodes), 0)
    chosen = (node == wanted_node(item // FACE, item % FACE)).astype(BF16)
    own = [u_ref[x, y] for x in range(planes) for y in range(rows_y)]
    pair = gy_size == 2
    if pair:
        row = jnp.where(place > 0, below_ref.shape[1] - 1, 0)
        other = [below_ref[x, row] for x in range(planes)]
    else:
        other = [below_ref[x, below_ref.shape[1] - 1] for x in range(planes)] + [above_ref[x, 0] for x in range(planes)]
    step = step_ref[...]
    row, lane = iota((2 * FACE, 128), 0), iota((2 * FACE, 128), 1)
    flip = (lane == row + FACE * (row >= FACE)).astype(BF16)
    turned = dot_rows(flip, step).astype(BF16)
    faces = dot(chosen, jnp.concatenate(own + other, axis=1))
    picks = []
    for at in range(planes * rows_y):
        picks.append(picked(label_ref[pl.ds(at, 1), :], step.shape[0] // FACE))
    linear = dot(turned, jnp.concatenate(picks, axis=1))
    faces = [faces[:, i * columns:(i + 1) * columns] for i in range(len(own) + len(other))]
    z_at = iota((FACE, columns), 1) % FACE
    has_below = jnp.where(place > 0, 1.0, 0.0)
    has_above = jnp.where(place < gy_size - 1, 1.0, 0.0)
    data = []
    for x in range(planes):
        under = faces[len(own) + x][16:32] * has_below
        over = faces[len(own) + (0 if pair else planes) + x][0:16] * has_above
        for y in range(rows_y):
            at = x * rows_y + y
            y_flag = label_ref[pl.ds(planes * rows_y + at, 1), :]
            z_flag = label_ref[pl.ds(2 * planes * rows_y + at, 1), :]
            from_below = faces[at - 1][16:32] if y > 0 else under
            from_above = faces[at + 1][0:16] if y < rows_y - 1 else over
            from_front = jnp.where(z_at == 0, 0.0, pltpu.roll(faces[at][48:64], 1, 1))
            from_back = jnp.where(z_at == FACE - 1, 0.0, pltpu.roll(faces[at][32:48], columns - 1, 1))
            lateral = jnp.concatenate(
                [
                    from_below * (1.0 - y_flag),
                    from_above * y_flag,
                    from_front * (1.0 - z_flag),
                    from_back * z_flag,
                ],
                axis=0,
            ).astype(BF16)
            here = jnp.concatenate([rhs_ref[x, y], lateral], axis=0)
            x_ref[x, y] = here
            data.append(here)
    data = jnp.concatenate(data, axis=1)
    every = dot(out_ref[...], jnp.concatenate([data, data], axis=0))
    keep = (iota((256, 256), 0) // FACE == iota((256, 256), 1) // FACE).astype(BF16)
    wholes, pairs = None, None
    for x in range(planes):
        here = [linear[:, at * 256:at * 256 + 256] for at in range(x * rows_y, (x + 1) * rows_y)]
        both = [(part[:FACE].astype(BF16), part[FACE:].astype(BF16)) for part in here]
        for y in range(rows_y):
            lin_ref[x, y] = here[y][:FACE] + here[y][FACE:]
        if wholes is None:
            wholes, pairs = [part[:FACE] + part[FACE:] for part in here], both
        else:
            blocks = [[jnp.concatenate([part] * 16, axis=0) * keep for part in parts] for parts in both]
            stacks = [jnp.concatenate(pair, axis=0) for pair in pairs]
            firsts = [dot(stack, block[0]) for stack, block in zip(stacks, blocks)]
            seconds = [dot(pair[0], block[1]) for pair, block in zip(pairs, blocks)]
            wholes = [first[:FACE] + first[FACE:] + second for first, second in zip(firsts, seconds)]
            pairs = [split(whole) for whole in wholes]
    total = None
    for x in range(planes):
        begin = x * rows_y * columns
        label = jnp.concatenate([label_ref[pl.ds(x * rows_y + y, 1), :] for y in range(rows_y)], axis=1)
        flow = class_sum(every[:, begin:begin + rows_y * columns], label, FACE)
        flow_ref[x] = flow
        if total is not None:
            flow = flow + class_sum(dot(step_ref[...], stacked(total)), label, FACE)
        total = flow
    for y in range(rows_y):
        map_ref[y, 0:FACE] = wholes[y]
        map_ref[y, FACE:] = encode(total[:, y * columns:(y + 1) * columns])


def block_diagonal(linear):
    keep = (iota((256, 256), 0) // FACE == iota((256, 256), 1) // FACE).astype(BF16)
    return [jnp.concatenate([part] * 16, axis=0) * keep for part in split(linear)]


def half_weights(high, low, begin):
    keep = (iota((128, 128), 0) // FACE == iota((128, 128), 1) // FACE).astype(BF16)
    parts = [jnp.concatenate([part[:, begin:begin + 128]] * 8, axis=0) * keep for part in (high, low)]
    return jnp.concatenate(parts, axis=0)


def half_rows(high, low, begin):
    high, low = high[:, begin:begin + 128], low[:, begin:begin + 128]
    upper = jnp.concatenate([high, high], axis=1)
    return jnp.concatenate([upper, jnp.concatenate([low, jnp.zeros_like(low)], axis=1)], axis=0)


def joined_rows(pairs):
    ready = [
        (half_rows(*rows, begin), half_weights(*linear, begin)) for rows, linear in pairs for begin in (0, 128)
    ]
    sums = [dot(rows, weights) for rows, weights in ready]
    sums = [both[:both.shape[0] // 2] + both[both.shape[0] // 2:] for both in sums]
    return [jnp.concatenate(sums[i:i + 2], axis=1) for i in range(0, len(sums), 2)]


def join_many(pairs):
    rest = jnp.zeros((8, 256), F32)
    split_pairs = [(split(jnp.concatenate([first, rest], axis=0)), split(second[:FACE])) for first, second in pairs]
    joined = []
    for total, (_, later) in zip(joined_rows(split_pairs), pairs):
        joined.append(jnp.concatenate([total[:FACE], total[FACE:24] + later[FACE:]], axis=0))
    return joined


def sent_steps(size, first):
    return (1, 3, 2) + tuple(range(4, size)) if size > 3 else tuple(range(1, size))


def advance_many(traces, maps):
    rest = jnp.zeros((8, 256), F32)
    pairs = [(split(jnp.concatenate([trace, rest], axis=0)), split(one[:FACE])) for trace, one in zip(traces, maps)]
    return [total[:8] + one[FACE:] for total, one in zip(joined_rows(pairs), maps)]


def block_slot(mine, other, size, power, first):
    step = (mine ^ other) if power else (mine - other + size) % size
    return step + 1 * (step == 2) - 1 * (step == 3) if size > 3 else step


def group_kernel(size, power, outer, *refs):
    blocks, total_ref, held = refs[:size], refs[size + 1], refs[size + 2]
    place = lax.axis_index("gx")
    mine = place % size
    rows_y = total_ref.shape[0]

    @pl.when(place // size < outer - 1)
    def _():
        for s in range(size):
            held[s] = blocks[s][...]
        slots = [block_slot(mine, j, size, power, 1) for j in range(size)]
        maps = [[held[slot, y] for slot in slots] for y in range(rows_y)]
        while len(maps[0]) > 1:
            length = len(maps[0])
            joined = join_many([(maps[y][i], maps[y][i + 1]) for y in range(rows_y) for i in range(0, length - 1, 2)])
            half = length // 2
            maps = [joined[y * half:y * half + half] + maps[y][2 * half:] for y in range(rows_y)]
        for y in range(rows_y):
            total_ref[y] = maps[y][0]

    @pl.when(place // size == outer - 1)
    def _():
        total_ref[...] = jnp.zeros(total_ref.shape, F32)


def carried(parts, traces, count):
    keep = (iota((128, 256), 0) % FACE == iota((128, 256), 1) // FACE).astype(BF16)
    here = []
    for trace in traces:
        rows = jnp.concatenate([jnp.broadcast_to(trace[t:t + 1], (FACE, 256)) for t in range(8)], axis=0)
        here.append([part * keep for part in split(rows)])
    by_first = [dot_rows(part, data[0]) for part, data in zip(parts, here)]
    by_second = [dot_rows(part[:count], data[1]) for part, data in zip(parts, here)]
    return [first[:count] + first[count:] + second for first, second in zip(by_first, by_second)]


def write_nodes(result_ref, out_ref, sems, base_ref, part_ref, traces):
    planes, rows_y, nodes, _ = result_ref.shape
    sums = carried([part_ref[y] for y in range(rows_y)], traces, planes * nodes)
    copies = []
    for y in range(rows_y):
        for x in range(planes):
            result_ref[x, y] = base_ref[x, y] + sums[y][x * nodes:(x + 1) * nodes]
            copies.append(pltpu.make_async_copy(result_ref.at[x, y], out_ref.at[x, y], sems.at[x, y]))
            copies[-1].start()
    for copy in copies:
        copy.wait()


def local_kernel(data_ref, label_ref, weight_ref, flow_ref, inv_ref, inflow_ref, base_ref, start_ref, chosen_ref, offset_ref, full_ref):
    planes, rows_y, nodes, columns = base_ref.shape
    coupling = jnp.zeros((nodes, 128), F32)
    count = inv_ref.shape[0]
    gathered = face_columns(inv_ref[...].reshape(count * nodes, nodes), nodes)
    for k in range(count):
        inv_rows = inv_ref[k]
        low = (count + k) * nodes
        products = class_products(
            gathered[k * nodes:k * nodes + nodes], gathered[low:low + nodes], weight_ref[:, 256 * k:256 * k + 256]
        )
        here = pl.ds(k * nodes, nodes)
        shifted = pltpu.roll(products, FACE * k, 1) if k else products
        coupling = jnp.where(iota((nodes, 128), 1) // FACE == k, shifted, coupling)
        full_ref[here, :] = in_parts(with_inverse(inv_rows, products))
    coupling = jnp.concatenate(split(coupling), axis=0)
    for y in range(rows_y):
        start_ref[y] = encode(inflow_ref[y])
    for x in range(planes):
        for y in range(rows_y):
            label = label_ref[pl.ds(x * rows_y + y, 1), :]
            data = data_ref[x, y]
            every = dot(full_ref[...], jnp.concatenate([data, data], axis=0))
            base_ref[x, y] = class_sum(every, label, nodes)
            chosen_ref[x, y] = dot(coupling, picked(label, count)).astype(BF16)
            if x < planes - 1:
                offset_ref[x, y] = encode(flow_ref[x, :, y * columns:(y + 1) * columns])


def ahead_kernel(size, power, *refs):
    blocks, ahead_ref, held = refs[:size], refs[size + 1], refs[size + 2]
    rows_y = ahead_ref.shape[0]
    for s in range(size):
        held[s] = blocks[s][...]
    mine = lax.axis_index("gx") % size
    same = (iota((24, 256), 1) % FACE == iota((24, 256), 0)).astype(F32)
    ahead = [same] * rows_y
    for j in range(size - 1):
        slot = block_slot(mine, j, size, power, 1)
        block = [held[slot, y] for y in range(rows_y)]
        joined = block if j == 0 else join_many([(ahead[y], block[y]) for y in range(rows_y)])
        ahead = [jnp.where(mine > j, joined[y], ahead[y]) for y in range(rows_y)]
    for y in range(rows_y):
        ahead_ref[y] = ahead[y]


def carry_kernel(size, swapped, ahead_ref, local_ref, start_ref, chosen_ref, offset_ref, lin_ref, base_ref, part_ref, out_ref, result_ref, sems):
    planes, rows_y, nodes, _ = base_ref.shape
    place = lax.axis_index("gx")
    if swapped:
        ahead_ref = ahead_ref.at[1 - lax.axis_index("gy") % 2]
    row_range = range(rows_y)

    def plane_map(x):
        return [jnp.concatenate([lin_ref[x, y], offset_ref[x, y]], axis=0) for y in row_range]

    @pl.when(place < size)
    def _():
        traces = advance_many([start_ref[y] for y in row_range], [ahead_ref[y] for y in row_range])
        entering = list(traces)
        for x in range(planes - 1):
            traces = advance_many(traces, plane_map(x))
            entering += traces
        sums = carried([chosen_ref[x, y] for x in range(planes) for y in row_range], entering, nodes)
        copies = []
        for x in range(planes):
            for y in row_range:
                result_ref[x, y] = local_ref[x, y] + sums[x * rows_y + y]
                copies.append(pltpu.make_async_copy(result_ref.at[x, y], out_ref.at[x, y], sems.at[x, y]))
                copies[-1].start()
        for copy in copies:
            copy.wait()

    @pl.when(place >= size)
    def _():
        ahead = [ahead_ref[y] for y in row_range]
        for x in range(planes):
            chosen = [chosen_ref[x, y] for y in row_range]
            sums = carried(chosen, [ahead[y][FACE:] for y in row_range], nodes)
            pairs = [block_diagonal(ahead[y][:FACE]) for y in row_range]
            firsts = [dot_rows(chosen[y], pairs[y][0]) for y in row_range]
            seconds = [dot_rows(chosen[y][:nodes], pairs[y][1]) for y in row_range]
            for y in row_range:
                base_ref[x, y] = local_ref[x, y] + sums[y]
                high, low = split(firsts[y][:nodes] + firsts[y][nodes:] + seconds[y])
                part_ref[y, pl.ds(x * nodes, nodes), :] = high
                part_ref[y, pl.ds((planes + x) * nodes, nodes), :] = low
            if x < planes - 1:
                ahead = join_many(list(zip(ahead, plane_map(x))))


def finish_places(places, steps, inner, *refs):
    blocks = refs[:len(steps)]
    start_ref, base_ref, part_ref, _, out_ref, result_ref, sems = refs[len(steps):]
    mine = lax.axis_index("gx") // inner
    for place in places:
        @pl.when(mine == place)
        def _():
            traces = [start_ref[y] for y in range(base_ref.shape[1])]
            for j in range(place):
                block = blocks[steps.index(place ^ j)]
                traces = advance_many(traces, [block[y] for y in range(len(traces))])
            write_nodes(result_ref, out_ref, sems, base_ref, part_ref, traces)


def finish_kernel(size, inner, power, *refs):
    blocks = refs[:size]
    start_ref, base_ref, part_ref, _, out_ref, result_ref, sems = refs[size:size + 7]
    rows_y = base_ref.shape[1]
    mine = lax.axis_index("gx") // inner
    held = refs[size + 7]
    for s in range(size):
        held[s] = blocks[s][...]

    @pl.when(mine > 0)
    def _():
        traces = []
        for y in range(rows_y):
            trace = start_ref[y]
            for j in range(size - 1):
                slot = block_slot(mine, j, size, power, 2)
                trace = jnp.where(mine > j, advance(trace, held[slot, y]), trace)
            traces.append(trace)
        write_nodes(result_ref, out_ref, sems, base_ref, part_ref, traces)


def moved(value, pairs):
    return lax.ppermute(value, ("gx", "gy"), pairs)


def shape(dims, kind=F32):
    return jax.ShapeDtypeStruct(dims, kind)


def call(kernel, outs, name, args, scratch=(), space=pltpu.VMEM, out_spaces=None, aliases=None, limit=48):
    many = isinstance(outs, tuple)
    spaces = out_spaces or ((pltpu.VMEM,) * len(outs) if many else pltpu.VMEM)
    if isinstance(space, tuple):
        in_specs = [pl.BlockSpec(memory_space=one) for one in space]
    else:
        in_specs = [pl.BlockSpec(memory_space=space)] * len(args)
    if many:
        out_specs = tuple(pl.BlockSpec(memory_space=one) for one in spaces)
    else:
        out_specs = pl.BlockSpec(memory_space=spaces)
    return pl.pallas_call(
        kernel,
        out_shape=outs,
        in_specs=in_specs,
        out_specs=out_specs,
        scratch_shapes=list(scratch),
        input_output_aliases=aliases or {},
        name=name,
        cost_estimate=pl.CostEstimate(flops=1000000, bytes_accessed=500000, transcendentals=0),
        compiler_params=pltpu.CompilerParams(vmem_limit_bytes=limit * 1024 * 1024),
    )(*args)


def on_device(gx_size, gy_size, u_old, rhs, classes, flags, inverse, x_face, lateral_faces, inflow):
    planes, rows_y, nodes, columns = u_old.shape
    count = inverse.shape[0]
    everyone = [(x, y) for x in range(gx_size) for y in range(gy_size)]

    def at(x, y):
        return x * gy_size + y

    if gy_size == 2:
        below = above = moved(u_old, [(at(x, y), at(x, 1 - y)) for x, y in everyone])
    else:
        below = moved(u_old[:, rows_y - 1:], [(at(x, y), at(x, y + 1)) for x, y in everyone if y + 1 < gy_size])
        above = moved(u_old[:, :1], [(at(x, y), at(x, y - 1)) for x, y in everyone if y > 0])
    weights, out_rows, step, labels = call(
        params_kernel,
        (
            shape((5 * FACE, count * 256), BF16),
            shape((count * FACE, 256), BF16),
            shape((count * FACE, 128), BF16),
            shape((3 * planes * rows_y, columns)),
        ),
        "class_matrices",
        tuple(
            pltpu.with_memory_space_constraint(value, pltpu.HBM)
            for value in (classes, flags, x_face, lateral_faces, inverse)
        ),
        [
            pltpu.VMEM(classes.shape, jnp.int32),
            pltpu.VMEM(flags.shape, jnp.int32),
            pltpu.VMEM(x_face.shape, F32),
            pltpu.VMEM(lateral_faces.shape, F32),
            pltpu.VMEM((count, FACE, nodes), F32),
            pltpu.SemaphoreType.DMA((5,)),
        ],
        space=pltpu.HBM,
    )
    data, flow, linear, here = call(
        functools.partial(sources_kernel, gy_size),
        (
            shape((planes, rows_y, 128, columns), BF16),
            shape((planes, FACE, rows_y * columns)),
            shape((planes, rows_y, FACE, 256)),
            shape((rows_y, 24, 256)),
        ),
        "sources",
        (u_old, rhs, below, above, labels, out_rows, step),
    )
    inner = 4 if gx_size % 4 == 0 else 1
    outer = gx_size // inner
    power = outer & (outer - 1) == 0
    other = 1 if gy_size % 2 == 0 else 0

    def exchanged(value, step):
        if power or step < inner:
            return moved(value, [(at(x, y), at(x ^ step, y ^ other)) for x, y in everyone])
        return moved(value, [(at(x, y), at((x + step) % gx_size, y ^ other)) for x, y in everyone])

    near = ((exchanged(here, 0) if other else here),) + tuple(exchanged(here, s) for s in sent_steps(inner, 1))
    nodes_shape = (planes, rows_y, nodes, columns)
    writing = [pltpu.VMEM(nodes_shape, F32), pltpu.SemaphoreType.DMA((planes, rows_y))]
    local, start, chosen, offsets = call(
        local_kernel,
        (
            shape(nodes_shape),
            shape((rows_y, 8, 256)),
            shape((planes, rows_y, 2 * nodes, 256), BF16),
            shape((max(planes - 1, 1), rows_y, 8, 256)),
        ),
        "local_solve",
        (data, labels, weights, flow, inverse, inflow),
        [pltpu.VMEM((count * nodes, 256), BF16)],
    )
    total = call(
        functools.partial(group_kernel, inner, True, outer),
        shape((rows_y, 24, 256)),
        "group_maps",
        near + (start,),
        [pltpu.VMEM((inner, rows_y, 24, 256), F32)],
    )
    blocks = [total] + [exchanged(total, s * inner) for s in sent_steps(outer, 2)]
    ahead = call(
        functools.partial(ahead_kernel, inner, True),
        shape((rows_y, 24, 256)),
        "maps_ahead",
        near + (total,),
        [pltpu.VMEM((inner, rows_y, 24, 256), F32)],
    )
    if other:
        couples = [[y, y + 1] for y in range(0, gy_size, 2)]
        ahead = lax.all_gather(ahead, "gy", axis_index_groups=couples)
    base, parts, out = call(
        functools.partial(carry_kernel, inner, other == 1),
        (
            shape(nodes_shape),
            shape((rows_y, 2 * planes * nodes, 256), BF16),
            pltpu.HBM(nodes_shape, F32),
        ),
        "carry_maps",
        (ahead, local, start, chosen, offsets, linear),
        writing,
        out_spaces=(pltpu.VMEM, pltpu.VMEM, pltpu.HBM),
    )
    def written(kernel, name, args, scratch):
        return call(
            kernel,
            pltpu.HBM(nodes_shape, F32),
            name,
            args,
            scratch,
            space=(pltpu.VMEM,) * (len(args) - 1) + (pltpu.HBM,),
            out_spaces=pltpu.HBM,
            aliases={len(args) - 1: 0},
        )

    if power and outer == 4:
        steps = sent_steps(outer, 2)
        early = (3, 1)
        out = written(
            functools.partial(finish_places, (1,), early, inner),
            "finish_second",
            tuple(blocks[1 + steps.index(one)] for one in early) + (start, base, parts, out),
            writing,
        )
        return written(
            functools.partial(finish_places, (2, 3), steps, inner),
            "finish_last",
            tuple(blocks[1:]) + (start, base, parts, out),
            writing,
        )
    return written(
        functools.partial(finish_kernel, outer, inner, power),
        "finish",
        tuple(blocks) + (start, base, parts, out),
        writing + [pltpu.VMEM((outer, rows_y, 24, 256), F32)],
    )


def solution(mesh):
    in_specs = (
        P("gx", "gy", None, None),
        P("gx", "gy", None, None),
        P("gx", "gy", None),
        P(None, "gx", "gy", None),
        P(),
        P(),
        P(),
        P("gy", None, None),
    )
    out_specs = P("gx", "gy", None, None)
    body = functools.partial(on_device, mesh.shape["gx"], mesh.shape["gy"])
    return jax.shard_map(body, mesh=mesh, in_specs=in_specs, out_specs=out_specs, check_vma=False)
```
